32 devices in a mesh: req: 8 (over y, x, core), wgt: 4 (over z).
Axes of the slice: x: 2, y: 2, z: 4, core: 2. Of those that a mesh axis runs over, the one named last changes fastest.
Arguments:
- arrivals: bfloat16 [32, 48, 6144], P('req', None, 'wgt'), may hold values from -6 to 6
- group_of: int32 [32], replicated, may hold values from 0 to 7, as said below
- lengths: int32 [32], P('req'), may hold values from 1 to 2048, as said below
- page_table: int32 [32, 16], P('req'), may hold values from 0 to 39, as said below
- ln_gain: bfloat16 [6144], replicated, may hold values from 0.25 to 1.75
- ln_bias: bfloat16 [6144], replicated, may hold values from -1.5 to 1.5
- w_qkv: bfloat16 [6144, 9216], P('req', 'wgt'), may hold values from -0.078125 to 0.078125
- qkv_bias: bfloat16 [9216], P('wgt'), may hold values from -4.5 to 4.5
- key_pool: bfloat16 [320, 128, 3072], P('req', None, 'wgt'), may hold values from -8 to 8
- value_pool: bfloat16 [320, 128, 3072], P('req', None, 'wgt'), may hold values from -6 to 6
Outputs:
- attended: bfloat16 [32, 48, 3072], P('req', None, 'wgt')
- new_keys: bfloat16 [32, 48, 3072], P('req', None, 'wgt')
- new_values: bfloat16 [32, 48, 3072], P('req', None, 'wgt')
The draws below stay inside these ranges and needn't reach their ends.
Inputs may be any that keep to these rules, and one draw needn't show every extreme that they name: `group_of`: every group number is named by exactly 4 requests; the requests that arrive at one group (consecutive blocks of 4 in arrival order) name different groups. `lengths`: in each group at most one request has more than 1024 cached tokens; some request has exactly 2048. `page_table`: entries name pages of the request's group's own pool of 40; the pages that hold cached tokens of one group's requests are all different.
All inputs are finite; a program needn't handle non-finite values.
Results may differ from the reference program's by a relative error of at most 0.0066.
Values may be sent and summed in bfloat16 or wider, within the bound.
No kernel may reach another device: no remote copies, remote signals or barrier semaphores. Data moves between devices by JAX's collectives and lax.ppermute only.
A program may use at most 128 MiB of HBM per device.

```python
import math
import jax
import jax.numpy as jnp
from jax import lax

D = 6144
HEADS = 32
HEAD = 96
ROT = 24
FRESH = 48
PAGE = 128
MAXP = 16
REQ_DEV = 4
REQS = 32
POOL_DEV = 40
POOLS = 320


def draw_group_of(key, part):
    groups_all = REQS // REQ_DEV
    base = jax.random.fold_in(key, 3)
    key_sigma, key_tau, key_offset, key_slot = jax.random.split(base, 4)
    sigma = jax.random.permutation(key_sigma, groups_all)
    tau = jax.random.permutation(key_tau, groups_all)
    offsets = jax.random.permutation(key_offset, groups_all)[:REQ_DEV]

    def slot_order(index):
        return jax.random.permutation(jax.random.fold_in(key_slot, index), REQ_DEV)
    slots = jax.vmap(slot_order)(jnp.arange(groups_all))
    target = sigma[(tau[:, None] + offsets[slots]) % groups_all]
    return target.reshape(REQS).astype(jnp.int32)


def layout(key):
    anchor = jax.random.fold_in(key, 11)
    key_short, key_long, key_place, key_peak, key_perm, key_fill = jax.random.split(anchor, 6)
    groups_all = REQS // REQ_DEV
    longest = MAXP * PAGE
    shorter = jax.random.randint(key_short, (groups_all, REQ_DEV), 1, longest // 2 + 1)
    longer = jax.random.randint(key_long, (groups_all, 1), longest // 2 + 1, longest + 1)
    placed = jax.random.randint(key_place, (groups_all, 1), 0, REQ_DEV)
    is_long = jnp.arange(REQ_DEV)[None, :] == placed
    cached = jnp.where(is_long, longer, shorter)
    peak_group = jax.random.randint(key_peak, (), 0, groups_all)
    cached = jnp.where((jnp.arange(groups_all)[:, None] == peak_group) & is_long, longest, cached)
    needed = (cached + PAGE - 1) // PAGE
    begins = jnp.cumsum(needed, axis=1) - needed

    def shuffle_one(index):
        return jax.random.permutation(jax.random.fold_in(key_perm, index), POOL_DEV)
    orders = jax.vmap(shuffle_one)(jnp.arange(groups_all))
    offsets = (begins[:, :, None] + jnp.arange(MAXP)[None, None, :]) % POOL_DEV

    def lookup(order_row, offset_rows):
        return order_row[offset_rows]
    used_pages = jax.vmap(lookup)(orders, offsets)
    filler = jax.random.randint(key_fill, (groups_all, REQ_DEV, MAXP), 0, POOL_DEV)
    table = jnp.where(jnp.arange(MAXP)[None, None, :] < needed[:, :, None], used_pages, filler)
    return (cached.reshape(REQS).astype(jnp.int32), table.reshape(REQS, MAXP).astype(jnp.int32))


def draw_lengths(key, part):
    return layout(key)[0]


def draw_page_table(key, part):
    return layout(key)[1]


def draw_qkv_bias(key, part):
    noise = jnp.clip(0.3 * jax.random.normal(jax.random.fold_in(key, 601), (HEADS, 3, HEAD), jnp.float32), -1.5, 1.5)
    return noise.reshape(3 * HEADS * HEAD).astype(jnp.bfloat16)


def draw_key_pool(key, part):
    values = jnp.clip(jax.random.normal(jax.random.fold_in(key, 701), (POOLS, PAGE, HEADS * HEAD), jnp.float32), -6.0, 6.0)
    return values.astype(jnp.bfloat16)


def level_of(own_key, extent, pieces, smallest, top_value):
    def one(position, shards_of):
        draws = jax.random.uniform(jax.random.fold_in(jax.random.fold_in(own_key, 6), position), (shards_of,), jnp.float32, smallest / len(pieces), top_value / len(pieces))
        return jnp.repeat(jnp.exp(draws), extent[position] // shards_of).reshape((-1,) + (1,) * (len(extent) - position - 1))

    loudness = one(*pieces[0])
    for cut in pieces[1:]:
        loudness = loudness * one(*cut)
    return loudness


def bell_draw(key, shape, deviation, reach, cuts=(), kind=jnp.bfloat16):
    values = deviation * jax.random.normal(key, shape, jnp.float32)
    if cuts:
        values = values * level_of(key, shape, cuts, -0.22, 0.18)
    return jnp.clip(values, -reach, reach).astype(kind)


def setup_inputs(seed: int = 0) -> dict:
    arg_keys = jax.random.split(jax.random.key(seed), 11)
    return {
        "arrivals": bell_draw(arg_keys[0], (REQS, FRESH, D), 1.0, 6.0, ((0, 8), (2, 4))),
        "group_of": draw_group_of(jax.random.fold_in(arg_keys[10], 71), 0),
        "lengths": draw_lengths(jax.random.fold_in(arg_keys[10], 71), 0),
        "page_table": draw_page_table(jax.random.fold_in(arg_keys[10], 71), 0),
        "ln_gain": jnp.clip(1.0 + 0.15 * jax.random.normal(arg_keys[4], (D,), jnp.float32), 0.25, 1.75).astype(jnp.bfloat16),
        "ln_bias": bell_draw(arg_keys[5], (D,), 0.3, 1.5),
        "w_qkv": bell_draw(arg_keys[6], (D, 3 * HEADS * HEAD), D ** -0.5, 0.078125, ((0, 8), (1, 4))),
        "qkv_bias": draw_qkv_bias(jax.random.fold_in(arg_keys[10], 71), 0),
        "key_pool": draw_key_pool(jax.random.fold_in(arg_keys[10], 71), 0),
        "value_pool": bell_draw(arg_keys[9], (POOLS, PAGE, HEADS * HEAD), 1.0, 6.0, ((0, 8), (2, 4))),
    }


EPS = 1e-05

def rotary(block, positions):
    half_rot = ROT // 2
    inverse = jnp.power(10000.0, -jnp.arange(half_rot, dtype=jnp.float32) * 2.0 / ROT)
    angles = positions[:, :, None] * inverse[None, None, :]
    cosine = jnp.cos(angles)[:, :, None, :]
    sine = jnp.sin(angles)[:, :, None, :]
    first = block[..., :half_rot]
    second = block[..., half_rot:ROT]
    return jnp.concatenate([first * cosine - second * sine, second * cosine + first * sine, block[..., ROT:]], axis=-1)

def reference(arrivals, group_of, lengths, page_table, ln_gain, ln_bias, w_qkv, qkv_bias, key_pool, value_pool):
    order = jnp.argsort(group_of, stable=True).astype(jnp.int32)
    tokens = arrivals[order].astype(jnp.float32)
    center = lax.optimization_barrier(jnp.mean(tokens, axis=-1, keepdims=True))
    spread = lax.optimization_barrier(jnp.mean(jnp.square(tokens - center), axis=-1, keepdims=True))
    normed = ((tokens - center) * lax.rsqrt(spread + EPS) * ln_gain.astype(jnp.float32) + ln_bias.astype(jnp.float32)).astype(jnp.bfloat16)
    projected = jnp.dot(normed.reshape(REQS * FRESH, D), w_qkv, preferred_element_type=jnp.float32) + qkv_bias.astype(jnp.float32)
    projected = projected.reshape(REQS, FRESH, HEADS, 3, HEAD)
    positions = (lengths[:, None] + jnp.arange(FRESH, dtype=jnp.int32)[None, :]).astype(jnp.float32)
    queries = rotary(projected[:, :, :, 0], positions).astype(jnp.bfloat16)
    new_keys = rotary(projected[:, :, :, 1], positions).astype(jnp.bfloat16)
    new_values = projected[:, :, :, 2].astype(jnp.bfloat16)
    owners = ((jnp.arange(REQS, dtype=jnp.int32) // REQ_DEV)[:, None] * POOL_DEV + page_table).astype(jnp.int32)
    scale = 1.0 / math.sqrt(HEAD)
    span = MAXP * PAGE

    def attend(items):
        query, key_new, value_new, length, pages = items
        cached_k = key_pool[pages].reshape(span, HEADS, HEAD).astype(jnp.float32)
        cached_v = value_pool[pages].reshape(span, HEADS, HEAD).astype(jnp.float32)
        query_f = query.astype(jnp.float32)
        scores_old = jnp.einsum('qhd,khd->hqk', query_f, cached_k) * scale
        visible = jnp.arange(span, dtype=jnp.int32)[None, None, :] < length
        scores_old = jnp.where(visible, scores_old, -1e+30)
        scores_new = jnp.einsum('qhd,khd->hqk', query_f, key_new.astype(jnp.float32)) * scale
        causal = jnp.arange(FRESH)[None, :, None] >= jnp.arange(FRESH)[None, None, :]
        scores_new = jnp.where(causal, scores_new, -1e+30)
        peak = jnp.maximum(lax.optimization_barrier(jnp.max(scores_old, axis=-1, keepdims=True)), lax.optimization_barrier(jnp.max(scores_new, axis=-1, keepdims=True)))
        exp_old = jnp.exp(scores_old - peak)
        exp_new = jnp.exp(scores_new - peak)
        denom = lax.optimization_barrier(jnp.sum(exp_old, axis=-1, keepdims=True)) + lax.optimization_barrier(jnp.sum(exp_new, axis=-1, keepdims=True))
        weight_old = (exp_old / denom).astype(jnp.bfloat16)
        weight_new = (exp_new / denom).astype(jnp.bfloat16)
        mixed = jnp.einsum('hqk,khd->qhd', weight_old.astype(jnp.float32), cached_v)
        mixed = mixed + jnp.einsum('hqk,khd->qhd', weight_new.astype(jnp.float32), value_new.astype(jnp.float32))
        return mixed.astype(jnp.bfloat16)
    attended = lax.map(attend, (queries, new_keys, new_values, lengths, owners))
    return (attended.reshape(REQS, FRESH, HEADS * HEAD), new_keys.reshape(REQS, FRESH, HEADS * HEAD), new_values.reshape(REQS, FRESH, HEADS * HEAD))
```

```python
import functools
import math

import jax
import jax.numpy as jnp
import numpy as np
from jax import lax
from jax.experimental import pallas as pl
from jax.experimental.pallas import tpu as pltpu
from jax.sharding import PartitionSpec as P

HEAD = 96
ROT = 24
EPS = 1e-05
LANES = 128
WINDOW = 2 * LANES
CHUNK_PAGES = 4
VMEM_LIMIT = 56 * 1024 * 1024

ANY = pl.BlockSpec(memory_space=pl.ANY)
SMEM = pl.BlockSpec(memory_space=pltpu.SMEM)
VMEM = pl.BlockSpec(memory_space=pltpu.VMEM)


def norm_kernel(depth, chips, place, *refs):
    pieces = refs[: 2 * depth - 1]
    gain, bias = refs[2 * depth - 1 : 2 * depth + 1]
    outs = refs[2 * depth + 1 : 2 * depth + 1 + chips]
    held, sems = refs[2 * depth + 1 + chips :]
    me, chip = place[0], place[1]
    copies = []
    for index, piece in enumerate(pieces):
        if index == 0:
            offset = 0
        elif index < depth:
            offset = -index
        else:
            offset = index - depth + 1
        copies.append((offset, pltpu.make_async_copy(piece, held.at[me + offset], sems.at[index])))

    def inside(offset):
        return (me + offset >= 0) & (me + offset < depth)

    for offset, copy in copies:

        @pl.when(inside(offset))
        def _():
            copy.start()

    for offset, copy in copies:

        @pl.when(inside(offset))
        def _():
            copy.wait()

    rows, width = held.shape[1], held.shape[2]
    step = 16
    total_width = depth * width
    block = total_width // chips
    per = chips // depth

    def body(index, carry):
        at = pl.ds(pl.multiple_of(index * step, step), step)
        values = [held[part, at, :].astype(jnp.float32) for part in range(depth)]
        total = sum(jnp.sum(value, axis=-1, keepdims=True) for value in values)
        center = total / total_width
        square = sum(
            jnp.sum(jnp.square(value - center), axis=-1, keepdims=True) for value in values
        )
        scale = lax.rsqrt(square / total_width + EPS)
        for offset in range(chips):
            target = chip ^ offset
            part = target // per
            lane = pl.ds(pl.multiple_of((target % per) * block, LANES), block)
            value = held[part, at, lane].astype(jnp.float32)
            value = (value - center) * scale * gain[target] + bias[target]
            outs[offset][at, :] = value.astype(jnp.bfloat16)
        return carry

    lax.fori_loop(0, rows // step, body, 0)


def project_kernel(fresh_len, req_count, place, source, *refs):
    groups = (len(refs) - 7) // 2
    tokens = refs[:groups]
    own_rows, other_rows = refs[groups : groups + 2]
    outs = refs[groups + 2 : 2 * groups + 2]
    held, weights, picked, sems, weight_sems = refs[2 * groups + 2 :]
    core = place[0]
    depth = own_rows.shape[0]
    copies = [
        pltpu.make_async_copy(
            token, held.at[pl.ds(index * req_count, req_count)], sems.at[index]
        )
        for index, token in enumerate(tokens)
    ]
    copies.append(
        pltpu.make_async_copy(
            own_rows,
            weights.at[pl.ds(pl.multiple_of(core * depth, 16), depth)],
            weight_sems.at[0],
        )
    )
    copies.append(
        pltpu.make_async_copy(
            other_rows,
            weights.at[pl.ds(pl.multiple_of((1 - core) * depth, 16), depth)],
            weight_sems.at[1],
        )
    )
    for copy in copies:
        copy.start()
    for copy in copies:
        copy.wait()
    rows = req_count * fresh_len
    for pair in range(groups // 2):
        for item in range(2 * req_count):
            picked[item * fresh_len : (item + 1) * fresh_len, :] = held[
                source[pair * 2 * req_count + item]
            ]
        result = jnp.dot(picked[...], weights[...], preferred_element_type=jnp.float32).astype(
            jnp.bfloat16
        )
        outs[2 * pair][...] = result[:rows]
        outs[2 * pair + 1][...] = result[rows:]


def attend_kernel(shape, place, lengths, table, *refs):
    groups, req_count, fresh_len, page, heads = shape
    parts = refs[:groups]
    bias, cosine, sine_up, sine_down, key_pool, value_pool = refs[groups : groups + 6]
    attended, new_keys, new_values = refs[groups + 6 : groups + 9]
    keys, values, sems = refs[groups + 9 :]
    core = place[0]
    chunk = CHUNK_PAGES * page
    pairs = heads // 2

    counts = [pl.cdiv(lengths[index], chunk) for index in range(req_count)]
    bases = [jnp.int32(0)]
    for count in counts[:-1]:
        bases.append(bases[-1] + count * CHUNK_PAGES)

    def copies(index, entry):
        number = table[index, entry]
        slot = bases[index] + entry
        return (
            pltpu.make_async_copy(key_pool.at[number], keys.at[slot], sems.at[index]),
            pltpu.make_async_copy(value_pool.at[number], values.at[slot], sems.at[index]),
        )

    for index in range(req_count):

        def start(entry, carry, index=index):
            for copy in copies(index, entry):
                copy.start()
            return carry

        lax.fori_loop(0, counts[index] * CHUNK_PAGES, start, 0)

    even = sum(parts[index][...].astype(jnp.float32) for index in range(0, groups, 2))
    odd = sum(parts[index][...].astype(jnp.float32) for index in range(1, groups, 2))
    halves = (jnp.where(core == 0, even, odd), jnp.where(core == 0, odd, even))
    halves = [
        half + bias[:, side * half.shape[1] : (side + 1) * half.shape[1]]
        for side, half in enumerate(halves)
    ]

    def kind(which):
        pieces = []
        for head in range(heads):
            half = halves[head // pairs]
            begin = (head % pairs) * 3 * HEAD + which * HEAD
            pieces.append(half[:, begin : begin + HEAD])
        return jnp.concatenate(pieces, axis=1)

    width = heads * HEAD

    def turn(block):
        half_rot = ROT // 2
        return (
            block * cosine[...]
            + pltpu.roll(block, width - half_rot, 1) * sine_up[...]
            + pltpu.roll(block, half_rot, 1) * sine_down[...]
        )

    queries = turn(kind(0)).astype(jnp.bfloat16)
    turned = turn(kind(1)).astype(jnp.bfloat16)
    plain = kind(2).astype(jnp.bfloat16)
    for index in range(req_count):
        rows = slice(index * fresh_len, (index + 1) * fresh_len)
        new_keys[index] = turned[rows]
        new_values[index] = plain[rows]

    factor = 1.0 / math.sqrt(HEAD) / math.log(2.0)
    starts = [(2 * HEAD * pair) // LANES * LANES for pair in range(pairs)]
    lane = lax.broadcasted_iota(jnp.int32, (fresh_len, WINDOW), 1)

    def owned(pair, member):
        begin = (2 * pair + member) * HEAD - starts[pair]
        return (lane >= begin) & (lane < begin + HEAD)

    def contract(left, right):
        return lax.dot_general(
            left, right, (((1,), (1,)), ((), ())), preferred_element_type=jnp.float32
        )

    zero = jnp.zeros((fresh_len, WINDOW), jnp.bfloat16)
    spread_rows = heads * fresh_len
    row = lax.broadcasted_iota(jnp.int32, (2 * fresh_len, fresh_len), 0)
    causal_pair = lax.rem(row, fresh_len) >= lax.broadcasted_iota(
        jnp.int32, (2 * fresh_len, fresh_len), 1
    )
    for index in range(req_count):
        rows = slice(index * fresh_len, (index + 1) * fresh_len)
        spread = []
        for pair in range(pairs):
            window = queries[rows, starts[pair] : starts[pair] + WINDOW]
            spread.append(
                jnp.concatenate(
                    [jnp.where(owned(pair, member), window, zero) for member in range(2)], axis=0
                )
            )
        scores = jnp.concatenate(
            [
                jnp.where(
                    causal_pair,
                    contract(spread[pair], turned[rows, starts[pair] : starts[pair] + WINDOW]),
                    -1e30,
                )
                for pair in range(pairs)
            ],
            axis=0,
        )
        peak = jnp.max(scores, axis=1, keepdims=True)
        weight = jnp.exp2((scores - peak) * factor)
        denom = jnp.sum(weight, axis=1, keepdims=True)
        weight = weight.astype(jnp.bfloat16)
        mixed = jnp.concatenate(
            [
                jnp.dot(
                    weight[pair * 2 * fresh_len : (pair + 1) * 2 * fresh_len],
                    plain[rows, starts[pair] : starts[pair] + WINDOW],
                    preferred_element_type=jnp.float32,
                )
                for pair in range(pairs)
            ],
            axis=0,
        )

        def finish(entry, carry, index=index):
            for copy in copies(index, entry):
                copy.wait()
            return carry

        lax.fori_loop(0, counts[index] * CHUNK_PAGES, finish, 0)

        def step(part, carry, index=index, spread=spread):
            peak, denom, mixed = carry
            first = bases[index] + part * CHUNK_PAGES
            key_block = keys[pl.ds(first, CHUNK_PAGES)].reshape(chunk, width)
            scores = jnp.concatenate(
                [
                    contract(spread[pair], key_block[:, starts[pair] : starts[pair] + WINDOW])
                    for pair in range(pairs)
                ],
                axis=0,
            )
            position = part * chunk + lax.broadcasted_iota(jnp.int32, (spread_rows, chunk), 1)
            scores = jnp.where(position < lengths[index], scores, -1e30)
            higher = jnp.maximum(peak, jnp.max(scores, axis=1, keepdims=True))
            shrink = jnp.exp2((peak - higher) * factor)
            weight = jnp.exp2((scores - higher) * factor)
            denom = denom * shrink + jnp.sum(weight, axis=1, keepdims=True)
            weight = weight.astype(jnp.bfloat16)
            value_block = values[pl.ds(first, CHUNK_PAGES)].reshape(chunk, width)
            added = jnp.concatenate(
                [
                    jnp.dot(
                        weight[pair * 2 * fresh_len : (pair + 1) * 2 * fresh_len],
                        value_block[:, starts[pair] : starts[pair] + WINDOW],
                        preferred_element_type=jnp.float32,
                    )
                    for pair in range(pairs)
                ],
                axis=0,
            )
            return higher, denom, mixed * shrink + added

        peak, denom, mixed = lax.fori_loop(0, counts[index], step, (peak, denom, mixed))
        mixed = mixed / denom
        tiles = [None] * (width // LANES)
        for pair in range(pairs):
            for member in range(2):
                begin = (2 * pair + member) * fresh_len
                part = jnp.where(owned(pair, member), mixed[begin : begin + fresh_len], 0.0)
                for side in range(2):
                    place_at = starts[pair] // LANES + side
                    tile = part[:, side * LANES : (side + 1) * LANES]
                    tiles[place_at] = tile if tiles[place_at] is None else tiles[place_at] + tile
        attended[index] = jnp.concatenate(tiles, axis=1).astype(jnp.bfloat16)


def per_device(
    req_size,
    wgt_size,
    arrivals,
    group_of,
    lengths,
    page_table,
    ln_gain,
    ln_bias,
    w_qkv,
    qkv_bias,
    key_pool,
    value_pool,
):
    req_count, fresh_len, width = arrivals.shape
    rows = req_count * fresh_len
    depth, local_cols = w_qkv.shape
    half_cols = local_cols // 2
    heads = local_cols // (3 * HEAD)
    page = key_pool.shape[1]
    chips = req_size // 2
    block = 2 * depth
    everyone = group_of.shape[0]
    me = lax.axis_index("req")
    layer = lax.axis_index("wgt")
    core = me & 1
    chip = me >> 1

    def swap(value, distance):
        return lax.ppermute(
            value, "req", [(device, device ^ distance) for device in range(req_size)]
        )

    own = arrivals.reshape(rows, width)
    upward, downward = [], []
    up = down = own
    for hop in range(1, wgt_size):
        up = lax.ppermute(up, "wgt", [(at, at + 1) for at in range(hop - 1, wgt_size - 1)])
        down = lax.ppermute(down, "wgt", [(at + 1, at) for at in range(wgt_size - hop)])
        upward.append(up)
        downward.append(down)

    own_rows = lax.dynamic_slice_in_dim(w_qkv, core * half_cols, half_cols, 1)
    other_rows = swap(lax.dynamic_slice_in_dim(w_qkv, (1 - core) * half_cols, half_cols, 1), 1)

    ids = jnp.arange(everyone, dtype=jnp.int32)
    same_group = group_of[:, None] == group_of[None, :]
    earlier = ids[None, :] < ids[:, None]
    rank = jnp.sum((same_group & earlier).astype(jnp.int32), axis=1)
    slot_of = group_of * req_count + rank
    target = (me ^ (ids // req_count)) * req_count + ids % req_count
    order = jnp.sum(jnp.where(slot_of[None, :] == target[:, None], ids[None, :], 0), axis=1)
    source = ((order // req_count) ^ me) * req_count + order % req_count

    lane = np.arange(heads * HEAD) % HEAD
    half_rot = ROT // 2
    inverse = jnp.power(10000.0, -jnp.asarray(lane % half_rot, jnp.float32) * 2.0 / ROT)
    positions = (
        lengths[:, None] + jnp.arange(fresh_len, dtype=jnp.int32)[None, :]
    ).astype(jnp.float32)
    angles = positions.reshape(rows, 1) * inverse[None, :]
    turns = jnp.asarray(lane < ROT)[None, :]
    cosine = jnp.where(turns, jnp.cos(angles), 1.0)
    sine = jnp.sin(angles)
    sine_up = jnp.where(jnp.asarray(lane < half_rot)[None, :], -sine, 0.0)
    sine_down = jnp.where(turns & jnp.asarray(lane >= half_rot)[None, :], sine, 0.0)

    normed = pl.pallas_call(
        functools.partial(norm_kernel, wgt_size, chips),
        out_shape=[jax.ShapeDtypeStruct((rows, block), jnp.bfloat16)] * chips,
        in_specs=[SMEM] + [ANY] * (2 * wgt_size - 1) + [VMEM] * 2,
        out_specs=[VMEM] * chips,
        scratch_shapes=[
            pltpu.VMEM((wgt_size, rows, width), jnp.bfloat16),
            pltpu.SemaphoreType.DMA((2 * wgt_size - 1,)),
        ],
        compiler_params=pltpu.CompilerParams(vmem_limit_bytes=VMEM_LIMIT),
        name="norm",
    )(
        jnp.stack([layer, chip]).astype(jnp.int32),
        own,
        *upward,
        *downward,
        ln_gain.astype(jnp.float32).reshape(chips, 1, block),
        ln_bias.astype(jnp.float32).reshape(chips, 1, block),
    )

    tokens = []
    for distance in range(chips):
        mine = normed[distance] if distance == 0 else swap(normed[distance], 2 * distance)
        tokens += [mine, swap(mine, 1)]

    place = jnp.stack([core]).astype(jnp.int32)
    partial = pl.pallas_call(
        functools.partial(project_kernel, fresh_len, req_count),
        out_shape=[jax.ShapeDtypeStruct((rows, half_cols), jnp.bfloat16)] * req_size,
        in_specs=[SMEM] * 2 + [ANY] * (req_size + 2),
        out_specs=[VMEM] * req_size,
        scratch_shapes=[
            pltpu.VMEM((everyone, fresh_len, block), jnp.bfloat16),
            pltpu.VMEM((block, half_cols), jnp.bfloat16),
            pltpu.VMEM((2 * rows, block), jnp.bfloat16),
            pltpu.SemaphoreType.DMA((req_size,)),
            pltpu.SemaphoreType.DMA((2,)),
        ],
        compiler_params=pltpu.CompilerParams(vmem_limit_bytes=VMEM_LIMIT),
        name="project",
    )(
        place,
        source,
        *[token.reshape(req_count, fresh_len, block) for token in tokens],
        own_rows,
        other_rows,
    )

    parts = [partial[0]] + [swap(partial[distance], distance) for distance in range(1, req_size)]

    slots = page_table.shape[1] * (req_count + 1) // 2
    out = jax.ShapeDtypeStruct((req_count, fresh_len, heads * HEAD), jnp.bfloat16)
    return pl.pallas_call(
        functools.partial(attend_kernel, (req_size, req_count, fresh_len, page, heads)),
        out_shape=[out] * 3,
        in_specs=[SMEM] * 3 + [VMEM] * (req_size + 4) + [ANY] * 2,
        out_specs=[VMEM] * 3,
        scratch_shapes=[
            pltpu.VMEM((slots, page, heads * HEAD), jnp.bfloat16),
            pltpu.VMEM((slots, page, heads * HEAD), jnp.bfloat16),
            pltpu.SemaphoreType.DMA((req_count,)),
        ],
        compiler_params=pltpu.CompilerParams(vmem_limit_bytes=VMEM_LIMIT),
        name="attend",
    )(
        place,
        lengths,
        page_table,
        *parts,
        qkv_bias.astype(jnp.float32).reshape(1, local_cols),
        cosine,
        sine_up,
        sine_down,
        key_pool,
        value_pool,
    )


def solution(mesh):
    in_specs = (
        P("req", None, "wgt"),
        P(),
        P("req"),
        P("req", None),
        P(),
        P(),
        P("req", "wgt"),
        P("wgt"),
        P("req", None, "wgt"),
        P("req", None, "wgt"),
    )
    out_specs = (P("req", None, "wgt"), P("req", None, "wgt"), P("req", None, "wgt"))
    return jax.shard_map(
        functools.partial(per_device, mesh.shape["req"], mesh.shape["wgt"]),
        mesh=mesh,
        in_specs=in_specs,
        out_specs=out_specs,
        check_vma=False,
    )
```

```python
import functools
import math

import jax
import jax.numpy as jnp
import numpy as np
from jax import lax
from jax.experimental import pallas as pl
from jax.experimental.pallas import tpu as pltpu
from jax.sharding import PartitionSpec as P

HEAD = 96
ROT = 24
EPS = 1e-05
LANES = 128
WINDOW = 2 * LANES
CHUNK_PAGES = 4
MIB = 1024 * 1024

ANY = pl.BlockSpec(memory_space=pl.ANY)
SMEM = pl.BlockSpec(memory_space=pltpu.SMEM)
VMEM = pl.BlockSpec(memory_space=pltpu.VMEM)


def plan_kernel(req_count, place, group_of, arrivals, slots, sources, *refs):
    chunks = refs[:2]
    order, slot_of, color, filled, sems = refs[2:]
    everyone = group_of.shape[0]
    groups = everyone // req_count
    half = req_count // 2
    me = place[0]

    def clear(group, carry):
        filled[group] = 0
        return carry

    lax.fori_loop(0, groups, clear, 0)

    def rank(item, carry):
        group = group_of[item]
        slot = group * req_count + filled[group]
        filled[group] = filled[group] + 1
        slot_of[item] = slot
        order[slot] = item
        color[item] = -1
        return carry

    lax.fori_loop(0, everyone, rank, 0)

    def walk(pair, carry):
        def body(state):
            item = state[0]
            color[item] = 0
            color[item ^ 1] = 1
            following = order[slot_of[item ^ 1] ^ 1]
            return following, color[following]

        lax.while_loop(lambda state: state[1] < 0, body, (2 * pair, color[2 * pair]))
        return carry

    lax.fori_loop(0, everyone // 2, walk, 0)

    copies = []
    for pair in range(half):
        first = color[me * req_count + 2 * pair]
        for part in range(2):
            copies.append(
                pltpu.make_async_copy(
                    arrivals.at[2 * pair + (first ^ part)],
                    chunks[part].at[pair],
                    sems.at[part * half + pair],
                )
            )
    for copy in copies:
        copy.start()

    def pick(group, pair, part):
        begin = group * req_count + 2 * pair
        return 2 * pair + (color[order[begin]] ^ part)

    for pair in range(half):
        for part in range(2):
            slots[part * half + pair] = pick(me, pair, part)

    def trace(distance, carry):
        group = me ^ distance
        for pair in range(half):
            for part in range(2):
                item = order[group * req_count + pick(group, pair, part)]
                origin = lax.div(item, req_count) ^ me
                within = lax.div(lax.rem(item, req_count), 2)
                sources[(part * groups + distance) * half + pair] = origin * half + within
        return carry

    lax.fori_loop(0, groups, trace, 0)
    for copy in copies:
        copy.wait()


def norm_kernel(depth, chips, place, *refs):
    pieces = refs[: 2 * depth - 1]
    gain, bias = refs[2 * depth - 1 : 2 * depth + 1]
    outs = refs[2 * depth + 1 : 2 * depth + 1 + chips]
    held, sems = refs[2 * depth + 1 + chips :]
    me, chip = place[0], place[1]
    copies = []
    for index, piece in enumerate(pieces):
        if index == 0:
            offset = 0
        elif index < depth:
            offset = -index
        else:
            offset = index - depth + 1
        copies.append((offset, pltpu.make_async_copy(piece, held.at[me + offset], sems.at[index])))

    def inside(offset):
        return (me + offset >= 0) & (me + offset < depth)

    for offset, copy in copies:

        @pl.when(inside(offset))
        def _():
            copy.start()

    for offset, copy in copies:

        @pl.when(inside(offset))
        def _():
            copy.wait()

    rows, width = held.shape[1], held.shape[2]
    step = 16
    total_width = depth * width
    block = total_width // chips
    per = chips // depth

    def body(index, carry):
        at = pl.ds(pl.multiple_of(index * step, step), step)
        values = [held[part, at, :].astype(jnp.float32) for part in range(depth)]
        total = sum(jnp.sum(value, axis=-1, keepdims=True) for value in values)
        center = total / total_width
        square = sum(
            jnp.sum(jnp.square(value - center), axis=-1, keepdims=True) for value in values
        )
        scale = lax.rsqrt(square / total_width + EPS)
        for offset in range(chips):
            target = chip ^ offset
            part = target // per
            lane = pl.ds(pl.multiple_of((target % per) * block, LANES), block)
            value = held[part, at, lane].astype(jnp.float32)
            value = (value - center) * scale * gain[target] + bias[target]
            outs[offset][at, :] = value.astype(jnp.bfloat16)
        return carry

    lax.fori_loop(0, rows // step, body, 0)


def project_kernel(fresh_len, held_count, part, place, source, *refs):
    groups = (len(refs) - 7) // 2
    tokens = refs[:groups]
    own_rows, other_rows = refs[groups : groups + 2]
    outs = refs[groups + 2 : 2 * groups + 2]
    held, weights, picked, sems, weight_sems = refs[2 * groups + 2 :]
    core = place[0]
    depth = own_rows.shape[0]
    copies = [
        pltpu.make_async_copy(
            own_rows,
            weights.at[pl.ds(pl.multiple_of(core * depth, 16), depth)],
            weight_sems.at[0],
        ),
        pltpu.make_async_copy(
            other_rows,
            weights.at[pl.ds(pl.multiple_of((1 - core) * depth, 16), depth)],
            weight_sems.at[1],
        ),
    ]
    copies += [
        pltpu.make_async_copy(
            token, held.at[pl.ds(index * held_count, held_count)], sems.at[index]
        )
        for index, token in enumerate(tokens)
    ]
    for copy in copies:
        copy.start()
    for copy in copies:
        copy.wait()
    rows = held_count * fresh_len
    together = min(groups, 4)
    for first in range(0, groups, together):
        for item in range(together * held_count):
            picked[item * fresh_len : (item + 1) * fresh_len, :] = held[
                source[(part * groups + first) * held_count + item]
            ]
        result = jnp.dot(picked[...], weights[...], preferred_element_type=jnp.float32).astype(
            jnp.bfloat16
        )
        for index in range(together):
            outs[first + index][...] = result[index * rows : (index + 1) * rows]


def attend_kernel(shape, place, slots, all_lengths, table, *refs):
    groups, held_count, fresh_len, page, heads, part = shape
    parts = refs[:groups]
    bias, cosine, sine_up, sine_down, key_pool, value_pool = refs[groups : groups + 6]
    outs = refs[-9:-6]
    keys, values, ready, sems, out_sems, new_sems = refs[-6:]
    core = place[0]
    chunk = CHUNK_PAGES * page
    pairs = heads // 2

    slot = [slots[part * held_count + index] for index in range(held_count)]
    lengths = [all_lengths[slot[index]] for index in range(held_count)]
    counts = [pl.cdiv(lengths[index], chunk) for index in range(held_count)]
    bases = [jnp.int32(0)]
    for count in counts[:-1]:
        bases.append(bases[-1] + count * CHUNK_PAGES)

    def copies(index, entry):
        number = table[slot[index], entry]
        to = bases[index] + entry
        return (
            pltpu.make_async_copy(key_pool.at[number], keys.at[to], sems.at[index]),
            pltpu.make_async_copy(value_pool.at[number], values.at[to], sems.at[index]),
        )

    for index in range(held_count):

        def start(entry, carry, index=index):
            for copy in copies(index, entry):
                copy.start()
            return carry

        lax.fori_loop(0, counts[index] * CHUNK_PAGES, start, 0)

    even = sum(parts[index][...].astype(jnp.float32) for index in range(0, groups, 2))
    odd = sum(parts[index][...].astype(jnp.float32) for index in range(1, groups, 2))
    halves = (jnp.where(core == 0, even, odd), jnp.where(core == 0, odd, even))
    halves = [
        half + bias[:, side * half.shape[1] : (side + 1) * half.shape[1]]
        for side, half in enumerate(halves)
    ]

    def kind(which):
        pieces = []
        for head in range(heads):
            half = halves[head // pairs]
            begin = (head % pairs) * 3 * HEAD + which * HEAD
            pieces.append(half[:, begin : begin + HEAD])
        return jnp.concatenate(pieces, axis=1)

    width = heads * HEAD

    def rows_of(ref):
        return jnp.concatenate([ref[slot[index]] for index in range(held_count)], axis=0)

    cosine, sine_up, sine_down = rows_of(cosine), rows_of(sine_up), rows_of(sine_down)

    def turn(block):
        half_rot = ROT // 2
        return (
            block * cosine
            + pltpu.roll(block, width - half_rot, 1) * sine_up
            + pltpu.roll(block, half_rot, 1) * sine_down
        )

    queries = turn(kind(0)).astype(jnp.bfloat16)
    turned = turn(kind(1)).astype(jnp.bfloat16)
    plain = kind(2).astype(jnp.bfloat16)
    for index in range(held_count):
        rows = slice(index * fresh_len, (index + 1) * fresh_len)
        ready[1, index] = turned[rows]
        ready[2, index] = plain[rows]
    new_copies = [
        pltpu.make_async_copy(
            ready.at[which, index], outs[which].at[slot[index]], new_sems.at[which - 1, index]
        )
        for which in (1, 2)
        for index in range(held_count)
    ]
    for copy in new_copies:
        copy.start()

    factor = 1.0 / math.sqrt(HEAD) / math.log(2.0)
    starts = [(2 * HEAD * pair) // LANES * LANES for pair in range(pairs)]
    lane = lax.broadcasted_iota(jnp.int32, (fresh_len, WINDOW), 1)

    def owned(pair, member):
        begin = (2 * pair + member) * HEAD - starts[pair]
        return (lane >= begin) & (lane < begin + HEAD)

    def contract(left, right):
        return lax.dot_general(
            left, right, (((1,), (1,)), ((), ())), preferred_element_type=jnp.float32
        )

    zero = jnp.zeros((fresh_len, WINDOW), jnp.bfloat16)
    spread_rows = heads * fresh_len
    row = lax.broadcasted_iota(jnp.int32, (2 * fresh_len, fresh_len), 0)
    causal_pair = lax.rem(row, fresh_len) >= lax.broadcasted_iota(
        jnp.int32, (2 * fresh_len, fresh_len), 1
    )
    for index in range(held_count):
        rows = slice(index * fresh_len, (index + 1) * fresh_len)
        spread = []
        for pair in range(pairs):
            window = queries[rows, starts[pair] : starts[pair] + WINDOW]
            spread.append(
                jnp.concatenate(
                    [jnp.where(owned(pair, member), window, zero) for member in range(2)], axis=0
                )
            )
        scores = jnp.concatenate(
            [
                jnp.where(
                    causal_pair,
                    contract(spread[pair], turned[rows, starts[pair] : starts[pair] + WINDOW]),
                    -1e30,
                )
                for pair in range(pairs)
            ],
            axis=0,
        )
        peak = jnp.max(scores, axis=1, keepdims=True)
        weight = jnp.exp2((scores - peak) * factor)
        denom = jnp.sum(weight, axis=1, keepdims=True)
        weight = weight.astype(jnp.bfloat16)
        mixed = jnp.concatenate(
            [
                jnp.dot(
                    weight[pair * 2 * fresh_len : (pair + 1) * 2 * fresh_len],
                    plain[rows, starts[pair] : starts[pair] + WINDOW],
                    preferred_element_type=jnp.float32,
                )
                for pair in range(pairs)
            ],
            axis=0,
        )

        def finish(entry, carry, index=index):
            for copy in copies(index, entry):
                copy.wait()
            return carry

        lax.fori_loop(0, counts[index] * CHUNK_PAGES, finish, 0)

        def step(part, carry, index=index, spread=spread):
            peak, denom, mixed = carry
            first = bases[index] + part * CHUNK_PAGES
            key_block = keys[pl.ds(first, CHUNK_PAGES)].reshape(chunk, width)
            scores = jnp.concatenate(
                [
                    contract(spread[pair], key_block[:, starts[pair] : starts[pair] + WINDOW])
                    for pair in range(pairs)
                ],
                axis=0,
            )
            position = part * chunk + lax.broadcasted_iota(jnp.int32, (spread_rows, chunk), 1)
            scores = jnp.where(position < lengths[index], scores, -1e30)
            higher = jnp.maximum(peak, jnp.max(scores, axis=1, keepdims=True))
            shrink = jnp.exp2((peak - higher) * factor)
            weight = jnp.exp2((scores - higher) * factor)
            denom = denom * shrink + jnp.sum(weight, axis=1, keepdims=True)
            weight = weight.astype(jnp.bfloat16)
            value_block = values[pl.ds(first, CHUNK_PAGES)].reshape(chunk, width)
            added = jnp.concatenate(
                [
                    jnp.dot(
                        weight[pair * 2 * fresh_len : (pair + 1) * 2 * fresh_len],
                        value_block[:, starts[pair] : starts[pair] + WINDOW],
                        preferred_element_type=jnp.float32,
                    )
                    for pair in range(pairs)
                ],
                axis=0,
            )
            return higher, denom, mixed * shrink + added

        peak, denom, mixed = lax.fori_loop(0, counts[index], step, (peak, denom, mixed))
        mixed = mixed / denom
        tiles = [None] * (width // LANES)
        for pair in range(pairs):
            for member in range(2):
                begin = (2 * pair + member) * fresh_len
                part = jnp.where(owned(pair, member), mixed[begin : begin + fresh_len], 0.0)
                for side in range(2):
                    place_at = starts[pair] // LANES + side
                    tile = part[:, side * LANES : (side + 1) * LANES]
                    tiles[place_at] = tile if tiles[place_at] is None else tiles[place_at] + tile
        ready[0, index] = jnp.concatenate(tiles, axis=1).astype(jnp.bfloat16)
        new_copies.append(
            pltpu.make_async_copy(
                ready.at[0, index], outs[0].at[slot[index]], out_sems.at[index]
            )
        )
        new_copies[-1].start()
    for copy in new_copies:
        copy.wait()


def per_device(
    req_size,
    wgt_size,
    arrivals,
    group_of,
    lengths,
    page_table,
    ln_gain,
    ln_bias,
    w_qkv,
    qkv_bias,
    key_pool,
    value_pool,
):
    req_count, fresh_len, width = arrivals.shape
    rows = req_count * fresh_len
    depth, local_cols = w_qkv.shape
    half_cols = local_cols // 2
    heads = local_cols // (3 * HEAD)
    page = key_pool.shape[1]
    chips = req_size // 2
    block = 2 * depth
    everyone = group_of.shape[0]
    me = lax.axis_index("req")
    layer = lax.axis_index("wgt")
    core = me & 1
    chip = me >> 1

    def swap(value, distance):
        return lax.ppermute(
            value, "req", [(device, device ^ distance) for device in range(req_size)]
        )

    own_rows = lax.dynamic_slice_in_dim(w_qkv, core * half_cols, half_cols, 1)
    other_rows = swap(lax.dynamic_slice_in_dim(w_qkv, (1 - core) * half_cols, half_cols, 1), 1)

    half = req_count // 2
    piece = jax.ShapeDtypeStruct((half, fresh_len, width), jnp.bfloat16)
    slots, sources, *chunks = pl.pallas_call(
        functools.partial(plan_kernel, req_count),
        out_shape=[
            jax.ShapeDtypeStruct((2 * half,), jnp.int32),
            jax.ShapeDtypeStruct((2 * req_size * half,), jnp.int32),
            piece,
            piece,
        ],
        in_specs=[SMEM, SMEM, ANY],
        out_specs=[SMEM, SMEM, ANY, ANY],
        scratch_shapes=[
            pltpu.SMEM((everyone,), jnp.int32),
            pltpu.SMEM((everyone,), jnp.int32),
            pltpu.SMEM((everyone,), jnp.int32),
            pltpu.SMEM((req_size,), jnp.int32),
            pltpu.SemaphoreType.DMA((2 * half,)),
        ],
        name="plan",
    )(jnp.stack([me]).astype(jnp.int32), group_of, arrivals)

    lane = np.arange(heads * HEAD) % HEAD
    half_rot = ROT // 2
    inverse = jnp.power(10000.0, -jnp.asarray(lane % half_rot, jnp.float32) * 2.0 / ROT)
    positions = (
        lengths[:, None] + jnp.arange(fresh_len, dtype=jnp.int32)[None, :]
    ).astype(jnp.float32)
    angles = positions.reshape(rows, 1) * inverse[None, :]
    turns = jnp.asarray(lane < ROT)[None, :]
    cosine = jnp.where(turns, jnp.cos(angles), 1.0)
    sine = jnp.sin(angles)
    sine_up = jnp.where(jnp.asarray(lane < half_rot)[None, :], -sine, 0.0)
    sine_down = jnp.where(turns & jnp.asarray(lane >= half_rot)[None, :], sine, 0.0)

    tables = [
        value.reshape(req_count, fresh_len, heads * HEAD)
        for value in (cosine, sine_up, sine_down)
    ]
    gain = ln_gain.astype(jnp.float32).reshape(chips, 1, block)
    shift = ln_bias.astype(jnp.float32).reshape(chips, 1, block)
    bias = qkv_bias.astype(jnp.float32).reshape(1, local_cols)
    place = jnp.stack([core]).astype(jnp.int32)
    where = jnp.stack([layer, chip]).astype(jnp.int32)
    chunk_rows = half * fresh_len
    span = page_table.shape[1]
    pages = span + (half - 1) * (span // 2)
    out = jax.ShapeDtypeStruct((req_count, fresh_len, heads * HEAD), jnp.bfloat16)

    pieces = [[chunk.reshape(chunk_rows, width)] for chunk in chunks]
    ends = [(own[0], own[0]) for own in pieces]
    downs = [[], []]
    for hop in range(1, wgt_size):
        for part in range(2):
            up, down = ends[part]
            up = lax.ppermute(up, "wgt", [(at, at + 1) for at in range(hop - 1, wgt_size - 1)])
            down = lax.ppermute(down, "wgt", [(at + 1, at) for at in range(wgt_size - hop)])
            ends[part] = (up, down)
            pieces[part].append(up)
            downs[part].append(down)

    results = []
    for part in range(2):
        normed = pl.pallas_call(
            functools.partial(norm_kernel, wgt_size, chips),
            out_shape=[jax.ShapeDtypeStruct((chunk_rows, block), jnp.bfloat16)] * chips,
            in_specs=[SMEM] + [ANY] * (2 * wgt_size - 1) + [VMEM] * 2,
            out_specs=[VMEM] * chips,
            scratch_shapes=[
                pltpu.VMEM((wgt_size, chunk_rows, width), jnp.bfloat16),
                pltpu.SemaphoreType.DMA((2 * wgt_size - 1,)),
            ],
            compiler_params=pltpu.CompilerParams(vmem_limit_bytes=12 * MIB),
            name="norm",
        )(where, *pieces[part], *downs[part], gain, shift)

        tokens = []
        for distance in range(chips):
            mine = normed[distance] if distance == 0 else swap(normed[distance], 2 * distance)
            tokens += [mine, swap(mine, 1)]

        partial = pl.pallas_call(
            functools.partial(project_kernel, fresh_len, half, part),
            out_shape=[jax.ShapeDtypeStruct((chunk_rows, half_cols), jnp.bfloat16)] * req_size,
            in_specs=[SMEM] * 2 + [ANY] * (req_size + 2),
            out_specs=[VMEM] * req_size,
            scratch_shapes=[
                pltpu.VMEM((req_size * half, fresh_len, block), jnp.bfloat16),
                pltpu.VMEM((block, half_cols), jnp.bfloat16),
                pltpu.VMEM((min(req_size, 4) * chunk_rows, block), jnp.bfloat16),
                pltpu.SemaphoreType.DMA((req_size,)),
                pltpu.SemaphoreType.DMA((2,)),
            ],
            compiler_params=pltpu.CompilerParams(vmem_limit_bytes=20 * MIB),
            name="project",
        )(
            place,
            sources,
            *[token.reshape(half, fresh_len, block) for token in tokens],
            own_rows,
            other_rows,
        )

        parts = [partial[0]]
        parts += [swap(partial[distance], distance) for distance in range(1, req_size)]

        operands = [
            place, slots, lengths, page_table, *parts, bias, *tables, key_pool, value_pool
        ]
        specs = [SMEM] * 4 + [VMEM] * (req_size + 4) + [ANY] * 2
        results = pl.pallas_call(
            functools.partial(
                attend_kernel, (req_size, half, fresh_len, page, heads, part)
            ),
            out_shape=[out] * 3,
            in_specs=specs + [ANY] * len(results),
            out_specs=[ANY] * 3,
            scratch_shapes=[
                pltpu.VMEM((pages, page, heads * HEAD), jnp.bfloat16),
                pltpu.VMEM((pages, page, heads * HEAD), jnp.bfloat16),
                pltpu.VMEM((3, half, fresh_len, heads * HEAD), jnp.bfloat16),
                pltpu.SemaphoreType.DMA((half,)),
                pltpu.SemaphoreType.DMA((half,)),
                pltpu.SemaphoreType.DMA((2, half)),
            ],
            input_output_aliases={len(specs) + index: index for index in range(len(results))},
            compiler_params=pltpu.CompilerParams(vmem_limit_bytes=24 * MIB),
            name="attend",
        )(*operands, *results)
    return results


def solution(mesh):
    in_specs = (
        P("req", None, "wgt"),
        P(),
        P("req"),
        P("req", None),
        P(),
        P(),
        P("req", "wgt"),
        P("wgt"),
        P("req", None, "wgt"),
        P("req", None, "wgt"),
    )
    out_specs = (P("req", None, "wgt"), P("req", None, "wgt"), P("req", None, "wgt"))
    return jax.shard_map(
        functools.partial(per_device, mesh.shape["req"], mesh.shape["wgt"]),
        mesh=mesh,
        in_specs=in_specs,
        out_specs=out_specs,
        check_vma=False,
    )
```

```python
import functools
import math

import jax
import jax.numpy as jnp
import numpy as np
from jax import lax
from jax.experimental import pallas as pl
from jax.experimental.pallas import tpu as pltpu
from jax.sharding import PartitionSpec as P

HEAD = 96
ROT = 24
EPS = 1e-05
LANES = 128
WINDOW = 2 * LANES
CHUNK_PAGES = 4
MIB = 1024 * 1024

ANY = pl.BlockSpec(memory_space=pl.ANY)
SMEM = pl.BlockSpec(memory_space=pltpu.SMEM)
VMEM = pl.BlockSpec(memory_space=pltpu.VMEM)


def plan_kernel(req_count, place, group_of, arrivals, slots, sources, *refs):
    chunks = refs[:2]
    order, slot_of, color, filled, sems = refs[2:]
    everyone = group_of.shape[0]
    groups = everyone // req_count
    half = req_count // 2
    me = place[0]

    def clear(group, carry):
        filled[group] = 0
        return carry

    lax.fori_loop(0, groups, clear, 0)

    def rank(item, carry):
        group = group_of[item]
        slot = group * req_count + filled[group]
        filled[group] = filled[group] + 1
        slot_of[item] = slot
        order[slot] = item
        color[item] = -1
        return carry

    lax.fori_loop(0, everyone, rank, 0)

    shift = req_count.bit_length() - 1

    def note(item, shade):
        color[item] = shade
        slot = slot_of[item]
        to = (shade * groups + (slot >> shift)) * half + ((slot & (req_count - 1)) >> 1)
        sources[to] = ((item >> shift) ^ me) * half + ((item & (req_count - 1)) >> 1)
        return slot

    def walk(pair, carry):
        def body(state):
            note(state[0], 0)
            following = order[note(state[0] ^ 1, 1) ^ 1]
            return following, color[following]

        lax.while_loop(lambda state: state[1] < 0, body, (2 * pair, color[2 * pair]))
        return carry

    lax.fori_loop(0, everyone // 2, walk, 0)

    copies = []
    for pair in range(half):
        first = color[me * req_count + 2 * pair]
        for part in range(2):
            copies.append(
                pltpu.make_async_copy(
                    arrivals.at[2 * pair + (first ^ part)],
                    chunks[part].at[pair],
                    sems.at[part * half + pair],
                )
            )
    for copy in copies:
        copy.start()
    for pair in range(half):
        first = color[order[me * req_count + 2 * pair]]
        for part in range(2):
            slots[part * half + pair] = 2 * pair + (first ^ part)
    for copy in copies:
        copy.wait()


def norm_kernel(depth, chips, place, *refs):
    pieces = refs[: 2 * depth - 1]
    gain, bias = refs[2 * depth - 1 : 2 * depth + 1]
    outs = refs[2 * depth + 1 : 2 * depth + 1 + chips]
    held, sems = refs[2 * depth + 1 + chips :]
    me, chip = place[0], place[1]
    copies = []
    for index, piece in enumerate(pieces):
        if index == 0:
            offset = 0
        elif index < depth:
            offset = -index
        else:
            offset = index - depth + 1
        copies.append((offset, pltpu.make_async_copy(piece, held.at[me + offset], sems.at[index])))

    def inside(offset):
        return (me + offset >= 0) & (me + offset < depth)

    for offset, copy in copies:

        @pl.when(inside(offset))
        def _():
            copy.start()

    for offset, copy in copies:

        @pl.when(inside(offset))
        def _():
            copy.wait()

    rows, width = held.shape[1], held.shape[2]
    step = 16
    total_width = depth * width
    block = total_width // chips
    per = chips // depth

    def body(index, carry):
        at = pl.ds(pl.multiple_of(index * step, step), step)
        values = [held[part, at, :].astype(jnp.float32) for part in range(depth)]
        total = sum(jnp.sum(value, axis=-1, keepdims=True) for value in values)
        center = total / total_width
        square = sum(
            jnp.sum(jnp.square(value - center), axis=-1, keepdims=True) for value in values
        )
        scale = lax.rsqrt(square / total_width + EPS)
        for offset in range(chips):
            target = chip ^ offset
            part = target // per
            lane = pl.ds(pl.multiple_of((target % per) * block, LANES), block)
            value = held[part, at, lane].astype(jnp.float32)
            value = (value - center) * scale * gain[target] + bias[target]
            outs[offset][at, :] = value.astype(jnp.bfloat16)
        return carry

    lax.fori_loop(0, rows // step, body, 0)


def project_kernel(fresh_len, held_count, part, place, source, *refs):
    groups = len(refs) - 8
    tokens = refs[:groups]
    own_rows, other_rows = refs[groups : groups + 2]
    out, held, weights, picked, sems, weight_sems = refs[groups + 2 :]
    core = place[0]
    depth = own_rows.shape[0]
    copies = [
        pltpu.make_async_copy(
            own_rows,
            weights.at[pl.ds(pl.multiple_of(core * depth, 16), depth)],
            weight_sems.at[0],
        ),
        pltpu.make_async_copy(
            other_rows,
            weights.at[pl.ds(pl.multiple_of((1 - core) * depth, 16), depth)],
            weight_sems.at[1],
        ),
    ]
    copies += [
        pltpu.make_async_copy(
            token, held.at[pl.ds(index * held_count, held_count)], sems.at[index]
        )
        for index, token in enumerate(tokens)
    ]
    for copy in copies:
        copy.start()
    for copy in copies:
        copy.wait()
    rows = held_count * fresh_len
    together = min(groups, 4)
    for first in range(0, groups, together):
        for item in range(together * held_count):
            picked[item * fresh_len : (item + 1) * fresh_len, :] = held[
                source[(part * groups + first) * held_count + item]
            ]
        result = jnp.dot(picked[...], weights[...], preferred_element_type=jnp.float32).astype(
            jnp.bfloat16
        )
        for index in range(together):
            out[first + index] = result[index * rows : (index + 1) * rows]


def attend_kernel(shape, slots, all_lengths, table, *refs):
    groups, held_count, fresh_len, page, heads, part = shape
    parts, bias, cosine, sine_up, sine_down, key_pool, value_pool = refs[:7]
    outs = refs[-6:-3]
    ready, out_sems, new_sems = refs[-3:]
    chunk = CHUNK_PAGES * page
    pairs = heads // 2

    slot = [slots[part * held_count + index] for index in range(held_count)]
    lengths = [all_lengths[slot[index]] for index in range(held_count)]
    counts = [pl.cdiv(lengths[index], chunk) for index in range(held_count)]

    def cached(pool, index, first, pair):
        return jnp.concatenate(
            [
                pool[table[slot[index], first + entry], :, starts[pair] : starts[pair] + WINDOW]
                for entry in range(CHUNK_PAGES)
            ],
            axis=0,
        )

    halves = [
        sum(parts[index].astype(jnp.float32) for index in range(side, groups, 2))
        for side in range(2)
    ]
    halves = [
        half + bias[:, side * half.shape[1] : (side + 1) * half.shape[1]]
        for side, half in enumerate(halves)
    ]

    def kind(which):
        pieces = []
        for head in range(heads):
            half = halves[head // pairs]
            begin = (head % pairs) * 3 * HEAD + which * HEAD
            pieces.append(half[:, begin : begin + HEAD])
        return jnp.concatenate(pieces, axis=1)

    width = heads * HEAD

    def rows_of(ref):
        return jnp.concatenate([ref[slot[index]] for index in range(held_count)], axis=0)

    cosine, sine_up, sine_down = rows_of(cosine), rows_of(sine_up), rows_of(sine_down)

    def turn(block):
        half_rot = ROT // 2
        return (
            block * cosine
            + pltpu.roll(block, width - half_rot, 1) * sine_up
            + pltpu.roll(block, half_rot, 1) * sine_down
        )

    queries = turn(kind(0)).astype(jnp.bfloat16)
    turned = turn(kind(1)).astype(jnp.bfloat16)
    plain = kind(2).astype(jnp.bfloat16)
    for index in range(held_count):
        rows = slice(index * fresh_len, (index + 1) * fresh_len)
        ready[1, index] = turned[rows]
        ready[2, index] = plain[rows]
    new_copies = [
        pltpu.make_async_copy(
            ready.at[which, index], outs[which].at[slot[index]], new_sems.at[which - 1, index]
        )
        for which in (1, 2)
        for index in range(held_count)
    ]
    for copy in new_copies:
        copy.start()

    factor = 1.0 / math.sqrt(HEAD) / math.log(2.0)
    starts = [(2 * HEAD * pair) // LANES * LANES for pair in range(pairs)]
    lane = lax.broadcasted_iota(jnp.int32, (fresh_len, WINDOW), 1)

    def owned(pair, member):
        begin = (2 * pair + member) * HEAD - starts[pair]
        return (lane >= begin) & (lane < begin + HEAD)

    def contract(left, right):
        return lax.dot_general(
            left, right, (((1,), (1,)), ((), ())), preferred_element_type=jnp.float32
        )

    zero = jnp.zeros((fresh_len, WINDOW), jnp.bfloat16)
    spread_rows = heads * fresh_len
    row = lax.broadcasted_iota(jnp.int32, (2 * fresh_len, fresh_len), 0)
    causal_pair = lax.rem(row, fresh_len) >= lax.broadcasted_iota(
        jnp.int32, (2 * fresh_len, fresh_len), 1
    )
    for index in range(held_count):
        rows = slice(index * fresh_len, (index + 1) * fresh_len)
        spread = []
        for pair in range(pairs):
            window = queries[rows, starts[pair] : starts[pair] + WINDOW]
            spread.append(
                jnp.concatenate(
                    [jnp.where(owned(pair, member), window, zero) for member in range(2)], axis=0
                )
            )
        scores = jnp.concatenate(
            [
                jnp.where(
                    causal_pair,
                    contract(spread[pair], turned[rows, starts[pair] : starts[pair] + WINDOW]),
                    -1e30,
                )
                for pair in range(pairs)
            ],
            axis=0,
        )
        peak = jnp.max(scores, axis=1, keepdims=True)
        weight = jnp.exp2((scores - peak) * factor)
        denom = jnp.sum(weight, axis=1, keepdims=True)
        weight = weight.astype(jnp.bfloat16)
        mixed = jnp.concatenate(
            [
                jnp.dot(
                    weight[pair * 2 * fresh_len : (pair + 1) * 2 * fresh_len],
                    plain[rows, starts[pair] : starts[pair] + WINDOW],
                    preferred_element_type=jnp.float32,
                )
                for pair in range(pairs)
            ],
            axis=0,
        )

        def step(part, carry, index=index, spread=spread):
            peak, denom, mixed = carry
            first = part * CHUNK_PAGES
            scores = jnp.concatenate(
                [
                    contract(spread[pair], cached(key_pool, index, first, pair))
                    for pair in range(pairs)
                ],
                axis=0,
            )
            position = part * chunk + lax.broadcasted_iota(jnp.int32, (spread_rows, chunk), 1)
            scores = jnp.where(position < lengths[index], scores, -1e30)
            higher = jnp.maximum(peak, jnp.max(scores, axis=1, keepdims=True))
            shrink = jnp.exp2((peak - higher) * factor)
            weight = jnp.exp2((scores - higher) * factor)
            denom = denom * shrink + jnp.sum(weight, axis=1, keepdims=True)
            weight = weight.astype(jnp.bfloat16)
            added = jnp.concatenate(
                [
                    jnp.dot(
                        weight[pair * 2 * fresh_len : (pair + 1) * 2 * fresh_len],
                        cached(value_pool, index, first, pair),
                        preferred_element_type=jnp.float32,
                    )
                    for pair in range(pairs)
                ],
                axis=0,
            )
            return higher, denom, mixed * shrink + added

        peak, denom, mixed = lax.fori_loop(0, counts[index], step, (peak, denom, mixed))
        mixed = mixed / denom
        tiles = [None] * (width // LANES)
        for pair in range(pairs):
            for member in range(2):
                begin = (2 * pair + member) * fresh_len
                part = jnp.where(owned(pair, member), mixed[begin : begin + fresh_len], 0.0)
                for side in range(2):
                    place_at = starts[pair] // LANES + side
                    tile = part[:, side * LANES : (side + 1) * LANES]
                    tiles[place_at] = tile if tiles[place_at] is None else tiles[place_at] + tile
        ready[0, index] = jnp.concatenate(tiles, axis=1).astype(jnp.bfloat16)
        new_copies.append(
            pltpu.make_async_copy(
                ready.at[0, index], outs[0].at[slot[index]], out_sems.at[index]
            )
        )
        new_copies[-1].start()
    for copy in new_copies:
        copy.wait()


def per_device(
    req_size,
    wgt_size,
    arrivals,
    group_of,
    lengths,
    page_table,
    ln_gain,
    ln_bias,
    w_qkv,
    qkv_bias,
    key_pool,
    value_pool,
):
    req_count, fresh_len, width = arrivals.shape
    rows = req_count * fresh_len
    depth, local_cols = w_qkv.shape
    half_cols = local_cols // 2
    heads = local_cols // (3 * HEAD)
    page = key_pool.shape[1]
    chips = req_size // 2
    block = 2 * depth
    everyone = group_of.shape[0]
    me = lax.axis_index("req")
    layer = lax.axis_index("wgt")
    core = me & 1
    chip = me >> 1

    def swap(value, distance):
        return lax.ppermute(
            value, "req", [(device, device ^ distance) for device in range(req_size)]
        )

    own_rows = lax.dynamic_slice_in_dim(w_qkv, core * half_cols, half_cols, 1)
    other_rows = swap(lax.dynamic_slice_in_dim(w_qkv, (1 - core) * half_cols, half_cols, 1), 1)

    half = req_count // 2
    piece = jax.ShapeDtypeStruct((half, fresh_len, width), jnp.bfloat16)
    slots, sources, *chunks = pl.pallas_call(
        functools.partial(plan_kernel, req_count),
        out_shape=[
            jax.ShapeDtypeStruct((2 * half,), jnp.int32),
            jax.ShapeDtypeStruct((2 * req_size * half,), jnp.int32),
            piece,
            piece,
        ],
        in_specs=[SMEM, SMEM, ANY],
        out_specs=[SMEM, SMEM, ANY, ANY],
        scratch_shapes=[
            pltpu.SMEM((everyone,), jnp.int32),
            pltpu.SMEM((everyone,), jnp.int32),
            pltpu.SMEM((everyone,), jnp.int32),
            pltpu.SMEM((req_size,), jnp.int32),
            pltpu.SemaphoreType.DMA((2 * half,)),
        ],
        name="plan",
    )(jnp.stack([me]).astype(jnp.int32), group_of, arrivals)

    lane = np.arange(heads * HEAD) % HEAD
    half_rot = ROT // 2
    inverse = jnp.power(10000.0, -jnp.asarray(lane % half_rot, jnp.float32) * 2.0 / ROT)
    positions = (
        lengths[:, None] + jnp.arange(fresh_len, dtype=jnp.int32)[None, :]
    ).astype(jnp.float32)
    angles = positions.reshape(rows, 1) * inverse[None, :]
    turns = jnp.asarray(lane < ROT)[None, :]
    cosine = jnp.where(turns, jnp.cos(angles), 1.0)
    sine = jnp.sin(angles)
    sine_up = jnp.where(jnp.asarray(lane < half_rot)[None, :], -sine, 0.0)
    sine_down = jnp.where(turns & jnp.asarray(lane >= half_rot)[None, :], sine, 0.0)

    tables = [
        value.reshape(req_count, fresh_len, heads * HEAD)
        for value in (cosine, sine_up, sine_down)
    ]
    gain = ln_gain.astype(jnp.float32).reshape(chips, 1, block)
    shift = ln_bias.astype(jnp.float32).reshape(chips, 1, block)
    bias = qkv_bias.astype(jnp.float32).reshape(1, local_cols)
    place = jnp.stack([core]).astype(jnp.int32)
    where = jnp.stack([layer, chip]).astype(jnp.int32)
    chunk_rows = half * fresh_len
    out = jax.ShapeDtypeStruct((req_count, fresh_len, heads * HEAD), jnp.bfloat16)

    pieces = [[chunk.reshape(chunk_rows, width)] for chunk in chunks]
    ends = [(own[0], own[0]) for own in pieces]
    downs = [[], []]
    for part in range(2):
        for hop in range(1, wgt_size):
            up, down = ends[part]
            if part == 1 and hop == 1:
                up, _ = lax.optimization_barrier((up, pieces[0][min(2, wgt_size - 1)]))
                down = up
            up = lax.ppermute(up, "wgt", [(at, at + 1) for at in range(hop - 1, wgt_size - 1)])
            down = lax.ppermute(down, "wgt", [(at + 1, at) for at in range(wgt_size - hop)])
            ends[part] = (up, down)
            pieces[part].append(up)
            downs[part].append(down)

    projected = []
    for part in range(2):
        if part == 1:
            pieces[1][-1], _ = lax.optimization_barrier((pieces[1][-1], projected[0]))
        normed = pl.pallas_call(
            functools.partial(norm_kernel, wgt_size, chips),
            out_shape=[jax.ShapeDtypeStruct((chunk_rows, block), jnp.bfloat16)] * chips,
            in_specs=[SMEM] + [ANY] * (2 * wgt_size - 1) + [VMEM] * 2,
            out_specs=[VMEM] * chips,
            scratch_shapes=[
                pltpu.VMEM((wgt_size, chunk_rows, width), jnp.bfloat16),
                pltpu.SemaphoreType.DMA((2 * wgt_size - 1,)),
            ],
            compiler_params=pltpu.CompilerParams(vmem_limit_bytes=12 * MIB),
            name="norm",
        )(where, *pieces[part], *downs[part], gain, shift)

        tokens = []
        for distance in range(chips):
            mine = normed[distance] if distance == 0 else swap(normed[distance], 2 * distance)
            tokens += [mine, swap(mine, 1)]

        partial = pl.pallas_call(
            functools.partial(project_kernel, fresh_len, half, part),
            out_shape=jax.ShapeDtypeStruct((req_size, chunk_rows, half_cols), jnp.bfloat16),
            in_specs=[SMEM] * 2 + [ANY] * (req_size + 2),
            out_specs=VMEM,
            scratch_shapes=[
                pltpu.VMEM((req_size * half, fresh_len, block), jnp.bfloat16),
                pltpu.VMEM((block, half_cols), jnp.bfloat16),
                pltpu.VMEM((min(req_size, 4) * chunk_rows, block), jnp.bfloat16),
                pltpu.SemaphoreType.DMA((req_size,)),
                pltpu.SemaphoreType.DMA((2,)),
            ],
            compiler_params=pltpu.CompilerParams(vmem_limit_bytes=20 * MIB),
            name="project",
        )(
            place,
            sources,
            *[token.reshape(half, fresh_len, block) for token in tokens],
            own_rows,
            other_rows,
        )

        projected.append(partial)

    results = []
    for part in range(2):
        parts = lax.all_to_all(projected[part], "req", 0, 0, tiled=True)

        operands = [
            slots, lengths, page_table, parts, bias, *tables, key_pool, value_pool
        ]
        specs = [SMEM] * 3 + [VMEM] * 7
        results = pl.pallas_call(
            functools.partial(
                attend_kernel, (req_size, half, fresh_len, page, heads, part)
            ),
            out_shape=[out] * 3,
            in_specs=specs + [ANY] * len(results),
            out_specs=[ANY] * 3,
            scratch_shapes=[
                pltpu.VMEM((3, half, fresh_len, heads * HEAD), jnp.bfloat16),
                pltpu.SemaphoreType.DMA((half,)),
                pltpu.SemaphoreType.DMA((2, half)),
            ],
            input_output_aliases={len(specs) + index: index for index in range(len(results))},
            compiler_params=pltpu.CompilerParams(vmem_limit_bytes=30 * MIB),
            name="attend",
        )(*operands, *results)
    return results


def solution(mesh):
    in_specs = (
        P("req", None, "wgt"),
        P(),
        P("req"),
        P("req", None),
        P(),
        P(),
        P("req", "wgt"),
        P("wgt"),
        P("req", None, "wgt"),
        P("req", None, "wgt"),
    )
    out_specs = (P("req", None, "wgt"), P("req", None, "wgt"), P("req", None, "wgt"))
    return jax.shard_map(
        functools.partial(per_device, mesh.shape["req"], mesh.shape["wgt"]),
        mesh=mesh,
        in_specs=in_specs,
        out_specs=out_specs,
        check_vma=False,
    )
```

```python
import functools
import math

import jax
import jax.numpy as jnp
import numpy as np
from jax import lax
from jax.experimental import pallas as pl
from jax.experimental.pallas import tpu as pltpu
from jax.sharding import PartitionSpec as P

HEAD = 96
ROT = 24
EPS = 1e-05
LANES = 128
WINDOW = 2 * LANES
CHUNK_PAGES = 4
MIB = 1024 * 1024

SMEM = pl.BlockSpec(memory_space=pltpu.SMEM)
VMEM = pl.BlockSpec(memory_space=pltpu.VMEM)
HBM = pl.BlockSpec(memory_space=pltpu.HBM)


def plan_kernel(req_count, place, group_of, arrivals, slots, sources, *refs):
    chunks = refs[:2]
    order, slot_of, color, filled, sems = refs[2:]
    everyone = group_of.shape[0]
    groups = everyone // req_count
    half = req_count // 2
    me = place[0]

    def clear(group, carry):
        filled[group] = 0
        return carry

    lax.fori_loop(0, groups, clear, 0)

    def rank(item, carry):
        group = group_of[item]
        slot = group * req_count + filled[group]
        filled[group] = filled[group] + 1
        slot_of[item] = slot
        order[slot] = item
        color[item] = -1
        return carry

    lax.fori_loop(0, everyone, rank, 0)

    shift = req_count.bit_length() - 1

    def note(item, shade):
        color[item] = shade
        slot = slot_of[item]
        to = (shade * groups + (slot >> shift)) * half + ((slot & (req_count - 1)) >> 1)
        sources[to] = ((item >> shift) ^ me) * half + ((item & (req_count - 1)) >> 1)
        return slot

    def walk(pair, carry):
        def body(state):
            note(state[0], 0)
            following = order[note(state[0] ^ 1, 1) ^ 1]
            return following, color[following]

        lax.while_loop(lambda state: state[1] < 0, body, (2 * pair, color[2 * pair]))
        return carry

    lax.fori_loop(0, everyone // 2, walk, 0)

    copies = []
    for pair in range(half):
        first = color[me * req_count + 2 * pair]
        for part in range(2):
            copies.append(
                pltpu.make_async_copy(
                    arrivals.at[2 * pair + (first ^ part)],
                    chunks[part].at[pair],
                    sems.at[part * half + pair],
                )
            )
    for copy in copies:
        copy.start()
    for pair in range(half):
        first = color[order[me * req_count + 2 * pair]]
        for part in range(2):
            slots[part * half + pair] = 2 * pair + (first ^ part)
    for copy in copies:
        copy.wait()


def norm_kernel(depth, chips, place, *refs):
    pieces = refs[: 2 * depth - 1]
    gain, bias = refs[2 * depth - 1 : 2 * depth + 1]
    outs = refs[2 * depth + 1 : 2 * depth + 1 + chips]
    held, sems = refs[2 * depth + 1 + chips :]
    me, chip = place[0], place[1]
    copies = []
    for index, piece in enumerate(pieces):
        if index == 0:
            offset = 0
        elif index < depth:
            offset = -index
        else:
            offset = index - depth + 1
        copies.append((offset, pltpu.make_async_copy(piece, held.at[me + offset], sems.at[index])))

    def inside(offset):
        return (me + offset >= 0) & (me + offset < depth)

    for offset, copy in copies:

        @pl.when(inside(offset))
        def _():
            copy.start()

    for offset, copy in copies:

        @pl.when(inside(offset))
        def _():
            copy.wait()

    rows, width = held.shape[1], held.shape[2]
    step = 16
    total_width = depth * width
    block = total_width // chips
    per = chips // depth

    def body(index, carry):
        at = pl.ds(pl.multiple_of(index * step, step), step)
        values = [held[part, at, :].astype(jnp.float32) for part in range(depth)]
        total = sum(jnp.sum(value, axis=-1, keepdims=True) for value in values)
        center = total / total_width
        square = sum(
            jnp.sum(jnp.square(value - center), axis=-1, keepdims=True) for value in values
        )
        scale = lax.rsqrt(square / total_width + EPS)
        for offset in range(chips):
            target = chip ^ offset
            part = target // per
            lane = pl.ds(pl.multiple_of((target % per) * block, LANES), block)
            value = held[part, at, lane].astype(jnp.float32)
            value = (value - center) * scale * gain[target] + bias[target]
            outs[offset][at, :] = value.astype(jnp.bfloat16)
        return carry

    lax.fori_loop(0, rows // step, body, 0, unroll=2)


def project_kernel(fresh_len, held_count, part, place, source, *refs):
    groups = len(refs) - 10
    tokens = refs[:groups]
    own_rows, other_rows = refs[groups : groups + 2]
    out, held, weights, picked, ready, sems, weight_sems, out_sems = refs[groups + 2 :]
    core = place[0]
    depth = own_rows.shape[0]
    copies = [
        pltpu.make_async_copy(
            own_rows,
            weights.at[pl.ds(pl.multiple_of(core * depth, 16), depth)],
            weight_sems.at[0],
        ),
        pltpu.make_async_copy(
            other_rows,
            weights.at[pl.ds(pl.multiple_of((1 - core) * depth, 16), depth)],
            weight_sems.at[1],
        ),
    ]
    copies += [
        pltpu.make_async_copy(
            token, held.at[pl.ds(index * held_count, held_count)], sems.at[index]
        )
        for index, token in enumerate(tokens)
    ]
    for copy in copies:
        copy.start()
    for copy in copies:
        copy.wait()
    rows = held_count * fresh_len
    together = min(groups, 4)
    for first in range(0, groups, together):
        for item in range(together * held_count):
            picked[item * fresh_len : (item + 1) * fresh_len, :] = held[
                source[(part * groups + first) * held_count + item]
            ]
        result = jnp.dot(picked[...], weights[...], preferred_element_type=jnp.float32).astype(
            jnp.bfloat16
        )
        for index in range(together):
            ready[first + index] = result[index * rows : (index + 1) * rows]
        targets = pl.ds(first, together)
        copies.append(
            pltpu.make_async_copy(
                ready.at[targets], out.at[targets], out_sems.at[first // together]
            )
        )
        copies[-1].start()
    for copy in copies[groups + 2 :]:
        copy.wait()


def attend_kernel(shape, slots, all_lengths, table, *refs):
    groups, held_count, fresh_len, page, heads, part = shape
    parts, bias, cosine, sine_up, sine_down, key_pool, value_pool = refs[:7]
    before = refs[7:-6]
    outs = refs[-6:-3]
    keys, values, sems = refs[-3:]
    chunk = CHUNK_PAGES * page
    pairs = heads // 2

    slot = [slots[part * held_count + index] for index in range(held_count)]
    lengths = [all_lengths[slot[index]] for index in range(held_count)]
    counts = [pl.cdiv(lengths[index], chunk) for index in range(held_count)]
    bases = [jnp.int32(0)]
    for count in counts[:-1]:
        bases.append(bases[-1] + count * CHUNK_PAGES)

    def copies(index, entry):
        number = table[slot[index], entry]
        to = bases[index] + entry
        return (
            pltpu.make_async_copy(key_pool.at[number], keys.at[to], sems.at[index]),
            pltpu.make_async_copy(value_pool.at[number], values.at[to], sems.at[index]),
        )

    for index in range(held_count):

        def start(entry, carry, index=index):
            for copy in copies(index, entry):
                copy.start()
            return carry

        lax.fori_loop(0, counts[index] * CHUNK_PAGES, start, 0)

    def cached(pages, index, part, pair):
        held = pages[
            pl.ds(bases[index] + part * CHUNK_PAGES, CHUNK_PAGES),
            :,
            starts[pair] : starts[pair] + WINDOW,
        ]
        return held.reshape(chunk, WINDOW)

    halves = [
        sum(parts[index].astype(jnp.float32) for index in range(side, groups, 2))
        for side in range(2)
    ]
    halves = [
        half + bias[:, side * half.shape[1] : (side + 1) * half.shape[1]]
        for side, half in enumerate(halves)
    ]

    def kind(which):
        pieces = []
        for head in range(heads):
            half = halves[head // pairs]
            begin = (head % pairs) * 3 * HEAD + which * HEAD
            pieces.append(half[:, begin : begin + HEAD])
        return jnp.concatenate(pieces, axis=1)

    width = heads * HEAD

    def rows_of(ref):
        return jnp.concatenate([ref[slot[index]] for index in range(held_count)], axis=0)

    cosine, sine_up, sine_down = rows_of(cosine), rows_of(sine_up), rows_of(sine_down)

    def turn(block):
        half_rot = ROT // 2
        return (
            block * cosine
            + pltpu.roll(block, width - half_rot, 1) * sine_up
            + pltpu.roll(block, half_rot, 1) * sine_down
        )

    queries = turn(kind(0)).astype(jnp.bfloat16)
    turned = turn(kind(1)).astype(jnp.bfloat16)
    plain = kind(2).astype(jnp.bfloat16)

    def put(which, index, value):
        outs[which][slot[index] if before else index] = value

    for which, held in enumerate(before):
        for index in range(held_count):
            outs[which][slots[index]] = held[index]
    for index in range(held_count):
        rows = slice(index * fresh_len, (index + 1) * fresh_len)
        put(1, index, turned[rows])
        put(2, index, plain[rows])

    factor = 1.0 / math.sqrt(HEAD) / math.log(2.0)
    starts = [(2 * HEAD * pair) // LANES * LANES for pair in range(pairs)]
    lane = lax.broadcasted_iota(jnp.int32, (fresh_len, WINDOW), 1)

    def owned(pair, member):
        begin = (2 * pair + member) * HEAD - starts[pair]
        return (lane >= begin) & (lane < begin + HEAD)

    def contract(left, right):
        return lax.dot_general(
            left, right, (((1,), (1,)), ((), ())), preferred_element_type=jnp.float32
        )

    zero = jnp.zeros((fresh_len, WINDOW), jnp.bfloat16)
    spread_rows = heads * fresh_len
    row = lax.broadcasted_iota(jnp.int32, (2 * fresh_len, fresh_len), 0)
    causal_pair = lax.rem(row, fresh_len) >= lax.broadcasted_iota(
        jnp.int32, (2 * fresh_len, fresh_len), 1
    )
    for index in range(held_count):
        rows = slice(index * fresh_len, (index + 1) * fresh_len)
        spread = []
        for pair in range(pairs):
            window = queries[rows, starts[pair] : starts[pair] + WINDOW]
            spread.append(
                jnp.concatenate(
                    [jnp.where(owned(pair, member), window, zero) for member in range(2)], axis=0
                )
            )
        scores = jnp.concatenate(
            [
                jnp.where(
                    causal_pair,
                    contract(spread[pair], turned[rows, starts[pair] : starts[pair] + WINDOW]),
                    -1e30,
                )
                for pair in range(pairs)
            ],
            axis=0,
        )
        peak = jnp.max(scores, axis=1, keepdims=True)
        weight = jnp.exp2((scores - peak) * factor)
        denom = jnp.sum(weight, axis=1, keepdims=True)
        weight = weight.astype(jnp.bfloat16)
        mixed = jnp.concatenate(
            [
                jnp.dot(
                    weight[pair * 2 * fresh_len : (pair + 1) * 2 * fresh_len],
                    plain[rows, starts[pair] : starts[pair] + WINDOW],
                    preferred_element_type=jnp.float32,
                )
                for pair in range(pairs)
            ],
            axis=0,
        )

        def finish(entry, carry, index=index):
            for copy in copies(index, entry):
                copy.wait()
            return carry

        lax.fori_loop(0, counts[index] * CHUNK_PAGES, finish, 0)

        def step(part, carry, index=index, spread=spread):
            peak, denom, mixed = carry
            scores = jnp.concatenate(
                [
                    contract(spread[pair], cached(keys, index, part, pair))
                    for pair in range(pairs)
                ],
                axis=0,
            )
            position = part * chunk + lax.broadcasted_iota(jnp.int32, (spread_rows, chunk), 1)
            scores = jnp.where(position < lengths[index], scores, -1e30)
            higher = jnp.maximum(peak, jnp.max(scores, axis=1, keepdims=True))
            shrink = jnp.exp2((peak - higher) * factor)
            weight = jnp.exp2((scores - higher) * factor)
            denom = denom * shrink + jnp.sum(weight, axis=1, keepdims=True)
            weight = weight.astype(jnp.bfloat16)
            added = jnp.concatenate(
                [
                    jnp.dot(
                        weight[pair * 2 * fresh_len : (pair + 1) * 2 * fresh_len],
                        cached(values, index, part, pair),
                        preferred_element_type=jnp.float32,
                    )
                    for pair in range(pairs)
                ],
                axis=0,
            )
            return higher, denom, mixed * shrink + added

        peak, denom, mixed = lax.fori_loop(0, counts[index], step, (peak, denom, mixed))
        mixed = mixed / denom
        tiles = [None] * (width // LANES)
        for pair in range(pairs):
            for member in range(2):
                begin = (2 * pair + member) * fresh_len
                part = jnp.where(owned(pair, member), mixed[begin : begin + fresh_len], 0.0)
                for side in range(2):
                    place_at = starts[pair] // LANES + side
                    tile = part[:, side * LANES : (side + 1) * LANES]
                    tiles[place_at] = tile if tiles[place_at] is None else tiles[place_at] + tile
        put(0, index, jnp.concatenate(tiles, axis=1).astype(jnp.bfloat16))


def per_device(
    req_size,
    wgt_size,
    arrivals,
    group_of,
    lengths,
    page_table,
    ln_gain,
    ln_bias,
    w_qkv,
    qkv_bias,
    key_pool,
    value_pool,
):
    req_count, fresh_len, width = arrivals.shape
    rows = req_count * fresh_len
    depth, local_cols = w_qkv.shape
    half_cols = local_cols // 2
    heads = local_cols // (3 * HEAD)
    page = key_pool.shape[1]
    chips = req_size // 2
    block = 2 * depth
    everyone = group_of.shape[0]
    me = lax.axis_index("req")
    layer = lax.axis_index("wgt")
    core = me & 1
    chip = me >> 1

    def swap(value, distance):
        return lax.ppermute(
            value, "req", [(device, device ^ distance) for device in range(req_size)]
        )

    def after(value, others):
        return lax.optimization_barrier((value, others))[0]

    half = req_count // 2
    piece = jax.ShapeDtypeStruct((half, fresh_len, width), jnp.bfloat16)
    slots, sources, *chunks = pl.pallas_call(
        functools.partial(plan_kernel, req_count),
        out_shape=[
            jax.ShapeDtypeStruct((2 * half,), jnp.int32),
            jax.ShapeDtypeStruct((2 * req_size * half,), jnp.int32),
            piece,
            piece,
        ],
        in_specs=[SMEM, SMEM, HBM],
        out_specs=[SMEM, SMEM, VMEM, VMEM],
        scratch_shapes=[
            pltpu.SMEM((everyone,), jnp.int32),
            pltpu.SMEM((everyone,), jnp.int32),
            pltpu.SMEM((everyone,), jnp.int32),
            pltpu.SMEM((req_size,), jnp.int32),
            pltpu.SemaphoreType.DMA((2 * half,)),
        ],
        name="plan",
    )(jnp.stack([me]).astype(jnp.int32), group_of, arrivals)

    lane = np.arange(heads * HEAD) % HEAD
    half_rot = ROT // 2
    inverse = jnp.power(10000.0, -jnp.asarray(lane % half_rot, jnp.float32) * 2.0 / ROT)
    positions = (
        lengths[:, None] + jnp.arange(fresh_len, dtype=jnp.int32)[None, :]
    ).astype(jnp.float32)
    angles = positions.reshape(rows, 1) * inverse[None, :]
    turns = jnp.asarray(lane < ROT)[None, :]
    cosine = jnp.where(turns, jnp.cos(angles), 1.0)
    sine = jnp.sin(angles)
    sine_up = jnp.where(jnp.asarray(lane < half_rot)[None, :], -sine, 0.0)
    sine_down = jnp.where(turns & jnp.asarray(lane >= half_rot)[None, :], sine, 0.0)

    tables = [
        value.reshape(req_count, fresh_len, heads * HEAD)
        for value in (cosine, sine_up, sine_down)
    ]
    gain = ln_gain.astype(jnp.float32).reshape(chips, 1, block)
    shift = ln_bias.astype(jnp.float32).reshape(chips, 1, block)
    bias = qkv_bias.astype(jnp.float32).reshape(1, local_cols)
    place = jnp.stack([core]).astype(jnp.int32)
    where = jnp.stack([layer, chip]).astype(jnp.int32)
    chunk_rows = half * fresh_len
    span = page_table.shape[1]
    pages = span + (half - 1) * (span // 2)

    pieces = [[chunk.reshape(chunk_rows, width)] for chunk in chunks]
    ends = [(own[0], own[0]) for own in pieces]
    downs = [[], []]
    for part in range(2):
        for hop in range(1, wgt_size):
            up, down = ends[part]
            if part == 1 and hop == 1:
                up = down = after(up, (pieces[0][min(2, wgt_size - 1)], downs[0][min(1, wgt_size - 2)]))
            up = lax.ppermute(up, "wgt", [(at, at + 1) for at in range(hop - 1, wgt_size - 1)])
            down = lax.ppermute(down, "wgt", [(at + 1, at) for at in range(wgt_size - hop)])
            ends[part] = (up, down)
            pieces[part].append(up)
            downs[part].append(down)

    rows_held = after(w_qkv, pieces[0][1])
    own_rows = lax.dynamic_slice_in_dim(rows_held, core * half_cols, half_cols, 1)
    other_rows = swap(
        lax.dynamic_slice_in_dim(rows_held, (1 - core) * half_cols, half_cols, 1), 1
    )

    projected = []
    for part in range(2):
        if part == 1:
            pieces[1][-1] = after(pieces[1][-1], projected[0])
        normed = pl.pallas_call(
            functools.partial(norm_kernel, wgt_size, chips),
            out_shape=[jax.ShapeDtypeStruct((chunk_rows, block), jnp.bfloat16)] * chips,
            in_specs=[SMEM] + [HBM] * (2 * wgt_size - 1) + [VMEM] * 2,
            out_specs=[VMEM] * chips,
            scratch_shapes=[
                pltpu.VMEM((wgt_size, chunk_rows, width), jnp.bfloat16),
                pltpu.SemaphoreType.DMA((2 * wgt_size - 1,)),
            ],
            compiler_params=pltpu.CompilerParams(vmem_limit_bytes=12 * MIB),
            name="norm",
        )(where, *pieces[part], *downs[part], gain, shift)

        tokens = []
        for distance in range(chips):
            mine = normed[distance] if distance == 0 else swap(normed[distance], 2 * distance)
            if part == 0:
                mine = after(mine, (pieces[1][1], downs[1][0]))
            tokens += [mine, swap(mine, 1)]
        if part == 0:
            hop = min(2, wgt_size - 1)
            tokens[-1] = after(tokens[-1], (pieces[1][hop], downs[1][hop - 1]))

        partial = pl.pallas_call(
            functools.partial(project_kernel, fresh_len, half, part),
            out_shape=jax.ShapeDtypeStruct((req_size, chunk_rows, half_cols), jnp.bfloat16),
            in_specs=[SMEM] * 2 + [HBM] * (req_size + 2),
            out_specs=HBM,
            scratch_shapes=[
                pltpu.VMEM((req_size * half, fresh_len, block), jnp.bfloat16),
                pltpu.VMEM((block, half_cols), jnp.bfloat16),
                pltpu.VMEM((min(req_size, 4) * chunk_rows, block), jnp.bfloat16),
                pltpu.VMEM((req_size, chunk_rows, half_cols), jnp.bfloat16),
                pltpu.SemaphoreType.DMA((req_size,)),
                pltpu.SemaphoreType.DMA((2,)),
                pltpu.SemaphoreType.DMA((req_size // min(req_size, 4),)),
            ],
            compiler_params=pltpu.CompilerParams(vmem_limit_bytes=20 * MIB),
            name="project",
        )(
            place,
            sources,
            *[token.reshape(half, fresh_len, block) for token in tokens],
            own_rows,
            other_rows,
        )

        projected.append(partial)

    results = []
    for part in range(2):
        parts = lax.all_to_all(projected[part], "req", 0, 0, tiled=True)
        if part == 0:
            parts = after(parts, projected[1])

        operands = [
            slots, lengths, page_table, parts, bias, *tables, key_pool, value_pool
        ]
        specs = [SMEM] * 3 + [VMEM] * 5 + [HBM] * 2
        count = half if part == 0 else req_count
        out = jax.ShapeDtypeStruct((count, fresh_len, heads * HEAD), jnp.bfloat16)
        results = pl.pallas_call(
            functools.partial(
                attend_kernel, (req_size, half, fresh_len, page, heads, part)
            ),
            out_shape=[out] * 3,
            in_specs=specs + [VMEM] * len(results),
            out_specs=[VMEM] * 3,
            scratch_shapes=[
                pltpu.VMEM((pages, page, heads * HEAD), jnp.bfloat16),
                pltpu.VMEM((pages, page, heads * HEAD), jnp.bfloat16),
                pltpu.SemaphoreType.DMA((half,)),
            ],
            compiler_params=pltpu.CompilerParams(vmem_limit_bytes=24 * MIB),
            name="attend",
        )(*operands, *results)
    return results


def solution(mesh):
    in_specs = (
        P("req", None, "wgt"),
        P(),
        P("req"),
        P("req", None),
        P(),
        P(),
        P("req", "wgt"),
        P("wgt"),
        P("req", None, "wgt"),
        P("req", None, "wgt"),
    )
    out_specs = (P("req", None, "wgt"), P("req", None, "wgt"), P("req", None, "wgt"))
    return jax.shard_map(
        functools.partial(per_device, mesh.shape["req"], mesh.shape["wgt"]),
        mesh=mesh,
        in_specs=in_specs,
        out_specs=out_specs,
        check_vma=False,
    )
```

```python
import functools
import math

import jax
import jax.numpy as jnp
import numpy as np
from jax import lax
from jax.experimental import pallas as pl
from jax.experimental.pallas import tpu as pltpu
from jax.sharding import PartitionSpec as P

HEAD = 96
ROT = 24
EPS = 1e-05
LANES = 128
WINDOW = 2 * LANES
CHUNK_PAGES = 4
VMEM_LIMIT = 58 * 1024 * 1024

SMEM = pl.BlockSpec(memory_space=pltpu.SMEM)
VMEM = pl.BlockSpec(memory_space=pltpu.VMEM)
HBM = pl.BlockSpec(memory_space=pltpu.HBM)


def plan_kernel(req_count, place, group_of, arrivals, slots, sources, *refs):
    chunks = refs[:2]
    order, slot_of, color, filled, sems = refs[2:]
    everyone = group_of.shape[0]
    groups = everyone // req_count
    half = req_count // 2
    me = place[0]

    def clear(group, carry):
        filled[group] = 0
        return carry

    lax.fori_loop(0, groups, clear, 0)

    def rank(item, carry):
        group = group_of[item]
        slot = group * req_count + filled[group]
        filled[group] = filled[group] + 1
        slot_of[item] = slot
        order[slot] = item
        color[item] = -1
        return carry

    lax.fori_loop(0, everyone, rank, 0)

    shift = req_count.bit_length() - 1

    def note(item, shade):
        color[item] = shade
        slot = slot_of[item]
        to = (shade * groups + (slot >> shift)) * half + ((slot & (req_count - 1)) >> 1)
        sources[to] = ((item >> shift) ^ me) * half + ((item & (req_count - 1)) >> 1)
        return slot

    def walk(pair, carry):
        def body(state):
            note(state[0], 0)
            following = order[note(state[0] ^ 1, 1) ^ 1]
            return following, color[following]

        lax.while_loop(lambda state: state[1] < 0, body, (2 * pair, color[2 * pair]))
        return carry

    lax.fori_loop(0, everyone // 2, walk, 0)

    copies = []
    for pair in range(half):
        first = color[me * req_count + 2 * pair]
        for part in range(2):
            copies.append(
                pltpu.make_async_copy(
                    arrivals.at[2 * pair + (first ^ part)],
                    chunks[part].at[pair],
                    sems.at[part * half + pair],
                )
            )
    for copy in copies:
        copy.start()
    for pair in range(half):
        first = color[order[me * req_count + 2 * pair]]
        for part in range(2):
            slots[part * half + pair] = 2 * pair + (first ^ part)
    for copy in copies:
        copy.wait()


def norm_kernel(depth, chips, place, *refs):
    pieces = refs[:depth]
    gain, bias = refs[depth : depth + 2]
    outs = refs[depth + 2 : depth + 2 + chips]
    held, sems = refs[depth + 2 + chips :]
    me, chip = place[0], place[1]
    copies = [
        pltpu.make_async_copy(piece, held.at[me ^ distance], sems.at[distance])
        for distance, piece in enumerate(pieces)
    ]
    for copy in copies:
        copy.start()
    for copy in copies:
        copy.wait()

    rows, width = held.shape[1], held.shape[2]
    step = 16
    total_width = depth * width
    block = total_width // chips
    per = chips // depth

    def body(index, carry):
        at = pl.ds(pl.multiple_of(index * step, step), step)
        values = [held[part, at, :].astype(jnp.float32) for part in range(depth)]
        total = sum(jnp.sum(value, axis=-1, keepdims=True) for value in values)
        center = total / total_width
        square = sum(
            jnp.sum(jnp.square(value - center), axis=-1, keepdims=True) for value in values
        )
        scale = lax.rsqrt(square / total_width + EPS)
        for offset in range(chips):
            target = chip ^ offset
            part = target // per
            lane = pl.ds(pl.multiple_of((target % per) * block, LANES), block)
            value = held[part, at, lane].astype(jnp.float32)
            value = (value - center) * scale * gain[target] + bias[target]
            outs[offset][at, :] = value.astype(jnp.bfloat16)
        return carry

    lax.fori_loop(0, rows // step, body, 0, unroll=2)


def project_kernel(fresh_len, held_count, part, place, source, *refs):
    groups = len(refs) - 10
    tokens = refs[:groups]
    own_rows, other_rows = refs[groups : groups + 2]
    out, held, weights, picked, ready, sems, weight_sems, out_sems = refs[groups + 2 :]
    core = place[0]
    depth = own_rows.shape[0]
    copies = [
        pltpu.make_async_copy(
            own_rows,
            weights.at[pl.ds(pl.multiple_of(core * depth, 16), depth)],
            weight_sems.at[0],
        ),
        pltpu.make_async_copy(
            other_rows,
            weights.at[pl.ds(pl.multiple_of((1 - core) * depth, 16), depth)],
            weight_sems.at[1],
        ),
    ]
    copies += [
        pltpu.make_async_copy(
            token, held.at[pl.ds(index * held_count, held_count)], sems.at[index]
        )
        for index, token in enumerate(tokens)
    ]
    for copy in copies:
        copy.start()
    for copy in copies:
        copy.wait()
    rows = held_count * fresh_len
    together = min(groups, 4)
    for first in range(0, groups, together):
        for item in range(together * held_count):
            picked[item * fresh_len : (item + 1) * fresh_len, :] = held[
                source[(part * groups + first) * held_count + item]
            ]
        result = jnp.dot(picked[...], weights[...], preferred_element_type=jnp.float32).astype(
            jnp.bfloat16
        )
        for index in range(together):
            ready[first + index] = result[index * rows : (index + 1) * rows]
        targets = pl.ds(first, together)
        copies.append(
            pltpu.make_async_copy(
                ready.at[targets], out.at[targets], out_sems.at[first // together]
            )
        )
        copies[-1].start()
    for copy in copies[groups + 2 :]:
        copy.wait()


def attend_kernel(shape, slots, all_lengths, table, *refs):
    groups, held_count, fresh_len, page, heads, part = shape
    parts, bias, cosine, sine_up, sine_down, key_pool, value_pool = refs[:7]
    before = refs[7:-6]
    outs = refs[-6:-3]
    keys, values, sems = refs[-3:]
    chunk = CHUNK_PAGES * page
    pairs = heads // 2

    slot = [slots[part * held_count + index] for index in range(held_count)]
    lengths = [all_lengths[slot[index]] for index in range(held_count)]
    counts = [pl.cdiv(lengths[index], chunk) for index in range(held_count)]
    bases = [jnp.int32(0)]
    for count in counts[:-1]:
        bases.append(bases[-1] + count * CHUNK_PAGES)

    def copies(index, entry):
        number = table[slot[index], entry]
        to = bases[index] + entry
        return (
            pltpu.make_async_copy(key_pool.at[number], keys.at[to], sems.at[index]),
            pltpu.make_async_copy(value_pool.at[number], values.at[to], sems.at[index]),
        )

    for index in range(held_count):

        def start(entry, carry, index=index):
            for copy in copies(index, entry):
                copy.start()
            return carry

        lax.fori_loop(0, counts[index] * CHUNK_PAGES, start, 0)

    def cached(pages, index, part, pair):
        held = pages[
            pl.ds(bases[index] + part * CHUNK_PAGES, CHUNK_PAGES),
            :,
            starts[pair] : starts[pair] + WINDOW,
        ]
        return held.reshape(chunk, WINDOW)

    halves = [
        sum(parts[index].astype(jnp.float32) for index in range(side, groups, 2))
        for side in range(2)
    ]
    halves = [
        half + bias[:, side * half.shape[1] : (side + 1) * half.shape[1]]
        for side, half in enumerate(halves)
    ]

    def kind(which):
        pieces = []
        for head in range(heads):
            half = halves[head // pairs]
            begin = (head % pairs) * 3 * HEAD + which * HEAD
            pieces.append(half[:, begin : begin + HEAD])
        return jnp.concatenate(pieces, axis=1)

    width = heads * HEAD

    def rows_of(ref):
        return jnp.concatenate([ref[slot[index]] for index in range(held_count)], axis=0)

    cosine, sine_up, sine_down = rows_of(cosine), rows_of(sine_up), rows_of(sine_down)

    def turn(block):
        half_rot = ROT // 2
        return (
            block * cosine
            + pltpu.roll(block, width - half_rot, 1) * sine_up
            + pltpu.roll(block, half_rot, 1) * sine_down
        )

    queries = turn(kind(0)).astype(jnp.bfloat16)
    turned = turn(kind(1)).astype(jnp.bfloat16)
    plain = kind(2).astype(jnp.bfloat16)

    def put(which, index, value):
        outs[which][slot[index] if before else index] = value

    for which, held in enumerate(before):
        for index in range(held_count):
            outs[which][slots[index]] = held[index]
    for index in range(held_count):
        rows = slice(index * fresh_len, (index + 1) * fresh_len)
        put(1, index, turned[rows])
        put(2, index, plain[rows])

    factor = 1.0 / math.sqrt(HEAD) / math.log(2.0)
    starts = [(2 * HEAD * pair) // LANES * LANES for pair in range(pairs)]
    lane = lax.broadcasted_iota(jnp.int32, (fresh_len, WINDOW), 1)

    def owned(pair, member):
        begin = (2 * pair + member) * HEAD - starts[pair]
        return (lane >= begin) & (lane < begin + HEAD)

    def contract(left, right):
        return lax.dot_general(
            left, right, (((1,), (1,)), ((), ())), preferred_element_type=jnp.float32
        )

    zero = jnp.zeros((fresh_len, WINDOW), jnp.bfloat16)
    spread_rows = heads * fresh_len
    row = lax.broadcasted_iota(jnp.int32, (2 * fresh_len, fresh_len), 0)
    causal_pair = lax.rem(row, fresh_len) >= lax.broadcasted_iota(
        jnp.int32, (2 * fresh_len, fresh_len), 1
    )
    for index in range(held_count):
        rows = slice(index * fresh_len, (index + 1) * fresh_len)
        spread = []
        for pair in range(pairs):
            window = queries[rows, starts[pair] : starts[pair] + WINDOW]
            spread.append(
                jnp.concatenate(
                    [jnp.where(owned(pair, member), window, zero) for member in range(2)], axis=0
                )
            )
        scores = jnp.concatenate(
            [
                jnp.where(
                    causal_pair,
                    contract(spread[pair], turned[rows, starts[pair] : starts[pair] + WINDOW]),
                    -1e30,
                )
                for pair in range(pairs)
            ],
            axis=0,
        )
        peak = jnp.max(scores, axis=1, keepdims=True)
        weight = jnp.exp2((scores - peak) * factor)
        denom = jnp.sum(weight, axis=1, keepdims=True)
        weight = weight.astype(jnp.bfloat16)
        mixed = jnp.concatenate(
            [
                jnp.dot(
                    weight[pair * 2 * fresh_len : (pair + 1) * 2 * fresh_len],
                    plain[rows, starts[pair] : starts[pair] + WINDOW],
                    preferred_element_type=jnp.float32,
                )
                for pair in range(pairs)
            ],
            axis=0,
        )

        def finish(entry, carry, index=index):
            for copy in copies(index, entry):
                copy.wait()
            return carry

        lax.fori_loop(0, counts[index] * CHUNK_PAGES, finish, 0)

        def step(part, carry, index=index, spread=spread):
            peak, denom, mixed = carry
            scores = jnp.concatenate(
                [
                    contract(spread[pair], cached(keys, index, part, pair))
                    for pair in range(pairs)
                ],
                axis=0,
            )
            position = part * chunk + lax.broadcasted_iota(jnp.int32, (spread_rows, chunk), 1)
            scores = jnp.where(position < lengths[index], scores, -1e30)
            higher = jnp.maximum(peak, jnp.max(scores, axis=1, keepdims=True))
            shrink = jnp.exp2((peak - higher) * factor)
            weight = jnp.exp2((scores - higher) * factor)
            denom = denom * shrink + jnp.sum(weight, axis=1, keepdims=True)
            weight = weight.astype(jnp.bfloat16)
            added = jnp.concatenate(
                [
                    jnp.dot(
                        weight[pair * 2 * fresh_len : (pair + 1) * 2 * fresh_len],
                        cached(values, index, part, pair),
                        preferred_element_type=jnp.float32,
                    )
                    for pair in range(pairs)
                ],
                axis=0,
            )
            return higher, denom, mixed * shrink + added

        peak, denom, mixed = lax.fori_loop(0, counts[index], step, (peak, denom, mixed))
        mixed = mixed / denom
        tiles = [None] * (width // LANES)
        for pair in range(pairs):
            for member in range(2):
                begin = (2 * pair + member) * fresh_len
                part = jnp.where(owned(pair, member), mixed[begin : begin + fresh_len], 0.0)
                for side in range(2):
                    place_at = starts[pair] // LANES + side
                    tile = part[:, side * LANES : (side + 1) * LANES]
                    tiles[place_at] = tile if tiles[place_at] is None else tiles[place_at] + tile
        put(0, index, jnp.concatenate(tiles, axis=1).astype(jnp.bfloat16))


def per_device(
    req_size,
    wgt_size,
    arrivals,
    group_of,
    lengths,
    page_table,
    ln_gain,
    ln_bias,
    w_qkv,
    qkv_bias,
    key_pool,
    value_pool,
):
    req_count, fresh_len, width = arrivals.shape
    rows = req_count * fresh_len
    depth, local_cols = w_qkv.shape
    half_cols = local_cols // 2
    heads = local_cols // (3 * HEAD)
    page = key_pool.shape[1]
    chips = req_size // 2
    block = 2 * depth
    everyone = group_of.shape[0]
    me = lax.axis_index("req")
    layer = lax.axis_index("wgt")
    core = me & 1
    chip = me >> 1

    def swap(value, distance):
        return lax.ppermute(
            value, "req", [(device, device ^ distance) for device in range(req_size)]
        )

    def after(value, others):
        return lax.optimization_barrier((value, others))[0]

    half = req_count // 2
    piece = jax.ShapeDtypeStruct((half, fresh_len, width), jnp.bfloat16)
    slots, sources, *chunks = pl.pallas_call(
        functools.partial(plan_kernel, req_count),
        out_shape=[
            jax.ShapeDtypeStruct((2 * half,), jnp.int32),
            jax.ShapeDtypeStruct((2 * req_size * half,), jnp.int32),
            piece,
            piece,
        ],
        in_specs=[SMEM, SMEM, HBM],
        out_specs=[SMEM, SMEM, VMEM, VMEM],
        scratch_shapes=[
            pltpu.SMEM((everyone,), jnp.int32),
            pltpu.SMEM((everyone,), jnp.int32),
            pltpu.SMEM((everyone,), jnp.int32),
            pltpu.SMEM((req_size,), jnp.int32),
            pltpu.SemaphoreType.DMA((2 * half,)),
        ],
        name="plan",
    )(jnp.stack([me]).astype(jnp.int32), group_of, arrivals)

    lane = np.arange(heads * HEAD) % HEAD
    half_rot = ROT // 2
    inverse = jnp.power(10000.0, -jnp.asarray(lane % half_rot, jnp.float32) * 2.0 / ROT)
    positions = (
        lengths[:, None] + jnp.arange(fresh_len, dtype=jnp.int32)[None, :]
    ).astype(jnp.float32)
    angles = positions.reshape(rows, 1) * inverse[None, :]
    turns = jnp.asarray(lane < ROT)[None, :]
    cosine = jnp.where(turns, jnp.cos(angles), 1.0)
    sine = jnp.sin(angles)
    sine_up = jnp.where(jnp.asarray(lane < half_rot)[None, :], -sine, 0.0)
    sine_down = jnp.where(turns & jnp.asarray(lane >= half_rot)[None, :], sine, 0.0)

    tables = [
        value.reshape(req_count, fresh_len, heads * HEAD)
        for value in (cosine, sine_up, sine_down)
    ]
    gain = ln_gain.astype(jnp.float32).reshape(chips, 1, block)
    shift = ln_bias.astype(jnp.float32).reshape(chips, 1, block)
    bias = qkv_bias.astype(jnp.float32).reshape(1, local_cols)
    place = jnp.stack([core]).astype(jnp.int32)
    where = jnp.stack([layer, chip]).astype(jnp.int32)
    chunk_rows = half * fresh_len
    span = page_table.shape[1]
    pages = span + (half - 1) * (span // 2)

    pieces = []
    for chunk in chunks:
        own = chunk.reshape(chunk_rows, width)
        if pieces:
            own = after(own, pieces[0][1])
        pieces.append([own])
        for distance in range(1, wgt_size):
            pairs = [(at, at ^ distance) for at in range(wgt_size)]
            pieces[-1].append(lax.ppermute(own, "wgt", pairs))

    rows_held = after(w_qkv, chunks[0])
    own_rows = lax.dynamic_slice_in_dim(rows_held, core * half_cols, half_cols, 1)
    other_rows = swap(
        lax.dynamic_slice_in_dim(rows_held, (1 - core) * half_cols, half_cols, 1), 1
    )

    projected = []
    for part in range(2):
        if part == 1:
            pieces[1][-1] = after(pieces[1][-1], projected[0])
        normed = pl.pallas_call(
            functools.partial(norm_kernel, wgt_size, chips),
            out_shape=[jax.ShapeDtypeStruct((chunk_rows, block), jnp.bfloat16)] * chips,
            in_specs=[SMEM] + [HBM] * wgt_size + [VMEM] * 2,
            out_specs=[VMEM] * chips,
            scratch_shapes=[
                pltpu.VMEM((wgt_size, chunk_rows, width), jnp.bfloat16),
                pltpu.SemaphoreType.DMA((wgt_size,)),
            ],
            compiler_params=pltpu.CompilerParams(vmem_limit_bytes=VMEM_LIMIT),
            name="norm",
        )(where, *pieces[part], gain, shift)

        tokens = []
        for distance in range(chips):
            mine = normed[distance] if distance == 0 else swap(normed[distance], 2 * distance)
            if part == 0:
                mine = after(mine, pieces[1][1])
            tokens += [mine, swap(mine, 1)]
        if part == 0:
            tokens[-1] = after(tokens[-1], pieces[1][wgt_size // 2])

        partial = pl.pallas_call(
            functools.partial(project_kernel, fresh_len, half, part),
            out_shape=jax.ShapeDtypeStruct((req_size, chunk_rows, half_cols), jnp.bfloat16),
            in_specs=[SMEM] * 2 + [HBM] * (req_size + 2),
            out_specs=HBM,
            scratch_shapes=[
                pltpu.VMEM((req_size * half, fresh_len, block), jnp.bfloat16),
                pltpu.VMEM((block, half_cols), jnp.bfloat16),
                pltpu.VMEM((min(req_size, 4) * chunk_rows, block), jnp.bfloat16),
                pltpu.VMEM((req_size, chunk_rows, half_cols), jnp.bfloat16),
                pltpu.SemaphoreType.DMA((req_size,)),
                pltpu.SemaphoreType.DMA((2,)),
                pltpu.SemaphoreType.DMA((req_size // min(req_size, 4),)),
            ],
            compiler_params=pltpu.CompilerParams(vmem_limit_bytes=VMEM_LIMIT),
            name="project",
        )(
            place,
            sources,
            *[token.reshape(half, fresh_len, block) for token in tokens],
            own_rows,
            other_rows,
        )

        projected.append(partial)

    results = []
    for part in range(2):
        parts = lax.all_to_all(projected[part], "req", 0, 0, tiled=True)
        if part == 0:
            parts = after(parts, projected[1])

        operands = [
            slots, lengths, page_table, parts, bias, *tables, key_pool, value_pool
        ]
        specs = [SMEM] * 3 + [VMEM] * 5 + [HBM] * 2
        count = half if part == 0 else req_count
        out = jax.ShapeDtypeStruct((count, fresh_len, heads * HEAD), jnp.bfloat16)
        results = pl.pallas_call(
            functools.partial(
                attend_kernel, (req_size, half, fresh_len, page, heads, part)
            ),
            out_shape=[out] * 3,
            in_specs=specs + [VMEM] * len(results),
            out_specs=[VMEM] * 3,
            scratch_shapes=[
                pltpu.VMEM((pages, page, heads * HEAD), jnp.bfloat16),
                pltpu.VMEM((pages, page, heads * HEAD), jnp.bfloat16),
                pltpu.SemaphoreType.DMA((half,)),
            ],
            compiler_params=pltpu.CompilerParams(vmem_limit_bytes=VMEM_LIMIT),
            name="attend",
        )(*operands, *results)
    return results


def solution(mesh):
    in_specs = (
        P("req", None, "wgt"),
        P(),
        P("req"),
        P("req", None),
        P(),
        P(),
        P("req", "wgt"),
        P("wgt"),
        P("req", None, "wgt"),
        P("req", None, "wgt"),
    )
    out_specs = (P("req", None, "wgt"), P("req", None, "wgt"), P("req", None, "wgt"))
    return jax.shard_map(
        functools.partial(per_device, mesh.shape["req"], mesh.shape["wgt"]),
        mesh=mesh,
        in_specs=in_specs,
        out_specs=out_specs,
        check_vma=False,
    )
```

```python
import functools
import math

import jax
import jax.numpy as jnp
import numpy as np
from jax import lax
from jax.experimental import pallas as pl
from jax.experimental.pallas import tpu as pltpu
from jax.sharding import PartitionSpec as P

HEAD = 96
ROT = 24
EPS = 1e-05
LANES = 128
WINDOW = 2 * LANES
CHUNK_PAGES = 4
VMEM_LIMIT = 58 * 1024 * 1024

SMEM = pl.BlockSpec(memory_space=pltpu.SMEM)
VMEM = pl.BlockSpec(memory_space=pltpu.VMEM)
HBM = pl.BlockSpec(memory_space=pltpu.HBM)


def plan_kernel(req_count, place, group_of, arrivals, slots, sources, *refs):
    chunks = refs[:2]
    order, slot_of, color, filled, sems = refs[2:]
    everyone = group_of.shape[0]
    groups = everyone // req_count
    half = req_count // 2
    me = place[0]

    def clear(group, carry):
        filled[group] = 0
        return carry

    lax.fori_loop(0, groups, clear, 0)

    def rank(item, carry):
        group = group_of[item]
        slot = group * req_count + filled[group]
        filled[group] = filled[group] + 1
        slot_of[item] = slot
        order[slot] = item
        color[item] = -1
        return carry

    lax.fori_loop(0, everyone, rank, 0)

    shift = req_count.bit_length() - 1

    def note(item, shade):
        color[item] = shade
        slot = slot_of[item]
        to = (shade * groups + (slot >> shift)) * half + ((slot & (req_count - 1)) >> 1)
        sources[to] = ((item >> shift) ^ me) * half + ((item & (req_count - 1)) >> 1)
        return slot

    def walk(pair, carry):
        def body(state):
            note(state[0], 0)
            following = order[note(state[0] ^ 1, 1) ^ 1]
            return following, color[following]

        lax.while_loop(lambda state: state[1] < 0, body, (2 * pair, color[2 * pair]))
        return carry

    lax.fori_loop(0, everyone // 2, walk, 0)

    copies = []
    for pair in range(half):
        first = color[me * req_count + 2 * pair]
        for part in range(2):
            copies.append(
                pltpu.make_async_copy(
                    arrivals.at[2 * pair + (first ^ part)],
                    chunks[part].at[pair],
                    sems.at[part * half + pair],
                )
            )
    for copy in copies:
        copy.start()
    for pair in range(half):
        first = color[order[me * req_count + 2 * pair]]
        for part in range(2):
            slots[part * half + pair] = 2 * pair + (first ^ part)
    for copy in copies:
        copy.wait()


def norm_kernel(depth, chips, place, *refs):
    gathered, gain, bias = refs[:3]
    outs = refs[3 : 3 + chips]
    held, sem = refs[3 + chips :]
    chip = place[0]
    copy = pltpu.make_async_copy(gathered, held, sem)
    copy.start()
    copy.wait()

    rows, width = held.shape[1], held.shape[2]
    step = 16
    total_width = depth * width
    block = total_width // chips
    per = chips // depth

    def body(index, carry):
        at = pl.ds(pl.multiple_of(index * step, step), step)
        values = [held[part, at, :].astype(jnp.float32) for part in range(depth)]
        total = sum(jnp.sum(value, axis=-1, keepdims=True) for value in values)
        center = total / total_width
        square = sum(
            jnp.sum(jnp.square(value - center), axis=-1, keepdims=True) for value in values
        )
        scale = lax.rsqrt(square / total_width + EPS)
        for offset in range(chips):
            target = chip ^ offset
            part = target // per
            lane = pl.ds(pl.multiple_of((target % per) * block, LANES), block)
            value = held[part, at, lane].astype(jnp.float32)
            value = (value - center) * scale * gain[target] + bias[target]
            outs[offset][at, :] = value.astype(jnp.bfloat16)
        return carry

    lax.fori_loop(0, rows // step, body, 0, unroll=2)


def project_kernel(fresh_len, held_count, part, place, source, *refs):
    groups = len(refs) - 10
    tokens = refs[:groups]
    own_rows, other_rows = refs[groups : groups + 2]
    out, held, weights, picked, ready, sems, weight_sems, out_sems = refs[groups + 2 :]
    core = place[0]
    depth = own_rows.shape[0]
    copies = [
        pltpu.make_async_copy(
            own_rows,
            weights.at[pl.ds(pl.multiple_of(core * depth, 16), depth)],
            weight_sems.at[0],
        ),
        pltpu.make_async_copy(
            other_rows,
            weights.at[pl.ds(pl.multiple_of((1 - core) * depth, 16), depth)],
            weight_sems.at[1],
        ),
    ]
    copies += [
        pltpu.make_async_copy(
            token, held.at[pl.ds(index * held_count, held_count)], sems.at[index]
        )
        for index, token in enumerate(tokens)
    ]
    for copy in copies:
        copy.start()
    for copy in copies:
        copy.wait()
    rows = held_count * fresh_len
    together = min(groups, 4)
    for first in range(0, groups, together):
        for item in range(together * held_count):
            picked[item * fresh_len : (item + 1) * fresh_len, :] = held[
                source[(part * groups + first) * held_count + item]
            ]
        result = jnp.dot(picked[...], weights[...], preferred_element_type=jnp.float32).astype(
            jnp.bfloat16
        )
        for index in range(together):
            ready[first + index] = result[index * rows : (index + 1) * rows]
        targets = pl.ds(first, together)
        copies.append(
            pltpu.make_async_copy(
                ready.at[targets], out.at[targets], out_sems.at[first // together]
            )
        )
        copies[-1].start()
    for copy in copies[groups + 2 :]:
        copy.wait()


def attend_kernel(shape, slots, all_lengths, table, *refs):
    groups, held_count, fresh_len, page, heads, part = shape
    parts, bias, cosine, sine_up, sine_down, key_pool, value_pool = refs[:7]
    before = refs[7:-6]
    outs = refs[-6:-3]
    keys, values, sems = refs[-3:]
    chunk = CHUNK_PAGES * page
    pairs = heads // 2

    slot = [slots[part * held_count + index] for index in range(held_count)]
    lengths = [all_lengths[slot[index]] for index in range(held_count)]
    counts = [pl.cdiv(lengths[index], chunk) for index in range(held_count)]
    bases = [jnp.int32(0)]
    for count in counts[:-1]:
        bases.append(bases[-1] + count * CHUNK_PAGES)

    def copies(index, entry):
        number = table[slot[index], entry]
        to = bases[index] + entry
        return (
            pltpu.make_async_copy(key_pool.at[number], keys.at[to], sems.at[index]),
            pltpu.make_async_copy(value_pool.at[number], values.at[to], sems.at[index]),
        )

    for index in range(held_count):

        def start(entry, carry, index=index):
            for copy in copies(index, entry):
                copy.start()
            return carry

        lax.fori_loop(0, counts[index] * CHUNK_PAGES, start, 0)

    def cached(pages, index, part, pair):
        held = pages[
            pl.ds(bases[index] + part * CHUNK_PAGES, CHUNK_PAGES),
            :,
            starts[pair] : starts[pair] + WINDOW,
        ]
        return held.reshape(chunk, WINDOW)

    halves = [
        sum(parts[index].astype(jnp.float32) for index in range(side, groups, 2))
        for side in range(2)
    ]
    halves = [
        half + bias[:, side * half.shape[1] : (side + 1) * half.shape[1]]
        for side, half in enumerate(halves)
    ]

    def kind(which):
        pieces = []
        for head in range(heads):
            half = halves[head // pairs]
            begin = (head % pairs) * 3 * HEAD + which * HEAD
            pieces.append(half[:, begin : begin + HEAD])
        return jnp.concatenate(pieces, axis=1)

    width = heads * HEAD

    def rows_of(ref):
        return jnp.concatenate([ref[slot[index]] for index in range(held_count)], axis=0)

    cosine, sine_up, sine_down = rows_of(cosine), rows_of(sine_up), rows_of(sine_down)

    def turn(block):
        half_rot = ROT // 2
        return (
            block * cosine
            + pltpu.roll(block, width - half_rot, 1) * sine_up
            + pltpu.roll(block, half_rot, 1) * sine_down
        )

    queries = turn(kind(0)).astype(jnp.bfloat16)
    turned = turn(kind(1)).astype(jnp.bfloat16)
    plain = kind(2).astype(jnp.bfloat16)

    def put(which, index, value):
        outs[which][slot[index] if before else index] = value

    for which, held in enumerate(before):
        for index in range(held_count):
            outs[which][slots[index]] = held[index]
    for index in range(held_count):
        rows = slice(index * fresh_len, (index + 1) * fresh_len)
        put(1, index, turned[rows])
        put(2, index, plain[rows])

    factor = 1.0 / math.sqrt(HEAD) / math.log(2.0)
    starts = [(2 * HEAD * pair) // LANES * LANES for pair in range(pairs)]
    lane = lax.broadcasted_iota(jnp.int32, (fresh_len, WINDOW), 1)

    def owned(pair, member):
        begin = (2 * pair + member) * HEAD - starts[pair]
        return (lane >= begin) & (lane < begin + HEAD)

    def contract(left, right):
        return lax.dot_general(
            left, right, (((1,), (1,)), ((), ())), preferred_element_type=jnp.float32
        )

    zero = jnp.zeros((fresh_len, WINDOW), jnp.bfloat16)
    spread_rows = heads * fresh_len
    row = lax.broadcasted_iota(jnp.int32, (2 * fresh_len, fresh_len), 0)
    causal_pair = lax.rem(row, fresh_len) >= lax.broadcasted_iota(
        jnp.int32, (2 * fresh_len, fresh_len), 1
    )
    for index in range(held_count):
        rows = slice(index * fresh_len, (index + 1) * fresh_len)
        spread = []
        for pair in range(pairs):
            window = queries[rows, starts[pair] : starts[pair] + WINDOW]
            spread.append(
                jnp.concatenate(
                    [jnp.where(owned(pair, member), window, zero) for member in range(2)], axis=0
                )
            )
        scores = jnp.concatenate(
            [
                jnp.where(
                    causal_pair,
                    contract(spread[pair], turned[rows, starts[pair] : starts[pair] + WINDOW]),
                    -1e30,
                )
                for pair in range(pairs)
            ],
            axis=0,
        )
        peak = jnp.max(scores, axis=1, keepdims=True)
        weight = jnp.exp2((scores - peak) * factor)
        denom = jnp.sum(weight, axis=1, keepdims=True)
        weight = weight.astype(jnp.bfloat16)
        mixed = jnp.concatenate(
            [
                jnp.dot(
                    weight[pair * 2 * fresh_len : (pair + 1) * 2 * fresh_len],
                    plain[rows, starts[pair] : starts[pair] + WINDOW],
                    preferred_element_type=jnp.float32,
                )
                for pair in range(pairs)
            ],
            axis=0,
        )

        def finish(entry, carry, index=index):
            for copy in copies(index, entry):
                copy.wait()
            return carry

        lax.fori_loop(0, counts[index] * CHUNK_PAGES, finish, 0)

        def step(part, carry, index=index, spread=spread):
            peak, denom, mixed = carry
            scores = jnp.concatenate(
                [
                    contract(spread[pair], cached(keys, index, part, pair))
                    for pair in range(pairs)
                ],
                axis=0,
            )
            position = part * chunk + lax.broadcasted_iota(jnp.int32, (spread_rows, chunk), 1)
            scores = jnp.where(position < lengths[index], scores, -1e30)
            higher = jnp.maximum(peak, jnp.max(scores, axis=1, keepdims=True))
            shrink = jnp.exp2((peak - higher) * factor)
            weight = jnp.exp2((scores - higher) * factor)
            denom = denom * shrink + jnp.sum(weight, axis=1, keepdims=True)
            weight = weight.astype(jnp.bfloat16)
            added = jnp.concatenate(
                [
                    jnp.dot(
                        weight[pair * 2 * fresh_len : (pair + 1) * 2 * fresh_len],
                        cached(values, index, part, pair),
                        preferred_element_type=jnp.float32,
                    )
                    for pair in range(pairs)
                ],
                axis=0,
            )
            return higher, denom, mixed * shrink + added

        peak, denom, mixed = lax.fori_loop(0, counts[index], step, (peak, denom, mixed))
        mixed = mixed / denom
        tiles = [None] * (width // LANES)
        for pair in range(pairs):
            for member in range(2):
                begin = (2 * pair + member) * fresh_len
                part = jnp.where(owned(pair, member), mixed[begin : begin + fresh_len], 0.0)
                for side in range(2):
                    place_at = starts[pair] // LANES + side
                    tile = part[:, side * LANES : (side + 1) * LANES]
                    tiles[place_at] = tile if tiles[place_at] is None else tiles[place_at] + tile
        put(0, index, jnp.concatenate(tiles, axis=1).astype(jnp.bfloat16))


def per_device(
    req_size,
    wgt_size,
    arrivals,
    group_of,
    lengths,
    page_table,
    ln_gain,
    ln_bias,
    w_qkv,
    qkv_bias,
    key_pool,
    value_pool,
):
    req_count, fresh_len, width = arrivals.shape
    rows = req_count * fresh_len
    depth, local_cols = w_qkv.shape
    half_cols = local_cols // 2
    heads = local_cols // (3 * HEAD)
    page = key_pool.shape[1]
    chips = req_size // 2
    block = 2 * depth
    everyone = group_of.shape[0]
    me = lax.axis_index("req")
    core = me & 1
    chip = me >> 1

    def swap(value, distance):
        return lax.ppermute(
            value, "req", [(device, device ^ distance) for device in range(req_size)]
        )

    def after(value, others):
        return lax.optimization_barrier((value, others))[0]

    half = req_count // 2
    piece = jax.ShapeDtypeStruct((half, fresh_len, width), jnp.bfloat16)
    slots, sources, *chunks = pl.pallas_call(
        functools.partial(plan_kernel, req_count),
        out_shape=[
            jax.ShapeDtypeStruct((2 * half,), jnp.int32),
            jax.ShapeDtypeStruct((2 * req_size * half,), jnp.int32),
            piece,
            piece,
        ],
        in_specs=[SMEM, SMEM, HBM],
        out_specs=[SMEM, SMEM, VMEM, VMEM],
        scratch_shapes=[
            pltpu.SMEM((everyone,), jnp.int32),
            pltpu.SMEM((everyone,), jnp.int32),
            pltpu.SMEM((everyone,), jnp.int32),
            pltpu.SMEM((req_size,), jnp.int32),
            pltpu.SemaphoreType.DMA((2 * half,)),
        ],
        name="plan",
    )(jnp.stack([me]).astype(jnp.int32), group_of, arrivals)

    lane = np.arange(heads * HEAD) % HEAD
    half_rot = ROT // 2
    inverse = jnp.power(10000.0, -jnp.asarray(lane % half_rot, jnp.float32) * 2.0 / ROT)
    positions = (
        lengths[:, None] + jnp.arange(fresh_len, dtype=jnp.int32)[None, :]
    ).astype(jnp.float32)
    angles = positions.reshape(rows, 1) * inverse[None, :]
    turns = jnp.asarray(lane < ROT)[None, :]
    cosine = jnp.where(turns, jnp.cos(angles), 1.0)
    sine = jnp.sin(angles)
    sine_up = jnp.where(jnp.asarray(lane < half_rot)[None, :], -sine, 0.0)
    sine_down = jnp.where(turns & jnp.asarray(lane >= half_rot)[None, :], sine, 0.0)

    tables = [
        value.reshape(req_count, fresh_len, heads * HEAD)
        for value in (cosine, sine_up, sine_down)
    ]
    gain = ln_gain.astype(jnp.float32).reshape(chips, 1, block)
    shift = ln_bias.astype(jnp.float32).reshape(chips, 1, block)
    bias = qkv_bias.astype(jnp.float32).reshape(1, local_cols)
    place = jnp.stack([core]).astype(jnp.int32)
    where = jnp.stack([chip]).astype(jnp.int32)
    chunk_rows = half * fresh_len
    span = page_table.shape[1]
    pages = span + (half - 1) * (span // 2)

    gathered = [
        lax.all_gather(chunk.reshape(chunk_rows, width), "wgt", axis=0) for chunk in chunks
    ]

    rows_held = after(w_qkv, chunks[0])
    own_rows = lax.dynamic_slice_in_dim(rows_held, core * half_cols, half_cols, 1)
    other_rows = swap(
        lax.dynamic_slice_in_dim(rows_held, (1 - core) * half_cols, half_cols, 1), 1
    )

    projected = []
    for part in range(2):
        if part == 1:
            gathered[1] = after(gathered[1], projected[0])
        normed = pl.pallas_call(
            functools.partial(norm_kernel, wgt_size, chips),
            out_shape=[jax.ShapeDtypeStruct((chunk_rows, block), jnp.bfloat16)] * chips,
            in_specs=[SMEM, HBM, VMEM, VMEM],
            out_specs=[VMEM] * chips,
            scratch_shapes=[
                pltpu.VMEM((wgt_size, chunk_rows, width), jnp.bfloat16),
                pltpu.SemaphoreType.DMA,
            ],
            compiler_params=pltpu.CompilerParams(vmem_limit_bytes=VMEM_LIMIT),
            name="norm",
        )(where, gathered[part], gain, shift)

        tokens = []
        for distance in range(chips):
            mine = normed[distance] if distance == 0 else swap(normed[distance], 2 * distance)
            tokens += [mine, swap(mine, 1)]

        partial = pl.pallas_call(
            functools.partial(project_kernel, fresh_len, half, part),
            out_shape=jax.ShapeDtypeStruct((req_size, chunk_rows, half_cols), jnp.bfloat16),
            in_specs=[SMEM] * 2 + [HBM] * (req_size + 2),
            out_specs=HBM,
            scratch_shapes=[
                pltpu.VMEM((req_size * half, fresh_len, block), jnp.bfloat16),
                pltpu.VMEM((block, half_cols), jnp.bfloat16),
                pltpu.VMEM((min(req_size, 4) * chunk_rows, block), jnp.bfloat16),
                pltpu.VMEM((req_size, chunk_rows, half_cols), jnp.bfloat16),
                pltpu.SemaphoreType.DMA((req_size,)),
                pltpu.SemaphoreType.DMA((2,)),
                pltpu.SemaphoreType.DMA((req_size // min(req_size, 4),)),
            ],
            compiler_params=pltpu.CompilerParams(vmem_limit_bytes=VMEM_LIMIT),
            name="project",
        )(
            place,
            sources,
            *[token.reshape(half, fresh_len, block) for token in tokens],
            own_rows,
            other_rows,
        )

        projected.append(partial)

    results = []
    for part in range(2):
        parts = lax.all_to_all(projected[part], "req", 0, 0, tiled=True)
        if part == 0:
            parts = after(parts, projected[1])

        operands = [
            slots, lengths, page_table, parts, bias, *tables, key_pool, value_pool
        ]
        specs = [SMEM] * 3 + [VMEM] * 5 + [HBM] * 2
        count = half if part == 0 else req_count
        out = jax.ShapeDtypeStruct((count, fresh_len, heads * HEAD), jnp.bfloat16)
        results = pl.pallas_call(
            functools.partial(
                attend_kernel, (req_size, half, fresh_len, page, heads, part)
            ),
            out_shape=[out] * 3,
            in_specs=specs + [VMEM] * len(results),
            out_specs=[VMEM] * 3,
            scratch_shapes=[
                pltpu.VMEM((pages, page, heads * HEAD), jnp.bfloat16),
                pltpu.VMEM((pages, page, heads * HEAD), jnp.bfloat16),
                pltpu.SemaphoreType.DMA((half,)),
            ],
            compiler_params=pltpu.CompilerParams(vmem_limit_bytes=VMEM_LIMIT),
            name="attend",
        )(*operands, *results)
    return results


def solution(mesh):
    in_specs = (
        P("req", None, "wgt"),
        P(),
        P("req"),
        P("req", None),
        P(),
        P(),
        P("req", "wgt"),
        P("wgt"),
        P("req", None, "wgt"),
        P("req", None, "wgt"),
    )
    out_specs = (P("req", None, "wgt"), P("req", None, "wgt"), P("req", None, "wgt"))
    return jax.shard_map(
        functools.partial(per_device, mesh.shape["req"], mesh.shape["wgt"]),
        mesh=mesh,
        in_specs=in_specs,
        out_specs=out_specs,
        check_vma=False,
    )
```

```python
import functools
import math

import jax
import jax.numpy as jnp
import numpy as np
from jax import lax
from jax.experimental import pallas as pl
from jax.experimental.pallas import tpu as pltpu
from jax.sharding import PartitionSpec as P

HEAD = 96
ROT = 24
EPS = 1e-05
LANES = 128
WINDOW = 2 * LANES
CHUNK_PAGES = 4
REQUESTS = 4
VMEM_LIMIT = 58 * 1024 * 1024

SMEM = pl.BlockSpec(memory_space=pltpu.SMEM)
VMEM = pl.BlockSpec(memory_space=pltpu.VMEM)
HBM = pl.BlockSpec(memory_space=pltpu.HBM)


def plan_kernel(place, group_of, arrivals, slots, sources, *refs):
    parts = refs[:REQUESTS]
    order, slot_of, color, shade, filled, sems = refs[REQUESTS:]
    everyone = group_of.shape[0]
    groups = everyone // REQUESTS
    me = place[0]
    core = me & 1

    def clear(group, carry):
        filled[group] = 0
        return carry

    lax.fori_loop(0, groups, clear, 0)

    def rank(item, carry):
        group = group_of[item]
        slot = group * REQUESTS + filled[group]
        filled[group] = filled[group] + 1
        slot_of[item] = slot
        order[slot] = item
        color[item] = -1
        shade[item] = -1
        return carry

    lax.fori_loop(0, everyone, rank, 0)

    def halve(pair, carry):
        def body(state):
            item = state[0]
            color[item] = 0
            color[item ^ 1] = 1
            following = order[slot_of[item ^ 1] ^ 1]
            return following, color[following]

        lax.while_loop(lambda state: state[1] < 0, body, (2 * pair, color[2 * pair]))
        return carry

    lax.fori_loop(0, everyone // 2, halve, 0)

    def note(item, part):
        slot = slot_of[item]
        origin = item >> 2
        row = ((origin & 1) ^ core) * (groups // 2) + (origin >> 1)
        sources[part * groups + (slot >> 2)] = row
        return slot

    def quarter(source, carry):
        for half in range(2):

            def body(state, half=half):
                item = state[0]
                other = (item & -4) + ((item & 2) ^ 2)
                other = other + (color[other] ^ half)
                shade[item] = 0
                shade[other] = 1
                note(item, 2 * half)
                slot = note(other, 2 * half + 1)
                following = (slot & -4) + ((slot & 2) ^ 2)
                following = order[following + (color[order[following]] ^ half)]
                return following, shade[following]

            first = REQUESTS * source
            first = first + (color[first] ^ half)
            lax.while_loop(lambda state: state[1] < 0, body, (first, shade[first]))
        return carry

    lax.fori_loop(0, groups, quarter, 0)

    depth = parts[0].shape[0]
    copies = []
    for half in range(2):
        first = REQUESTS * me
        first = first + (color[first] ^ half)
        second = REQUESTS * me + 2
        second = second + (color[second] ^ half)
        tone = shade[first]
        for which in range(2):
            item = jnp.where(tone == which, first, second)
            for layer in range(depth):
                copies.append(
                    pltpu.make_async_copy(
                        arrivals.at[item & 3],
                        parts[2 * half + which].at[layer],
                        sems.at[2 * half + which, layer],
                    )
                )
    for copy in copies:
        copy.start()
    for half in range(2):
        first = REQUESTS * me
        first = first + (color[order[first]] ^ half)
        second = REQUESTS * me + 2
        second = second + (color[order[second]] ^ half)
        tone = shade[order[first]]
        for which in range(2):
            slots[2 * half + which] = jnp.where(tone == which, first, second) & 3
    for copy in copies:
        copy.wait()


def norm_kernel(gathered, gain, bias, out, held, sem):
    depth, rows, width = held.shape
    chips, _, block = out.shape
    copy = pltpu.make_async_copy(gathered, held, sem)
    copy.start()
    copy.wait()
    step = 16
    per = chips // depth

    def body(index, carry):
        at = pl.ds(pl.multiple_of(index * step, step), step)
        values = [held[layer, at, :].astype(jnp.float32) for layer in range(depth)]
        total = sum(jnp.sum(value, axis=-1, keepdims=True) for value in values)
        center = total / (depth * width)
        values = [value - center for value in values]
        square = sum(jnp.sum(jnp.square(value), axis=-1, keepdims=True) for value in values)
        scale = lax.rsqrt(square / (depth * width) + EPS)
        for chip in range(chips):
            begin = chip % per * block
            value = values[chip // per][:, begin : begin + block]
            value = value * scale * gain[chip] + bias[chip]
            out[chip, at, :] = value.astype(jnp.bfloat16)
        return carry

    lax.fori_loop(0, rows // step, body, 0, unroll=True)


def project_kernel(part, place, source, *refs):
    mine, other, own_rows, other_rows, out, held, weights, picked, ready, sems = refs
    core = place[0]
    depth = own_rows.shape[0]
    chips = mine.shape[0]
    groups, rows, _ = out.shape
    copies = [
        pltpu.make_async_copy(
            own_rows, weights.at[pl.ds(pl.multiple_of(core * depth, 16), depth)], sems.at[0]
        ),
        pltpu.make_async_copy(
            other_rows,
            weights.at[pl.ds(pl.multiple_of((1 - core) * depth, 16), depth)],
            sems.at[1],
        ),
        pltpu.make_async_copy(mine, held.at[pl.ds(0, chips)], sems.at[2]),
        pltpu.make_async_copy(other, held.at[pl.ds(chips, chips)], sems.at[3]),
    ]
    for copy in copies:
        copy.start()
    for copy in copies[2:]:
        copy.wait()
    for group in range(groups):
        picked[group * rows : (group + 1) * rows, :] = held[source[part * groups + group]]
    for copy in copies[:2]:
        copy.wait()
    together = min(groups, 8)
    for first in range(0, groups, together):
        result = jnp.dot(
            picked[first * rows : (first + together) * rows, :],
            weights[...],
            preferred_element_type=jnp.float32,
        ).astype(jnp.bfloat16)
        for index in range(together):
            ready[first + index] = result[index * rows : (index + 1) * rows]
    copy = pltpu.make_async_copy(ready, out, sems.at[0])
    copy.start()
    copy.wait()


def attend_kernel(shape, slots, all_lengths, table, *refs):
    groups, held_count, fresh_len, page, heads, part = shape
    parts, bias, cosine, sine_up, sine_down, key_pool, value_pool = refs[:7]
    before = refs[7:-6]
    outs = refs[-6:-3]
    keys, values, sems = refs[-3:]
    chunk = CHUNK_PAGES * page
    pairs = heads // 2

    slot = [slots[part * held_count + index] for index in range(held_count)]
    lengths = [all_lengths[slot[index]] for index in range(held_count)]
    counts = [pl.cdiv(lengths[index], chunk) for index in range(held_count)]
    bases = [jnp.int32(0)]
    for count in counts[:-1]:
        bases.append(bases[-1] + count * CHUNK_PAGES)

    def copies(index, entry):
        number = table[slot[index], entry]
        to = bases[index] + entry
        return (
            pltpu.make_async_copy(key_pool.at[number], keys.at[to], sems.at[index]),
            pltpu.make_async_copy(value_pool.at[number], values.at[to], sems.at[index]),
        )

    for index in range(held_count):

        def start(entry, carry, index=index):
            for copy in copies(index, entry):
                copy.start()
            return carry

        lax.fori_loop(0, counts[index] * CHUNK_PAGES, start, 0)

    def cached(pages, index, part, pair):
        held = pages[
            pl.ds(bases[index] + part * CHUNK_PAGES, CHUNK_PAGES),
            :,
            starts[pair] : starts[pair] + WINDOW,
        ]
        return held.reshape(chunk, WINDOW)

    halves = [
        sum(parts[index].astype(jnp.float32) for index in range(side, groups, 2))
        for side in range(2)
    ]
    halves = [
        half + bias[:, side * half.shape[1] : (side + 1) * half.shape[1]]
        for side, half in enumerate(halves)
    ]

    def kind(which):
        pieces = []
        for head in range(heads):
            half = halves[head // pairs]
            begin = (head % pairs) * 3 * HEAD + which * HEAD
            pieces.append(half[:, begin : begin + HEAD])
        return jnp.concatenate(pieces, axis=1)

    width = heads * HEAD

    def rows_of(ref):
        return jnp.concatenate([ref[slot[index]] for index in range(held_count)], axis=0)

    cosine, sine_up, sine_down = rows_of(cosine), rows_of(sine_up), rows_of(sine_down)

    def turn(block):
        half_rot = ROT // 2
        return (
            block * cosine
            + pltpu.roll(block, width - half_rot, 1) * sine_up
            + pltpu.roll(block, half_rot, 1) * sine_down
        )

    queries = turn(kind(0)).astype(jnp.bfloat16)
    turned = turn(kind(1)).astype(jnp.bfloat16)
    plain = kind(2).astype(jnp.bfloat16)

    def put(which, index, value):
        outs[which][slot[index] if before else index] = value

    for number, held in enumerate(before):
        for index in range(held_count):
            outs[number % 3][slots[number // 3 * held_count + index]] = held[index]
    for index in range(held_count):
        rows = slice(index * fresh_len, (index + 1) * fresh_len)
        put(1, index, turned[rows])
        put(2, index, plain[rows])

    factor = 1.0 / math.sqrt(HEAD) / math.log(2.0)
    starts = [(2 * HEAD * pair) // LANES * LANES for pair in range(pairs)]
    lane = lax.broadcasted_iota(jnp.int32, (fresh_len, WINDOW), 1)

    def owned(pair, member):
        begin = (2 * pair + member) * HEAD - starts[pair]
        return (lane >= begin) & (lane < begin + HEAD)

    def contract(left, right):
        return lax.dot_general(
            left, right, (((1,), (1,)), ((), ())), preferred_element_type=jnp.float32
        )

    zero = jnp.zeros((fresh_len, WINDOW), jnp.bfloat16)
    spread_rows = heads * fresh_len
    row = lax.broadcasted_iota(jnp.int32, (2 * fresh_len, fresh_len), 0)
    causal_pair = lax.rem(row, fresh_len) >= lax.broadcasted_iota(
        jnp.int32, (2 * fresh_len, fresh_len), 1
    )
    for index in range(held_count):
        rows = slice(index * fresh_len, (index + 1) * fresh_len)
        spread = []
        for pair in range(pairs):
            window = queries[rows, starts[pair] : starts[pair] + WINDOW]
            spread.append(
                jnp.concatenate(
                    [jnp.where(owned(pair, member), window, zero) for member in range(2)], axis=0
                )
            )
        scores = jnp.concatenate(
            [
                jnp.where(
                    causal_pair,
                    contract(spread[pair], turned[rows, starts[pair] : starts[pair] + WINDOW]),
                    -1e30,
                )
                for pair in range(pairs)
            ],
            axis=0,
        )
        peak = jnp.max(scores, axis=1, keepdims=True)
        weight = jnp.exp2((scores - peak) * factor)
        denom = jnp.sum(weight, axis=1, keepdims=True)
        weight = weight.astype(jnp.bfloat16)
        mixed = jnp.concatenate(
            [
                jnp.dot(
                    weight[pair * 2 * fresh_len : (pair + 1) * 2 * fresh_len],
                    plain[rows, starts[pair] : starts[pair] + WINDOW],
                    preferred_element_type=jnp.float32,
                )
                for pair in range(pairs)
            ],
            axis=0,
        )

        def finish(entry, carry, index=index):
            for copy in copies(index, entry):
                copy.wait()
            return carry

        lax.fori_loop(0, counts[index] * CHUNK_PAGES, finish, 0)

        def step(part, carry, index=index, spread=spread):
            peak, denom, mixed = carry
            scores = jnp.concatenate(
                [
                    contract(spread[pair], cached(keys, index, part, pair))
                    for pair in range(pairs)
                ],
                axis=0,
            )
            position = part * chunk + lax.broadcasted_iota(jnp.int32, (spread_rows, chunk), 1)
            scores = jnp.where(position < lengths[index], scores, -1e30)
            higher = jnp.maximum(peak, jnp.max(scores, axis=1, keepdims=True))
            shrink = jnp.exp2((peak - higher) * factor)
            weight = jnp.exp2((scores - higher) * factor)
            denom = denom * shrink + jnp.sum(weight, axis=1, keepdims=True)
            weight = weight.astype(jnp.bfloat16)
            added = jnp.concatenate(
                [
                    jnp.dot(
                        weight[pair * 2 * fresh_len : (pair + 1) * 2 * fresh_len],
                        cached(values, index, part, pair),
                        preferred_element_type=jnp.float32,
                    )
                    for pair in range(pairs)
                ],
                axis=0,
            )
            return higher, denom, mixed * shrink + added

        peak, denom, mixed = lax.fori_loop(0, counts[index], step, (peak, denom, mixed))
        mixed = mixed / denom
        tiles = [None] * (width // LANES)
        for pair in range(pairs):
            for member in range(2):
                begin = (2 * pair + member) * fresh_len
                part = jnp.where(owned(pair, member), mixed[begin : begin + fresh_len], 0.0)
                for side in range(2):
                    place_at = starts[pair] // LANES + side
                    tile = part[:, side * LANES : (side + 1) * LANES]
                    tiles[place_at] = tile if tiles[place_at] is None else tiles[place_at] + tile
        put(0, index, jnp.concatenate(tiles, axis=1).astype(jnp.bfloat16))


def per_device(
    req_size,
    wgt_size,
    arrivals,
    group_of,
    lengths,
    page_table,
    ln_gain,
    ln_bias,
    w_qkv,
    qkv_bias,
    key_pool,
    value_pool,
):
    req_count, fresh_len, width = arrivals.shape
    rows = req_count * fresh_len
    depth, local_cols = w_qkv.shape
    half_cols = local_cols // 2
    heads = local_cols // (3 * HEAD)
    page = key_pool.shape[1]
    chips = req_size // 2
    block = 2 * depth
    everyone = group_of.shape[0]
    me = lax.axis_index("req")
    core = me & 1

    def swap(value, distance):
        return lax.ppermute(
            value, "req", [(device, device ^ distance) for device in range(req_size)]
        )

    def after(value, others):
        return lax.optimization_barrier((value, others))[0]

    piece = jax.ShapeDtypeStruct((wgt_size, fresh_len, width), jnp.bfloat16)
    slots, sources, *quarters = pl.pallas_call(
        plan_kernel,
        out_shape=[
            jax.ShapeDtypeStruct((REQUESTS,), jnp.int32),
            jax.ShapeDtypeStruct((REQUESTS * req_size,), jnp.int32),
        ]
        + [piece] * REQUESTS,
        in_specs=[SMEM, SMEM, HBM],
        out_specs=[SMEM, SMEM] + [VMEM] * REQUESTS,
        scratch_shapes=[pltpu.SMEM((everyone,), jnp.int32)] * 4
        + [
            pltpu.SMEM((req_size,), jnp.int32),
            pltpu.SemaphoreType.DMA((REQUESTS, wgt_size)),
        ],
        name="plan",
    )(jnp.stack([me]).astype(jnp.int32), group_of, arrivals)

    lane = np.arange(heads * HEAD) % HEAD
    half_rot = ROT // 2
    inverse = jnp.power(10000.0, -jnp.asarray(lane % half_rot, jnp.float32) * 2.0 / ROT)
    positions = (
        lengths[:, None] + jnp.arange(fresh_len, dtype=jnp.int32)[None, :]
    ).astype(jnp.float32)
    angles = positions.reshape(rows, 1) * inverse[None, :]
    turns = jnp.asarray(lane < ROT)[None, :]
    cosine = jnp.where(turns, jnp.cos(angles), 1.0)
    sine = jnp.sin(angles)
    sine_up = jnp.where(jnp.asarray(lane < half_rot)[None, :], -sine, 0.0)
    sine_down = jnp.where(turns & jnp.asarray(lane >= half_rot)[None, :], sine, 0.0)

    tables = [
        value.reshape(req_count, fresh_len, heads * HEAD)
        for value in (cosine, sine_up, sine_down)
    ]
    gain = ln_gain.astype(jnp.float32).reshape(chips, 1, block)
    shift = ln_bias.astype(jnp.float32).reshape(chips, 1, block)
    bias = qkv_bias.astype(jnp.float32).reshape(1, local_cols)
    place = jnp.stack([core]).astype(jnp.int32)
    span = page_table.shape[1]
    plane = [[2 * at + side for at in range(chips)] for side in range(2)]
    params = pltpu.CompilerParams(vmem_limit_bytes=VMEM_LIMIT)

    projected, gathered, normed = [], [], None
    for part in range(REQUESTS):
        quarter = quarters[part]
        if part:
            quarter = after(quarter, gathered[-1])
        gathered.append(lax.all_to_all(quarter, "wgt", 0, 0, tiled=True))

        normed = pl.pallas_call(
            norm_kernel,
            out_shape=jax.ShapeDtypeStruct((chips, fresh_len, block), jnp.bfloat16),
            in_specs=[HBM, VMEM, VMEM],
            out_specs=VMEM,
            scratch_shapes=[
                pltpu.VMEM((wgt_size, fresh_len, width), jnp.bfloat16),
                pltpu.SemaphoreType.DMA,
            ],
            compiler_params=params,
            name="norm",
        )(gathered[-1], gain, shift)

        if part == 0:
            held = after(w_qkv, normed)
            own_rows = lax.dynamic_slice_in_dim(held, core * half_cols, half_cols, 1)
            other_rows = swap(
                lax.dynamic_slice_in_dim(held, (1 - core) * half_cols, half_cols, 1), 1
            )

        mine = lax.all_to_all(normed, "req", 0, 0, axis_index_groups=plane, tiled=True)
        other = swap(mine, 1)

        projected.append(
            pl.pallas_call(
                functools.partial(project_kernel, part),
                out_shape=jax.ShapeDtypeStruct((req_size, fresh_len, half_cols), jnp.bfloat16),
                in_specs=[SMEM] * 2 + [HBM] * 4,
                out_specs=HBM,
                scratch_shapes=[
                    pltpu.VMEM((req_size, fresh_len, block), jnp.bfloat16),
                    pltpu.VMEM((block, half_cols), jnp.bfloat16),
                    pltpu.VMEM((req_size * fresh_len, block), jnp.bfloat16),
                    pltpu.VMEM((req_size, fresh_len, half_cols), jnp.bfloat16),
                    pltpu.SemaphoreType.DMA((4,)),
                ],
                compiler_params=params,
                name="project",
            )(place, sources, mine, other, own_rows, other_rows)
        )

    results = []
    for part in range(REQUESTS):
        sums = lax.all_to_all(projected[part], "req", 0, 0, tiled=True)
        last = part == REQUESTS - 1
        if not last:
            sums = after(sums, projected[part + 1])
        before = results if last else []
        out = jax.ShapeDtypeStruct(
            (REQUESTS if last else 1, fresh_len, heads * HEAD), jnp.bfloat16
        )
        results += pl.pallas_call(
            functools.partial(attend_kernel, (req_size, 1, fresh_len, page, heads, part)),
            out_shape=[out] * 3,
            in_specs=[SMEM] * 3 + [VMEM] * 5 + [HBM] * 2 + [VMEM] * len(before),
            out_specs=[VMEM] * 3,
            scratch_shapes=[
                pltpu.VMEM((span, page, heads * HEAD), jnp.bfloat16),
                pltpu.VMEM((span, page, heads * HEAD), jnp.bfloat16),
                pltpu.SemaphoreType.DMA((1,)),
            ],
            compiler_params=params,
            name="attend",
        )(slots, lengths, page_table, sums, bias, *tables, key_pool, value_pool, *before)
    return tuple(results[-3:])


def solution(mesh):
    in_specs = (
        P("req", None, "wgt"),
        P(),
        P("req"),
        P("req", None),
        P(),
        P(),
        P("req", "wgt"),
        P("wgt"),
        P("req", None, "wgt"),
        P("req", None, "wgt"),
    )
    out_specs = (P("req", None, "wgt"), P("req", None, "wgt"), P("req", None, "wgt"))
    return jax.shard_map(
        functools.partial(per_device, mesh.shape["req"], mesh.shape["wgt"]),
        mesh=mesh,
        in_specs=in_specs,
        out_specs=out_specs,
        check_vma=False,
    )
```

```python
import functools
import math

import jax
import jax.numpy as jnp
import numpy as np
from jax import lax
from jax.experimental import pallas as pl
from jax.experimental.pallas import tpu as pltpu
from jax.sharding import PartitionSpec as P

HEAD = 96
ROT = 24
EPS = 1e-05
LANES = 128
WINDOW = 2 * LANES
CHUNK_PAGES = 4
VMEM_LIMIT = 58 * 1024 * 1024

SMEM = pl.BlockSpec(memory_space=pltpu.SMEM)
VMEM = pl.BlockSpec(memory_space=pltpu.VMEM)
HBM = pl.BlockSpec(memory_space=pltpu.HBM)


def plan_kernel(req_count, place, group_of, arrivals, slots, sources, picks, stats, *refs):
    order, slot_of, color, filled = refs
    everyone = group_of.shape[0]
    groups = everyone // req_count
    half = req_count // 2
    me = place[0]

    def clear(group, carry):
        filled[group] = 0
        return carry

    lax.fori_loop(0, groups, clear, 0)

    def rank(item, carry):
        group = group_of[item]
        slot = group * req_count + filled[group]
        filled[group] = filled[group] + 1
        slot_of[item] = slot
        order[slot] = item
        color[item] = -1
        return carry

    lax.fori_loop(0, everyone, rank, 0)

    shift = req_count.bit_length() - 1

    def note(item, shade):
        color[item] = shade
        slot = slot_of[item]
        to = (shade * groups + (slot >> shift)) * half + ((slot & (req_count - 1)) >> 1)
        origin = item >> shift
        row = ((origin & 1) ^ (me & 1)) * (groups // 2) + (origin >> 1)
        sources[to] = row * half + ((item & (req_count - 1)) >> 1)
        return slot

    def walk(pair, carry):
        def body(state):
            note(state[0], 0)
            following = order[note(state[0] ^ 1, 1) ^ 1]
            return following, color[following]

        lax.while_loop(lambda state: state[1] < 0, body, (2 * pair, color[2 * pair]))
        return carry

    lax.fori_loop(0, everyone // 2, walk, 0)

    for pair in range(half):
        first = color[me * req_count + 2 * pair]
        for part in range(2):
            picks[part * half + pair] = 2 * pair + (first ^ part)
        first = color[order[me * req_count + 2 * pair]]
        for part in range(2):
            slots[part * half + pair] = 2 * pair + (first ^ part)

    fresh_len, width = arrivals.shape[1:]

    def measure(index, carry):
        value = arrivals[index].astype(jnp.float32)
        center = jnp.sum(value, axis=-1, keepdims=True) / width
        square = jnp.sum(jnp.square(value - center), axis=-1, keepdims=True)
        lane = lax.broadcasted_iota(jnp.int32, (fresh_len, LANES), 1)
        stats[index] = jnp.where(lane == 0, center, jnp.where(lane == 1, square, 0.0))
        return carry

    lax.fori_loop(0, req_count, measure, 0)


def norm_kernel(picks, arrivals, gain, bias, *refs):
    stats, outs = refs[:-2], refs[-2:]
    depth = len(stats)
    width = arrivals.shape[2]
    blocks, rows, block = outs[0].shape
    fresh_len = arrivals.shape[1]
    held_count = rows // fresh_len
    for part, out in enumerate(outs):
        for item in range(held_count):
            index = picks[part * held_count + item]
            pairs = [ref[index] for ref in stats]
            center = sum(pair[:, 0:1] for pair in pairs) / depth
            square = sum(
                pair[:, 1:2] + width * jnp.square(pair[:, 0:1] - center) for pair in pairs
            )
            scale = lax.rsqrt(square / (depth * width) + EPS)
            value = (arrivals[index].astype(jnp.float32) - center) * scale
            value = (value * gain[...] + bias[...]).astype(jnp.bfloat16)
            for place in range(blocks):
                out[place, item * fresh_len : (item + 1) * fresh_len, :] = value[
                    :, place * block : (place + 1) * block
                ]


def project_kernel(fresh_len, held_count, part, place, source, *refs):
    groups = len(refs) - 10
    tokens = refs[:groups]
    own_rows, other_rows = refs[groups : groups + 2]
    out, held, weights, picked, ready, sems, weight_sems, out_sems = refs[groups + 2 :]
    core, begin = place[0], place[1]
    depth = own_rows.shape[0]
    copies = [
        pltpu.make_async_copy(
            own_rows,
            weights.at[pl.ds(pl.multiple_of(core * depth, 16), depth)],
            weight_sems.at[0],
        ),
        pltpu.make_async_copy(
            other_rows,
            weights.at[pl.ds(pl.multiple_of((1 - core) * depth, 16), depth)],
            weight_sems.at[1],
        ),
    ]
    chips = groups // 2
    copies += [
        pltpu.make_async_copy(
            token,
            held.at[
                pl.ds(
                    (index // chips * chips + (index % chips ^ begin)) * held_count, held_count
                )
            ],
            sems.at[index],
        )
        for index, token in enumerate(tokens)
    ]
    for copy in copies:
        copy.start()
    for copy in copies:
        copy.wait()
    rows = held_count * fresh_len
    together = min(groups, 4)
    for first in range(0, groups, together):
        for item in range(together * held_count):
            picked[item * fresh_len : (item + 1) * fresh_len, :] = held[
                source[(part * groups + first) * held_count + item]
            ]
        result = jnp.dot(picked[...], weights[...], preferred_element_type=jnp.float32).astype(
            jnp.bfloat16
        )
        for index in range(together):
            ready[first + index] = result[index * rows : (index + 1) * rows]
        targets = pl.ds(first, together)
        copies.append(
            pltpu.make_async_copy(
                ready.at[targets], out.at[targets], out_sems.at[first // together]
            )
        )
        copies[-1].start()
    for copy in copies[groups + 2 :]:
        copy.wait()


def attend_kernel(shape, slots, all_lengths, table, *refs):
    groups, held_count, fresh_len, page, heads, part = shape
    parts, bias, cosine, sine_up, sine_down, key_pool, value_pool = refs[:7]
    before = refs[7:-6]
    outs = refs[-6:-3]
    keys, values, sems = refs[-3:]
    chunk = CHUNK_PAGES * page
    pairs = heads // 2

    slot = [slots[part * held_count + index] for index in range(held_count)]
    lengths = [all_lengths[slot[index]] for index in range(held_count)]
    counts = [pl.cdiv(lengths[index], chunk) for index in range(held_count)]
    bases = [jnp.int32(0)]
    for count in counts[:-1]:
        bases.append(bases[-1] + count * CHUNK_PAGES)

    def copies(index, entry):
        number = table[slot[index], entry]
        to = bases[index] + entry
        return (
            pltpu.make_async_copy(key_pool.at[number], keys.at[to], sems.at[index]),
            pltpu.make_async_copy(value_pool.at[number], values.at[to], sems.at[index]),
        )

    for index in range(held_count):

        def start(entry, carry, index=index):
            for copy in copies(index, entry):
                copy.start()
            return carry

        lax.fori_loop(0, counts[index] * CHUNK_PAGES, start, 0)

    def cached(pages, index, part, pair):
        held = pages[
            pl.ds(bases[index] + part * CHUNK_PAGES, CHUNK_PAGES),
            :,
            starts[pair] : starts[pair] + WINDOW,
        ]
        return held.reshape(chunk, WINDOW)

    halves = [
        sum(parts[index].astype(jnp.float32) for index in range(side, groups, 2))
        for side in range(2)
    ]
    halves = [
        half + bias[:, side * half.shape[1] : (side + 1) * half.shape[1]]
        for side, half in enumerate(halves)
    ]

    def kind(which):
        pieces = []
        for head in range(heads):
            half = halves[head // pairs]
            begin = (head % pairs) * 3 * HEAD + which * HEAD
            pieces.append(half[:, begin : begin + HEAD])
        return jnp.concatenate(pieces, axis=1)

    width = heads * HEAD

    def rows_of(ref):
        return jnp.concatenate([ref[slot[index]] for index in range(held_count)], axis=0)

    cosine, sine_up, sine_down = rows_of(cosine), rows_of(sine_up), rows_of(sine_down)

    def turn(block):
        half_rot = ROT // 2
        return (
            block * cosine
            + pltpu.roll(block, width - half_rot, 1) * sine_up
            + pltpu.roll(block, half_rot, 1) * sine_down
        )

    queries = turn(kind(0)).astype(jnp.bfloat16)
    turned = turn(kind(1)).astype(jnp.bfloat16)
    plain = kind(2).astype(jnp.bfloat16)

    def put(which, index, value):
        outs[which][slot[index] if before else index] = value

    for which, held in enumerate(before):
        for index in range(held_count):
            outs[which][slots[index]] = held[index]
    for index in range(held_count):
        rows = slice(index * fresh_len, (index + 1) * fresh_len)
        put(1, index, turned[rows])
        put(2, index, plain[rows])

    factor = 1.0 / math.sqrt(HEAD) / math.log(2.0)
    starts = [(2 * HEAD * pair) // LANES * LANES for pair in range(pairs)]
    lane = lax.broadcasted_iota(jnp.int32, (fresh_len, WINDOW), 1)

    def owned(pair, member):
        begin = (2 * pair + member) * HEAD - starts[pair]
        return (lane >= begin) & (lane < begin + HEAD)

    def contract(left, right):
        return lax.dot_general(
            left, right, (((1,), (1,)), ((), ())), preferred_element_type=jnp.float32
        )

    zero = jnp.zeros((fresh_len, WINDOW), jnp.bfloat16)
    spread_rows = heads * fresh_len
    row = lax.broadcasted_iota(jnp.int32, (2 * fresh_len, fresh_len), 0)
    causal_pair = lax.rem(row, fresh_len) >= lax.broadcasted_iota(
        jnp.int32, (2 * fresh_len, fresh_len), 1
    )
    for index in range(held_count):
        rows = slice(index * fresh_len, (index + 1) * fresh_len)
        spread = []
        for pair in range(pairs):
            window = queries[rows, starts[pair] : starts[pair] + WINDOW]
            spread.append(
                jnp.concatenate(
                    [jnp.where(owned(pair, member), window, zero) for member in range(2)], axis=0
                )
            )
        scores = jnp.concatenate(
            [
                jnp.where(
                    causal_pair,
                    contract(spread[pair], turned[rows, starts[pair] : starts[pair] + WINDOW]),
                    -1e30,
                )
                for pair in range(pairs)
            ],
            axis=0,
        )
        peak = jnp.max(scores, axis=1, keepdims=True)
        weight = jnp.exp2((scores - peak) * factor)
        denom = jnp.sum(weight, axis=1, keepdims=True)
        weight = weight.astype(jnp.bfloat16)
        mixed = jnp.concatenate(
            [
                jnp.dot(
                    weight[pair * 2 * fresh_len : (pair + 1) * 2 * fresh_len],
                    plain[rows, starts[pair] : starts[pair] + WINDOW],
                    preferred_element_type=jnp.float32,
                )
                for pair in range(pairs)
            ],
            axis=0,
        )

        def finish(entry, carry, index=index):
            for copy in copies(index, entry):
                copy.wait()
            return carry

        lax.fori_loop(0, counts[index] * CHUNK_PAGES, finish, 0)

        def step(part, carry, index=index, spread=spread):
            peak, denom, mixed = carry
            scores = jnp.concatenate(
                [
                    contract(spread[pair], cached(keys, index, part, pair))
                    for pair in range(pairs)
                ],
                axis=0,
            )
            position = part * chunk + lax.broadcasted_iota(jnp.int32, (spread_rows, chunk), 1)
            scores = jnp.where(position < lengths[index], scores, -1e30)
            higher = jnp.maximum(peak, jnp.max(scores, axis=1, keepdims=True))
            shrink = jnp.exp2((peak - higher) * factor)
            weight = jnp.exp2((scores - higher) * factor)
            denom = denom * shrink + jnp.sum(weight, axis=1, keepdims=True)
            weight = weight.astype(jnp.bfloat16)
            added = jnp.concatenate(
                [
                    jnp.dot(
                        weight[pair * 2 * fresh_len : (pair + 1) * 2 * fresh_len],
                        cached(values, index, part, pair),
                        preferred_element_type=jnp.float32,
                    )
                    for pair in range(pairs)
                ],
                axis=0,
            )
            return higher, denom, mixed * shrink + added

        peak, denom, mixed = lax.fori_loop(0, counts[index], step, (peak, denom, mixed))
        mixed = mixed / denom
        tiles = [None] * (width // LANES)
        for pair in range(pairs):
            for member in range(2):
                begin = (2 * pair + member) * fresh_len
                part = jnp.where(owned(pair, member), mixed[begin : begin + fresh_len], 0.0)
                for side in range(2):
                    place_at = starts[pair] // LANES + side
                    tile = part[:, side * LANES : (side + 1) * LANES]
                    tiles[place_at] = tile if tiles[place_at] is None else tiles[place_at] + tile
        put(0, index, jnp.concatenate(tiles, axis=1).astype(jnp.bfloat16))


def per_device(
    req_size,
    wgt_size,
    arrivals,
    group_of,
    lengths,
    page_table,
    ln_gain,
    ln_bias,
    w_qkv,
    qkv_bias,
    key_pool,
    value_pool,
):
    req_count, fresh_len, width = arrivals.shape
    rows = req_count * fresh_len
    depth, local_cols = w_qkv.shape
    half_cols = local_cols // 2
    heads = local_cols // (3 * HEAD)
    page = key_pool.shape[1]
    chips = req_size // 2
    block = 2 * depth
    everyone = group_of.shape[0]
    me = lax.axis_index("req")
    layer = lax.axis_index("wgt")
    core = me & 1
    chip = me >> 1

    def swap(value, distance):
        return lax.ppermute(
            value, "req", [(device, device ^ distance) for device in range(req_size)]
        )

    def after(value, others):
        return lax.optimization_barrier((value, others))[0]

    half = req_count // 2
    slots, sources, picks, stats = pl.pallas_call(
        functools.partial(plan_kernel, req_count),
        out_shape=[
            jax.ShapeDtypeStruct((2 * half,), jnp.int32),
            jax.ShapeDtypeStruct((2 * req_size * half,), jnp.int32),
            jax.ShapeDtypeStruct((2 * half,), jnp.int32),
            jax.ShapeDtypeStruct((req_count, fresh_len, LANES), jnp.float32),
        ],
        in_specs=[SMEM, SMEM, VMEM],
        out_specs=[SMEM, SMEM, SMEM, VMEM],
        scratch_shapes=[
            pltpu.SMEM((everyone,), jnp.int32),
            pltpu.SMEM((everyone,), jnp.int32),
            pltpu.SMEM((everyone,), jnp.int32),
            pltpu.SMEM((req_size,), jnp.int32),
        ],
        name="plan",
    )(jnp.stack([me]).astype(jnp.int32), group_of, arrivals)

    lane = np.arange(heads * HEAD) % HEAD
    half_rot = ROT // 2
    inverse = jnp.power(10000.0, -jnp.asarray(lane % half_rot, jnp.float32) * 2.0 / ROT)
    positions = (
        lengths[:, None] + jnp.arange(fresh_len, dtype=jnp.int32)[None, :]
    ).astype(jnp.float32)
    angles = positions.reshape(rows, 1) * inverse[None, :]
    turns = jnp.asarray(lane < ROT)[None, :]
    cosine = jnp.where(turns, jnp.cos(angles), 1.0)
    sine = jnp.sin(angles)
    sine_up = jnp.where(jnp.asarray(lane < half_rot)[None, :], -sine, 0.0)
    sine_down = jnp.where(turns & jnp.asarray(lane >= half_rot)[None, :], sine, 0.0)

    tables = [
        value.reshape(req_count, fresh_len, heads * HEAD)
        for value in (cosine, sine_up, sine_down)
    ]
    layer = lax.axis_index("wgt")
    per = chips // wgt_size
    gain, shift = (
        lax.dynamic_slice_in_dim(value, layer * width, width).astype(jnp.float32).reshape(1, width)
        for value in (ln_gain, ln_bias)
    )
    bias = qkv_bias.astype(jnp.float32).reshape(1, local_cols)
    place = jnp.stack([core, layer * per + chip % per]).astype(jnp.int32)
    chunk_rows = half * fresh_len
    span = page_table.shape[1]
    pages = span + (half - 1) * (span // 2)

    measured = [stats] + [
        lax.ppermute(stats, "wgt", [(at, at ^ distance) for at in range(wgt_size)])
        for distance in range(1, wgt_size)
    ]
    normed = pl.pallas_call(
        norm_kernel,
        out_shape=[jax.ShapeDtypeStruct((per, chunk_rows, block), jnp.bfloat16)] * 2,
        in_specs=[SMEM] + [VMEM] * (3 + wgt_size),
        out_specs=[VMEM] * 2,
        compiler_params=pltpu.CompilerParams(vmem_limit_bytes=VMEM_LIMIT),
        name="norm",
    )(picks, arrivals, gain, shift, *measured)

    def route(value, turn):
        pairs = []
        for device in range(req_size):
            for at in range(wgt_size):
                to = device // 2
                origin = turn ^ (at * per + to % per)
                pairs.append(
                    ((2 * origin + device % 2) * wgt_size + to // per, device * wgt_size + at)
                )
        return lax.ppermute(value, ("req", "wgt"), pairs)

    pieces = []
    for part in range(2):
        received = []
        for turn in range(chips):
            sent = normed[part]
            sent = sent[0] if per == 1 else lax.dynamic_index_in_dim(
                sent, (chip ^ turn) % per, 0, False
            )
            if part:
                sent = after(sent, pieces[0][turn])
            received.append(route(sent, turn))
        pieces.append(received)

    rows_held = after(w_qkv, stats)
    own_rows = lax.dynamic_slice_in_dim(rows_held, core * half_cols, half_cols, 1)
    other_rows = swap(
        lax.dynamic_slice_in_dim(rows_held, (1 - core) * half_cols, half_cols, 1), 1
    )

    projected = []
    for part in range(2):
        tokens = pieces[part] + [swap(piece, 1) for piece in pieces[part]]

        partial = pl.pallas_call(
            functools.partial(project_kernel, fresh_len, half, part),
            out_shape=jax.ShapeDtypeStruct((req_size, chunk_rows, half_cols), jnp.bfloat16),
            in_specs=[SMEM] * 2 + [HBM] * (req_size + 2),
            out_specs=HBM,
            scratch_shapes=[
                pltpu.VMEM((req_size * half, fresh_len, block), jnp.bfloat16),
                pltpu.VMEM((block, half_cols), jnp.bfloat16),
                pltpu.VMEM((min(req_size, 4) * chunk_rows, block), jnp.bfloat16),
                pltpu.VMEM((req_size, chunk_rows, half_cols), jnp.bfloat16),
                pltpu.SemaphoreType.DMA((req_size,)),
                pltpu.SemaphoreType.DMA((2,)),
                pltpu.SemaphoreType.DMA((req_size // min(req_size, 4),)),
            ],
            compiler_params=pltpu.CompilerParams(vmem_limit_bytes=VMEM_LIMIT),
            name="project",
        )(
            place,
            sources,
            *[token.reshape(half, fresh_len, block) for token in tokens],
            own_rows,
            other_rows,
        )

        projected.append(partial)

    results = []
    for part in range(2):
        parts = lax.all_to_all(projected[part], "req", 0, 0, tiled=True)
        if part == 0:
            parts = after(parts, projected[1])

        operands = [
            slots, lengths, page_table, parts, bias, *tables, key_pool, value_pool
        ]
        specs = [SMEM] * 3 + [VMEM] * 5 + [HBM] * 2
        count = half if part == 0 else req_count
        out = jax.ShapeDtypeStruct((count, fresh_len, heads * HEAD), jnp.bfloat16)
        results = pl.pallas_call(
            functools.partial(
                attend_kernel, (req_size, half, fresh_len, page, heads, part)
            ),
            out_shape=[out] * 3,
            in_specs=specs + [VMEM] * len(results),
            out_specs=[VMEM] * 3,
            scratch_shapes=[
                pltpu.VMEM((pages, page, heads * HEAD), jnp.bfloat16),
                pltpu.VMEM((pages, page, heads * HEAD), jnp.bfloat16),
                pltpu.SemaphoreType.DMA((half,)),
            ],
            compiler_params=pltpu.CompilerParams(vmem_limit_bytes=VMEM_LIMIT),
            name="attend",
        )(*operands, *results)
    return results


def solution(mesh):
    in_specs = (
        P("req", None, "wgt"),
        P(),
        P("req"),
        P("req", None),
        P(),
        P(),
        P("req", "wgt"),
        P("wgt"),
        P("req", None, "wgt"),
        P("req", None, "wgt"),
    )
    out_specs = (P("req", None, "wgt"), P("req", None, "wgt"), P("req", None, "wgt"))
    return jax.shard_map(
        functools.partial(per_device, mesh.shape["req"], mesh.shape["wgt"]),
        mesh=mesh,
        in_specs=in_specs,
        out_specs=out_specs,
        check_vma=False,
    )
```

```python
import functools
import math

import jax
import jax.numpy as jnp
import numpy as np
from jax import lax
from jax.experimental import pallas as pl
from jax.experimental.pallas import tpu as pltpu
from jax.sharding import PartitionSpec as P

HEAD = 96
ROT = 24
EPS = 1e-05
LANES = 128
WINDOW = 2 * LANES
CHUNK_PAGES = 4
VMEM_LIMIT = 58 * 1024 * 1024

SMEM = pl.BlockSpec(memory_space=pltpu.SMEM)
VMEM = pl.BlockSpec(memory_space=pltpu.VMEM)
HBM = pl.BlockSpec(memory_space=pltpu.HBM)


def project_kernel(part, place, source, *refs):
    groups = len(refs) - 14
    tokens = refs[:groups]
    center, scale, gain, bias, own_rows, other_rows = refs[groups : groups + 6]
    out, held, weights, picked, ready, sems, weight_sems, out_sems = refs[groups + 6 :]
    core, begin = place[0], place[1]
    depth = own_rows.shape[0]
    chips = groups // 2
    req_count, fresh_len = tokens[0].shape[:2]
    rows = out.shape[1]
    held_count = rows // fresh_len
    copies = [
        pltpu.make_async_copy(
            token,
            held.at[
                pl.ds((index // chips * chips + (index % chips ^ begin)) * req_count, req_count)
            ],
            sems.at[index],
        )
        for index, token in enumerate(tokens)
    ]
    copies += [
        pltpu.make_async_copy(
            own_rows,
            weights.at[pl.ds(pl.multiple_of(core * depth, 16), depth)],
            weight_sems.at[0],
        ),
        pltpu.make_async_copy(
            other_rows,
            weights.at[pl.ds(pl.multiple_of((1 - core) * depth, 16), depth)],
            weight_sems.at[1],
        ),
    ]
    for copy in copies:
        copy.start()
    for copy in copies:
        copy.wait()
    together = min(groups, 4)
    sent = []
    for first in range(0, groups, together):
        for item in range(together * held_count):
            row = source[(part * groups + first) * held_count + item]
            value = held[row].astype(jnp.float32)
            value = (value - center[row][:, 0:1]) * scale[row][:, 0:1]
            value = value * gain[...] + bias[...]
            picked[item * fresh_len : (item + 1) * fresh_len, :] = value.astype(jnp.bfloat16)
        result = jnp.dot(picked[...], weights[...], preferred_element_type=jnp.float32).astype(
            jnp.bfloat16
        )
        for index in range(together):
            ready[first + index] = result[index * rows : (index + 1) * rows]
        targets = pl.ds(first, together)
        sent.append(
            pltpu.make_async_copy(
                ready.at[targets], out.at[targets], out_sems.at[first // together]
            )
        )
        sent[-1].start()
    for copy in sent:
        copy.wait()


def attend_kernel(shape, all_lengths, table, *refs):
    groups, held_count, fresh_len, page, heads, part = shape
    parts, bias, cosine, sine_up, sine_down, key_pool, value_pool = refs[:7]
    before = refs[7:-6]
    outs = refs[-6:-3]
    keys, values, sems = refs[-3:]
    chunk = CHUNK_PAGES * page
    pairs = heads // 2

    slot = [part * held_count + index for index in range(held_count)]
    lengths = [all_lengths[slot[index]] for index in range(held_count)]
    counts = [pl.cdiv(lengths[index], chunk) for index in range(held_count)]
    bases = [jnp.int32(0)]
    for count in counts[:-1]:
        bases.append(bases[-1] + count * CHUNK_PAGES)

    def copies(index, entry):
        number = table[slot[index], entry]
        to = bases[index] + entry
        return (
            pltpu.make_async_copy(key_pool.at[number], keys.at[to], sems.at[index]),
            pltpu.make_async_copy(value_pool.at[number], values.at[to], sems.at[index]),
        )

    for index in range(held_count):

        def start(entry, carry, index=index):
            for copy in copies(index, entry):
                copy.start()
            return carry

        lax.fori_loop(0, counts[index] * CHUNK_PAGES, start, 0)

    def cached(pages, index, part, pair):
        held = pages[
            pl.ds(bases[index] + part * CHUNK_PAGES, CHUNK_PAGES),
            :,
            starts[pair] : starts[pair] + WINDOW,
        ]
        return held.reshape(chunk, WINDOW)

    halves = [
        sum(parts[index].astype(jnp.float32) for index in range(side, groups, 2))
        for side in range(2)
    ]
    halves = [
        half + bias[:, side * half.shape[1] : (side + 1) * half.shape[1]]
        for side, half in enumerate(halves)
    ]

    def kind(which):
        pieces = []
        for head in range(heads):
            half = halves[head // pairs]
            begin = (head % pairs) * 3 * HEAD + which * HEAD
            pieces.append(half[:, begin : begin + HEAD])
        return jnp.concatenate(pieces, axis=1)

    width = heads * HEAD

    def rows_of(ref):
        return jnp.concatenate([ref[slot[index]] for index in range(held_count)], axis=0)

    cosine, sine_up, sine_down = rows_of(cosine), rows_of(sine_up), rows_of(sine_down)

    def turn(block):
        half_rot = ROT // 2
        return (
            block * cosine
            + pltpu.roll(block, width - half_rot, 1) * sine_up
            + pltpu.roll(block, half_rot, 1) * sine_down
        )

    queries = turn(kind(0)).astype(jnp.bfloat16)
    turned = turn(kind(1)).astype(jnp.bfloat16)
    plain = kind(2).astype(jnp.bfloat16)

    def put(which, index, value):
        outs[which][slot[index] if before else index] = value

    for which, held in enumerate(before):
        for index in range(held_count):
            outs[which][index] = held[index]
    for index in range(held_count):
        rows = slice(index * fresh_len, (index + 1) * fresh_len)
        put(1, index, turned[rows])
        put(2, index, plain[rows])

    factor = 1.0 / math.sqrt(HEAD) / math.log(2.0)
    starts = [(2 * HEAD * pair) // LANES * LANES for pair in range(pairs)]
    lane = lax.broadcasted_iota(jnp.int32, (fresh_len, WINDOW), 1)

    def owned(pair, member):
        begin = (2 * pair + member) * HEAD - starts[pair]
        return (lane >= begin) & (lane < begin + HEAD)

    def contract(left, right):
        return lax.dot_general(
            left, right, (((1,), (1,)), ((), ())), preferred_element_type=jnp.float32
        )

    zero = jnp.zeros((fresh_len, WINDOW), jnp.bfloat16)
    spread_rows = heads * fresh_len
    row = lax.broadcasted_iota(jnp.int32, (2 * fresh_len, fresh_len), 0)
    causal_pair = lax.rem(row, fresh_len) >= lax.broadcasted_iota(
        jnp.int32, (2 * fresh_len, fresh_len), 1
    )
    for index in range(held_count):
        rows = slice(index * fresh_len, (index + 1) * fresh_len)
        spread = []
        for pair in range(pairs):
            window = queries[rows, starts[pair] : starts[pair] + WINDOW]
            spread.append(
                jnp.concatenate(
                    [jnp.where(owned(pair, member), window, zero) for member in range(2)], axis=0
                )
            )
        scores = jnp.concatenate(
            [
                jnp.where(
                    causal_pair,
                    contract(spread[pair], turned[rows, starts[pair] : starts[pair] + WINDOW]),
                    -1e30,
                )
                for pair in range(pairs)
            ],
            axis=0,
        )
        peak = jnp.max(scores, axis=1, keepdims=True)
        weight = jnp.exp2((scores - peak) * factor)
        denom = jnp.sum(weight, axis=1, keepdims=True)
        weight = weight.astype(jnp.bfloat16)
        mixed = jnp.concatenate(
            [
                jnp.dot(
                    weight[pair * 2 * fresh_len : (pair + 1) * 2 * fresh_len],
                    plain[rows, starts[pair] : starts[pair] + WINDOW],
                    preferred_element_type=jnp.float32,
                )
                for pair in range(pairs)
            ],
            axis=0,
        )

        def finish(entry, carry, index=index):
            for copy in copies(index, entry):
                copy.wait()
            return carry

        lax.fori_loop(0, counts[index] * CHUNK_PAGES, finish, 0)

        def step(part, carry, index=index, spread=spread):
            peak, denom, mixed = carry
            scores = jnp.concatenate(
                [
                    contract(spread[pair], cached(keys, index, part, pair))
                    for pair in range(pairs)
                ],
                axis=0,
            )
            position = part * chunk + lax.broadcasted_iota(jnp.int32, (spread_rows, chunk), 1)
            scores = jnp.where(position < lengths[index], scores, -1e30)
            higher = jnp.maximum(peak, jnp.max(scores, axis=1, keepdims=True))
            shrink = jnp.exp2((peak - higher) * factor)
            weight = jnp.exp2((scores - higher) * factor)
            denom = denom * shrink + jnp.sum(weight, axis=1, keepdims=True)
            weight = weight.astype(jnp.bfloat16)
            added = jnp.concatenate(
                [
                    jnp.dot(
                        weight[pair * 2 * fresh_len : (pair + 1) * 2 * fresh_len],
                        cached(values, index, part, pair),
                        preferred_element_type=jnp.float32,
                    )
                    for pair in range(pairs)
                ],
                axis=0,
            )
            return higher, denom, mixed * shrink + added

        peak, denom, mixed = lax.fori_loop(0, counts[index], step, (peak, denom, mixed))
        mixed = mixed / denom
        tiles = [None] * (width // LANES)
        for pair in range(pairs):
            for member in range(2):
                begin = (2 * pair + member) * fresh_len
                part = jnp.where(owned(pair, member), mixed[begin : begin + fresh_len], 0.0)
                for side in range(2):
                    place_at = starts[pair] // LANES + side
                    tile = part[:, side * LANES : (side + 1) * LANES]
                    tiles[place_at] = tile if tiles[place_at] is None else tiles[place_at] + tile
        put(0, index, jnp.concatenate(tiles, axis=1).astype(jnp.bfloat16))


def per_device(
    req_size,
    wgt_size,
    arrivals,
    group_of,
    lengths,
    page_table,
    ln_gain,
    ln_bias,
    w_qkv,
    qkv_bias,
    key_pool,
    value_pool,
):
    req_count, fresh_len, width = arrivals.shape
    rows = req_count * fresh_len
    depth, local_cols = w_qkv.shape
    half_cols = local_cols // 2
    heads = local_cols // (3 * HEAD)
    page = key_pool.shape[1]
    chips = req_size // 2
    block = 2 * depth
    everyone = group_of.shape[0]
    me = lax.axis_index("req")
    layer = lax.axis_index("wgt")
    core = me & 1
    chip = me >> 1

    def swap(value, distance):
        return lax.ppermute(
            value, "req", [(device, device ^ distance) for device in range(req_size)]
        )

    def after(value, others):
        return lax.optimization_barrier((value, others))[0]

    half = req_count // 2
    layer = lax.axis_index("wgt")
    per = chips // wgt_size
    tokens = arrivals.reshape(rows, per, block) if per > 1 else arrivals.reshape(rows, width)

    def route(turn):
        pairs = []
        for device in range(req_size):
            for at in range(wgt_size):
                to = device // 2
                origin = turn ^ (at * per + to % per)
                pairs.append(
                    ((2 * origin + device % 2) * wgt_size + to // per, device * wgt_size + at)
                )
        value = tokens
        if per > 1:
            value = lax.dynamic_index_in_dim(tokens, (chip ^ turn) % per, 1, False)
        return lax.ppermute(value, ("req", "wgt"), pairs)

    received = [route(turn) for turn in range(chips)]

    widened = arrivals.reshape(rows, width).astype(jnp.float32)
    middle = jnp.mean(widened, axis=-1)
    square = jnp.sum(jnp.square(widened - middle[:, None]), axis=-1)
    stats = jnp.broadcast_to(jnp.stack([middle, square])[None], (wgt_size, 2, rows))
    stats = lax.all_to_all(stats, "wgt", 0, 0, tiled=True)
    center = jnp.mean(stats[:, 0], axis=0)
    square = jnp.sum(stats[:, 1] + width * jnp.square(stats[:, 0] - center[None]), axis=0)
    scale = lax.rsqrt(square / (width * wgt_size) + EPS)
    stats = jnp.broadcast_to(jnp.stack([center, scale])[None], (req_size, 2, rows))
    stats = lax.all_to_all(stats, "req", 0, 0, tiled=True)
    stats = stats.reshape(chips, 2, 2, req_count, fresh_len).transpose(2, 1, 0, 3, 4)
    stats = jnp.where(core == 0, stats, stats[:, ::-1])
    stats = jnp.broadcast_to(
        stats.reshape(2, everyone, fresh_len)[..., None], (2, everyone, fresh_len, LANES)
    )
    center, scale = stats[0], stats[1]

    ids = jnp.arange(everyone, dtype=jnp.int32)
    same_group = group_of[:, None] == group_of[None, :]
    earlier = ids[None, :] < ids[:, None]
    rank = jnp.sum((same_group & earlier).astype(jnp.int32), axis=1)
    part_of, within = rank // half, rank % half
    wanted = (part_of * req_size + group_of) * half + within
    origin = ids // req_count
    row = (((origin & 1) ^ core) * chips + (origin >> 1)) * req_count + ids % req_count
    sources = jnp.sum(jnp.where(wanted[None, :] == ids[:, None], row[None, :], 0), axis=1)

    lane = np.arange(heads * HEAD) % HEAD
    half_rot = ROT // 2
    inverse = jnp.power(10000.0, -jnp.asarray(lane % half_rot, jnp.float32) * 2.0 / ROT)
    positions = (
        lengths[:, None] + jnp.arange(fresh_len, dtype=jnp.int32)[None, :]
    ).astype(jnp.float32)
    angles = positions.reshape(rows, 1) * inverse[None, :]
    turns = jnp.asarray(lane < ROT)[None, :]
    cosine = jnp.where(turns, jnp.cos(angles), 1.0)
    sine = jnp.sin(angles)
    sine_up = jnp.where(jnp.asarray(lane < half_rot)[None, :], -sine, 0.0)
    sine_down = jnp.where(turns & jnp.asarray(lane >= half_rot)[None, :], sine, 0.0)

    tables = [
        value.reshape(req_count, fresh_len, heads * HEAD)
        for value in (cosine, sine_up, sine_down)
    ]
    gain, shift = (
        lax.dynamic_slice_in_dim(value, chip * block, block).astype(jnp.float32).reshape(1, block)
        for value in (ln_gain, ln_bias)
    )
    bias = qkv_bias.astype(jnp.float32).reshape(1, local_cols)
    place = jnp.stack([core, layer * per + chip % per]).astype(jnp.int32)
    chunk_rows = half * fresh_len
    span = page_table.shape[1]
    pages = span + (half - 1) * (span // 2)

    own_rows = lax.dynamic_slice_in_dim(w_qkv, core * half_cols, half_cols, 1)
    other_rows = swap(lax.dynamic_slice_in_dim(w_qkv, (1 - core) * half_cols, half_cols, 1), 1)

    received += [swap(piece, 1) for piece in received]
    received = [piece.reshape(req_count, fresh_len, block) for piece in received]

    projected = []
    for part in range(2):
        projected.append(
            pl.pallas_call(
                functools.partial(project_kernel, part),
                out_shape=jax.ShapeDtypeStruct((req_size, chunk_rows, half_cols), jnp.bfloat16),
                in_specs=[SMEM] * 2 + [HBM] * req_size + [VMEM] * 4 + [HBM] * 2,
                out_specs=HBM,
                scratch_shapes=[
                    pltpu.VMEM((everyone, fresh_len, block), jnp.bfloat16),
                    pltpu.VMEM((block, half_cols), jnp.bfloat16),
                    pltpu.VMEM((min(req_size, 4) * chunk_rows, block), jnp.bfloat16),
                    pltpu.VMEM((req_size, chunk_rows, half_cols), jnp.bfloat16),
                    pltpu.SemaphoreType.DMA((req_size,)),
                    pltpu.SemaphoreType.DMA((2,)),
                    pltpu.SemaphoreType.DMA((req_size // min(req_size, 4),)),
                ],
                compiler_params=pltpu.CompilerParams(vmem_limit_bytes=VMEM_LIMIT),
                name="project",
            )(place, sources, *received, center, scale, gain, shift, own_rows, other_rows)
        )

    results = []
    for part in range(2):
        parts = lax.all_to_all(projected[part], "req", 0, 0, tiled=True)
        if part == 0:
            parts = after(parts, projected[1])

        operands = [
            lengths, page_table, parts, bias, *tables, key_pool, value_pool
        ]
        specs = [SMEM] * 2 + [VMEM] * 5 + [HBM] * 2
        count = half if part == 0 else req_count
        out = jax.ShapeDtypeStruct((count, fresh_len, heads * HEAD), jnp.bfloat16)
        results = pl.pallas_call(
            functools.partial(
                attend_kernel, (req_size, half, fresh_len, page, heads, part)
            ),
            out_shape=[out] * 3,
            in_specs=specs + [VMEM] * len(results),
            out_specs=[VMEM] * 3,
            scratch_shapes=[
                pltpu.VMEM((pages, page, heads * HEAD), jnp.bfloat16),
                pltpu.VMEM((pages, page, heads * HEAD), jnp.bfloat16),
                pltpu.SemaphoreType.DMA((half,)),
            ],
            compiler_params=pltpu.CompilerParams(vmem_limit_bytes=VMEM_LIMIT),
            name="attend",
        )(*operands, *results)
    return tuple(results)


def solution(mesh):
    in_specs = (
        P("req", None, "wgt"),
        P(),
        P("req"),
        P("req", None),
        P(),
        P(),
        P("req", "wgt"),
        P("wgt"),
        P("req", None, "wgt"),
        P("req", None, "wgt"),
    )
    out_specs = (P("req", None, "wgt"), P("req", None, "wgt"), P("req", None, "wgt"))
    return jax.shard_map(
        functools.partial(per_device, mesh.shape["req"], mesh.shape["wgt"]),
        mesh=mesh,
        in_specs=in_specs,
        out_specs=out_specs,
        check_vma=False,
    )
```

```python
import functools
import math

import jax
import jax.numpy as jnp
import numpy as np
from jax import lax
from jax.experimental import pallas as pl
from jax.experimental.pallas import tpu as pltpu
from jax.sharding import PartitionSpec as P

HEAD = 96
ROT = 24
EPS = 1e-05
LANES = 128
WINDOW = 2 * LANES
CHUNK_PAGES = 4
VMEM_LIMIT = 58 * 1024 * 1024

SMEM = pl.BlockSpec(memory_space=pltpu.SMEM)
VMEM = pl.BlockSpec(memory_space=pltpu.VMEM)
HBM = pl.BlockSpec(memory_space=pltpu.HBM)


def project_kernel(part, place, source, *refs):
    groups = len(refs) - 10
    tokens = refs[:groups]
    own_rows, other_rows = refs[groups : groups + 2]
    out, held, weights, picked, ready, sems, weight_sems, out_sems = refs[groups + 2 :]
    core, begin = place[0], place[1]
    depth = own_rows.shape[0]
    chips = groups // 2
    req_count, fresh_len = tokens[0].shape[:2]
    rows = out.shape[1]
    held_count = rows // fresh_len
    copies = [
        pltpu.make_async_copy(
            token,
            held.at[
                pl.ds((index // chips * chips + (index % chips ^ begin)) * req_count, req_count)
            ],
            sems.at[index],
        )
        for index, token in enumerate(tokens)
    ]
    copies += [
        pltpu.make_async_copy(
            own_rows,
            weights.at[pl.ds(pl.multiple_of(core * depth, 16), depth)],
            weight_sems.at[0],
        ),
        pltpu.make_async_copy(
            other_rows,
            weights.at[pl.ds(pl.multiple_of((1 - core) * depth, 16), depth)],
            weight_sems.at[1],
        ),
    ]
    for copy in copies:
        copy.start()
    for copy in copies:
        copy.wait()
    together = min(groups, 4)
    sent = []
    for first in range(0, groups, together):
        for item in range(together * held_count):
            picked[item * fresh_len : (item + 1) * fresh_len, :] = held[
                source[(part * groups + first) * held_count + item]
            ]
        result = jnp.dot(picked[...], weights[...], preferred_element_type=jnp.float32).astype(
            jnp.bfloat16
        )
        for index in range(together):
            ready[first + index] = result[index * rows : (index + 1) * rows]
        targets = pl.ds(first, together)
        sent.append(
            pltpu.make_async_copy(
                ready.at[targets], out.at[targets], out_sems.at[first // together]
            )
        )
        sent[-1].start()
    for copy in sent:
        copy.wait()


def attend_kernel(shape, all_lengths, table, *refs):
    groups, held_count, fresh_len, page, heads, part = shape
    parts, bias, cosine, sine_up, sine_down, key_pool, value_pool = refs[:7]
    before = refs[7:-6]
    outs = refs[-6:-3]
    keys, values, sems = refs[-3:]
    chunk = CHUNK_PAGES * page
    pairs = heads // 2

    slot = [part * held_count + index for index in range(held_count)]
    lengths = [all_lengths[slot[index]] for index in range(held_count)]
    counts = [pl.cdiv(lengths[index], chunk) for index in range(held_count)]
    bases = [jnp.int32(0)]
    for count in counts[:-1]:
        bases.append(bases[-1] + count * CHUNK_PAGES)

    def copies(index, entry):
        number = table[slot[index], entry]
        to = bases[index] + entry
        return (
            pltpu.make_async_copy(key_pool.at[number], keys.at[to], sems.at[index]),
            pltpu.make_async_copy(value_pool.at[number], values.at[to], sems.at[index]),
        )

    for index in range(held_count):

        def start(entry, carry, index=index):
            for copy in copies(index, entry):
                copy.start()
            return carry

        lax.fori_loop(0, counts[index] * CHUNK_PAGES, start, 0)

    def cached(pages, index, part, pair):
        held = pages[
            pl.ds(bases[index] + part * CHUNK_PAGES, CHUNK_PAGES),
            :,
            starts[pair] : starts[pair] + WINDOW,
        ]
        return held.reshape(chunk, WINDOW)

    halves = [
        sum(parts[index].astype(jnp.float32) for index in range(side, groups, 2))
        for side in range(2)
    ]
    halves = [
        half + bias[:, side * half.shape[1] : (side + 1) * half.shape[1]]
        for side, half in enumerate(halves)
    ]

    def kind(which):
        pieces = []
        for head in range(heads):
            half = halves[head // pairs]
            begin = (head % pairs) * 3 * HEAD + which * HEAD
            pieces.append(half[:, begin : begin + HEAD])
        return jnp.concatenate(pieces, axis=1)

    width = heads * HEAD

    def rows_of(ref):
        return jnp.concatenate([ref[slot[index]] for index in range(held_count)], axis=0)

    cosine, sine_up, sine_down = rows_of(cosine), rows_of(sine_up), rows_of(sine_down)

    def turn(block):
        half_rot = ROT // 2
        return (
            block * cosine
            + pltpu.roll(block, width - half_rot, 1) * sine_up
            + pltpu.roll(block, half_rot, 1) * sine_down
        )

    queries = turn(kind(0)).astype(jnp.bfloat16)
    turned = turn(kind(1)).astype(jnp.bfloat16)
    plain = kind(2).astype(jnp.bfloat16)

    def put(which, index, value):
        outs[which][slot[index] if before else index] = value

    for which, held in enumerate(before):
        for index in range(held_count):
            outs[which][index] = held[index]
    for index in range(held_count):
        rows = slice(index * fresh_len, (index + 1) * fresh_len)
        put(1, index, turned[rows])
        put(2, index, plain[rows])

    factor = 1.0 / math.sqrt(HEAD) / math.log(2.0)
    starts = [(2 * HEAD * pair) // LANES * LANES for pair in range(pairs)]
    lane = lax.broadcasted_iota(jnp.int32, (fresh_len, WINDOW), 1)

    def owned(pair, member):
        begin = (2 * pair + member) * HEAD - starts[pair]
        return (lane >= begin) & (lane < begin + HEAD)

    def contract(left, right):
        return lax.dot_general(
            left, right, (((1,), (1,)), ((), ())), preferred_element_type=jnp.float32
        )

    zero = jnp.zeros((fresh_len, WINDOW), jnp.bfloat16)
    spread_rows = heads * fresh_len
    row = lax.broadcasted_iota(jnp.int32, (2 * fresh_len, fresh_len), 0)
    causal_pair = lax.rem(row, fresh_len) >= lax.broadcasted_iota(
        jnp.int32, (2 * fresh_len, fresh_len), 1
    )
    for index in range(held_count):
        rows = slice(index * fresh_len, (index + 1) * fresh_len)
        spread = []
        for pair in range(pairs):
            window = queries[rows, starts[pair] : starts[pair] + WINDOW]
            spread.append(
                jnp.concatenate(
                    [jnp.where(owned(pair, member), window, zero) for member in range(2)], axis=0
                )
            )
        scores = jnp.concatenate(
            [
                jnp.where(
                    causal_pair,
                    contract(spread[pair], turned[rows, starts[pair] : starts[pair] + WINDOW]),
                    -1e30,
                )
                for pair in range(pairs)
            ],
            axis=0,
        )
        peak = jnp.max(scores, axis=1, keepdims=True)
        weight = jnp.exp2((scores - peak) * factor)
        denom = jnp.sum(weight, axis=1, keepdims=True)
        weight = weight.astype(jnp.bfloat16)
        mixed = jnp.concatenate(
            [
                jnp.dot(
                    weight[pair * 2 * fresh_len : (pair + 1) * 2 * fresh_len],
                    plain[rows, starts[pair] : starts[pair] + WINDOW],
                    preferred_element_type=jnp.float32,
                )
                for pair in range(pairs)
            ],
            axis=0,
        )

        def finish(entry, carry, index=index):
            for copy in copies(index, entry):
                copy.wait()
            return carry

        lax.fori_loop(0, counts[index] * CHUNK_PAGES, finish, 0)

        def step(part, carry, index=index, spread=spread):
            peak, denom, mixed = carry
            scores = jnp.concatenate(
                [
                    contract(spread[pair], cached(keys, index, part, pair))
                    for pair in range(pairs)
                ],
                axis=0,
            )
            position = part * chunk + lax.broadcasted_iota(jnp.int32, (spread_rows, chunk), 1)
            scores = jnp.where(position < lengths[index], scores, -1e30)
            higher = jnp.maximum(peak, jnp.max(scores, axis=1, keepdims=True))
            shrink = jnp.exp2((peak - higher) * factor)
            weight = jnp.exp2((scores - higher) * factor)
            denom = denom * shrink + jnp.sum(weight, axis=1, keepdims=True)
            weight = weight.astype(jnp.bfloat16)
            added = jnp.concatenate(
                [
                    jnp.dot(
                        weight[pair * 2 * fresh_len : (pair + 1) * 2 * fresh_len],
                        cached(values, index, part, pair),
                        preferred_element_type=jnp.float32,
                    )
                    for pair in range(pairs)
                ],
                axis=0,
            )
            return higher, denom, mixed * shrink + added

        peak, denom, mixed = lax.fori_loop(0, counts[index], step, (peak, denom, mixed))
        mixed = mixed / denom
        tiles = [None] * (width // LANES)
        for pair in range(pairs):
            for member in range(2):
                begin = (2 * pair + member) * fresh_len
                part = jnp.where(owned(pair, member), mixed[begin : begin + fresh_len], 0.0)
                for side in range(2):
                    place_at = starts[pair] // LANES + side
                    tile = part[:, side * LANES : (side + 1) * LANES]
                    tiles[place_at] = tile if tiles[place_at] is None else tiles[place_at] + tile
        put(0, index, jnp.concatenate(tiles, axis=1).astype(jnp.bfloat16))


def per_device(
    req_size,
    wgt_size,
    arrivals,
    group_of,
    lengths,
    page_table,
    ln_gain,
    ln_bias,
    w_qkv,
    qkv_bias,
    key_pool,
    value_pool,
):
    req_count, fresh_len, width = arrivals.shape
    rows = req_count * fresh_len
    depth, local_cols = w_qkv.shape
    half_cols = local_cols // 2
    heads = local_cols // (3 * HEAD)
    page = key_pool.shape[1]
    chips = req_size // 2
    block = 2 * depth
    everyone = group_of.shape[0]
    me = lax.axis_index("req")
    layer = lax.axis_index("wgt")
    core = me & 1
    chip = me >> 1

    def swap(value, distance):
        return lax.ppermute(
            value, "req", [(device, device ^ distance) for device in range(req_size)]
        )

    def after(value, others):
        return lax.optimization_barrier((value, others))[0]

    half = req_count // 2
    layer = lax.axis_index("wgt")
    per = chips // wgt_size

    widened = arrivals.reshape(rows, width).astype(jnp.float32)
    middle = jnp.mean(widened, axis=-1)
    square = jnp.sum(jnp.square(widened - middle[:, None]), axis=-1)
    local = jnp.stack([middle, square])
    stats = jnp.broadcast_to(local[None], (wgt_size, 2, rows))
    stats = lax.all_to_all(stats, "wgt", 0, 0, tiled=True)
    center = jnp.mean(stats[:, 0], axis=0)
    square = jnp.sum(stats[:, 1] + width * jnp.square(stats[:, 0] - center[None]), axis=0)
    scale = lax.rsqrt(square / (width * wgt_size) + EPS)
    gain, shift = (
        lax.dynamic_slice_in_dim(value, layer * width, width).astype(jnp.float32)
        for value in (ln_gain, ln_bias)
    )
    tokens = (widened - center[:, None]) * scale[:, None] * gain + shift
    tokens = tokens.astype(jnp.bfloat16)
    if per > 1:
        tokens = tokens.reshape(rows, per, block)

    def route(turn):
        pairs = []
        for device in range(req_size):
            for at in range(wgt_size):
                to = device // 2
                origin = turn ^ (at * per + to % per)
                pairs.append(
                    ((2 * origin + device % 2) * wgt_size + to // per, device * wgt_size + at)
                )
        value = tokens
        if per > 1:
            value = lax.dynamic_index_in_dim(tokens, (chip ^ turn) % per, 1, False)
        return lax.ppermute(value, ("req", "wgt"), pairs)

    received = [route(turn) for turn in range(chips)]

    ids = jnp.arange(everyone, dtype=jnp.int32)
    same_group = group_of[:, None] == group_of[None, :]
    earlier = ids[None, :] < ids[:, None]
    rank = jnp.sum((same_group & earlier).astype(jnp.int32), axis=1)
    part_of, within = rank // half, rank % half
    wanted = (part_of * req_size + group_of) * half + within
    origin = ids // req_count
    row = (((origin & 1) ^ core) * chips + (origin >> 1)) * req_count + ids % req_count
    sources = jnp.sum(jnp.where(wanted[None, :] == ids[:, None], row[None, :], 0), axis=1)

    lane = np.arange(heads * HEAD) % HEAD
    half_rot = ROT // 2
    inverse = jnp.power(10000.0, -jnp.asarray(lane % half_rot, jnp.float32) * 2.0 / ROT)
    positions = (
        lengths[:, None] + jnp.arange(fresh_len, dtype=jnp.int32)[None, :]
    ).astype(jnp.float32)
    angles = positions.reshape(rows, 1) * inverse[None, :]
    turns = jnp.asarray(lane < ROT)[None, :]
    cosine = jnp.where(turns, jnp.cos(angles), 1.0)
    sine = jnp.sin(angles)
    sine_up = jnp.where(jnp.asarray(lane < half_rot)[None, :], -sine, 0.0)
    sine_down = jnp.where(turns & jnp.asarray(lane >= half_rot)[None, :], sine, 0.0)

    tables = [
        value.reshape(req_count, fresh_len, heads * HEAD)
        for value in (cosine, sine_up, sine_down)
    ]
    bias = qkv_bias.astype(jnp.float32).reshape(1, local_cols)
    place = jnp.stack([core, layer * per + chip % per]).astype(jnp.int32)
    chunk_rows = half * fresh_len
    span = page_table.shape[1]
    pages = span + (half - 1) * (span // 2)

    held = after(w_qkv, local)
    own_rows = lax.dynamic_slice_in_dim(held, core * half_cols, half_cols, 1)
    other_rows = swap(lax.dynamic_slice_in_dim(held, (1 - core) * half_cols, half_cols, 1), 1)

    received += [swap(piece, 1) for piece in received]
    received = [piece.reshape(req_count, fresh_len, block) for piece in received]

    projected = []
    for part in range(2):
        projected.append(
            pl.pallas_call(
                functools.partial(project_kernel, part),
                out_shape=jax.ShapeDtypeStruct((req_size, chunk_rows, half_cols), jnp.bfloat16),
                in_specs=[SMEM] * 2 + [HBM] * (req_size + 2),
                out_specs=HBM,
                scratch_shapes=[
                    pltpu.VMEM((everyone, fresh_len, block), jnp.bfloat16),
                    pltpu.VMEM((block, half_cols), jnp.bfloat16),
                    pltpu.VMEM((min(req_size, 4) * chunk_rows, block), jnp.bfloat16),
                    pltpu.VMEM((req_size, chunk_rows, half_cols), jnp.bfloat16),
                    pltpu.SemaphoreType.DMA((req_size,)),
                    pltpu.SemaphoreType.DMA((2,)),
                    pltpu.SemaphoreType.DMA((req_size // min(req_size, 4),)),
                ],
                compiler_params=pltpu.CompilerParams(vmem_limit_bytes=VMEM_LIMIT),
                name="project",
            )(place, sources, *received, own_rows, other_rows)
        )

    results = []
    for part in range(2):
        parts = lax.all_to_all(projected[part], "req", 0, 0, tiled=True)
        if part == 0:
            parts = after(parts, projected[1])

        operands = [
            lengths, page_table, parts, bias, *tables, key_pool, value_pool
        ]
        specs = [SMEM] * 2 + [VMEM] * 5 + [HBM] * 2
        count = half if part == 0 else req_count
        out = jax.ShapeDtypeStruct((count, fresh_len, heads * HEAD), jnp.bfloat16)
        results = pl.pallas_call(
            functools.partial(
                attend_kernel, (req_size, half, fresh_len, page, heads, part)
            ),
            out_shape=[out] * 3,
            in_specs=specs + [VMEM] * len(results),
            out_specs=[VMEM] * 3,
            scratch_shapes=[
                pltpu.VMEM((pages, page, heads * HEAD), jnp.bfloat16),
                pltpu.VMEM((pages, page, heads * HEAD), jnp.bfloat16),
                pltpu.SemaphoreType.DMA((half,)),
            ],
            compiler_params=pltpu.CompilerParams(vmem_limit_bytes=VMEM_LIMIT),
            name="attend",
        )(*operands, *results)
    return tuple(results)


def solution(mesh):
    in_specs = (
        P("req", None, "wgt"),
        P(),
        P("req"),
        P("req", None),
        P(),
        P(),
        P("req", "wgt"),
        P("wgt"),
        P("req", None, "wgt"),
        P("req", None, "wgt"),
    )
    out_specs = (P("req", None, "wgt"), P("req", None, "wgt"), P("req", None, "wgt"))
    return jax.shard_map(
        functools.partial(per_device, mesh.shape["req"], mesh.shape["wgt"]),
        mesh=mesh,
        in_specs=in_specs,
        out_specs=out_specs,
        check_vma=False,
    )
```

```python
import functools
import math

import jax
import jax.numpy as jnp
import numpy as np
from jax import lax
from jax.experimental import pallas as pl
from jax.experimental.pallas import tpu as pltpu
from jax.sharding import PartitionSpec as P

HEAD = 96
ROT = 24
EPS = 1e-05
LANES = 128
WINDOW = 2 * LANES
CHUNK_PAGES = 4
VMEM_LIMIT = 58 * 1024 * 1024

SMEM = pl.BlockSpec(memory_space=pltpu.SMEM)
VMEM = pl.BlockSpec(memory_space=pltpu.VMEM)
HBM = pl.BlockSpec(memory_space=pltpu.HBM)


def project_kernel(part, plan, place, source, *refs):
    groups = sum(len(members) for members, _ in plan)
    tokens = refs[:groups]
    own_rows, other_rows = refs[groups : groups + 2]
    outs = refs[groups + 2 : -5]
    held, weights, picked, sems, weight_sems = refs[-5:]
    core, begin = place[0], place[1]
    depth = own_rows.shape[0]
    chips = groups // 2
    req_count, fresh_len = tokens[0].shape[:2]
    rows = outs[0].shape[1]
    held_count = rows // fresh_len
    copies = [
        pltpu.make_async_copy(
            token,
            held.at[
                pl.ds((index // chips * chips + (index % chips ^ begin)) * req_count, req_count)
            ],
            sems.at[index],
        )
        for index, token in enumerate(tokens)
    ]
    copies += [
        pltpu.make_async_copy(
            own_rows,
            weights.at[pl.ds(pl.multiple_of(core * depth, 16), depth)],
            weight_sems.at[0],
        ),
        pltpu.make_async_copy(
            other_rows,
            weights.at[pl.ds(pl.multiple_of((1 - core) * depth, 16), depth)],
            weight_sems.at[1],
        ),
    ]
    for copy in copies:
        copy.start()
    for copy in copies:
        copy.wait()
    together = min(groups, 4)
    targets = [
        (output, index, target)
        for output, (members, _) in enumerate(plan)
        for index, target in enumerate(members)
    ]
    for first in range(0, groups, together):
        these = targets[first : first + together]
        for count, (_, _, target) in enumerate(these):
            for item in range(held_count):
                at = (count * held_count + item) * fresh_len
                picked[at : at + fresh_len, :] = held[
                    source[(part * groups + target) * held_count + item]
                ]
        result = jnp.dot(picked[...], weights[...], preferred_element_type=jnp.float32)
        for count, (output, index, _) in enumerate(these):
            outs[output][index] = result[count * rows : (count + 1) * rows].astype(
                outs[output].dtype
            )


def attend_kernel(shape, place, all_lengths, table, *refs):
    terms, held_count, fresh_len, page, heads, part = shape
    near, far = refs[: terms[0]], refs[terms[0] : sum(terms)]
    refs = refs[sum(terms) :]
    bias, cosine, sine_up, sine_down, key_pool, value_pool = refs[:6]
    before = refs[6:-6]
    outs = refs[-6:-3]
    keys, values, sems = refs[-3:]
    chunk = CHUNK_PAGES * page
    pairs = heads // 2

    slot = [part * held_count + index for index in range(held_count)]
    lengths = [all_lengths[slot[index]] for index in range(held_count)]
    counts = [pl.cdiv(lengths[index], chunk) for index in range(held_count)]
    bases = [jnp.int32(0)]
    for count in counts[:-1]:
        bases.append(bases[-1] + count * CHUNK_PAGES)

    def copies(index, entry):
        number = table[slot[index], entry]
        to = bases[index] + entry
        return (
            pltpu.make_async_copy(key_pool.at[number], keys.at[to], sems.at[index]),
            pltpu.make_async_copy(value_pool.at[number], values.at[to], sems.at[index]),
        )

    for index in range(held_count):

        def start(entry, carry, index=index):
            for copy in copies(index, entry):
                copy.start()
            return carry

        lax.fori_loop(0, counts[index] * CHUNK_PAGES, start, 0)

    def cached(pages, index, part, pair):
        held = pages[
            pl.ds(bases[index] + part * CHUNK_PAGES, CHUNK_PAGES),
            :,
            starts[pair] : starts[pair] + WINDOW,
        ]
        return held.reshape(chunk, WINDOW)

    near, far = (sum(ref[0].astype(jnp.float32) for ref in refs) for refs in (near, far))
    core = place[0]
    halves = jnp.where(core == 0, near, far), jnp.where(core == 0, far, near)
    halves = [
        half + bias[:, side * half.shape[1] : (side + 1) * half.shape[1]]
        for side, half in enumerate(halves)
    ]

    def kind(which):
        pieces = []
        for head in range(heads):
            half = halves[head // pairs]
            begin = (head % pairs) * 3 * HEAD + which * HEAD
            pieces.append(half[:, begin : begin + HEAD])
        return jnp.concatenate(pieces, axis=1)

    width = heads * HEAD

    def rows_of(ref):
        return jnp.concatenate([ref[slot[index]] for index in range(held_count)], axis=0)

    cosine, sine_up, sine_down = rows_of(cosine), rows_of(sine_up), rows_of(sine_down)

    def turn(block):
        half_rot = ROT // 2
        return (
            block * cosine
            + pltpu.roll(block, width - half_rot, 1) * sine_up
            + pltpu.roll(block, half_rot, 1) * sine_down
        )

    queries = turn(kind(0)).astype(jnp.bfloat16)
    turned = turn(kind(1)).astype(jnp.bfloat16)
    plain = kind(2).astype(jnp.bfloat16)

    def put(which, index, value):
        outs[which][slot[index] if before else index] = value

    for which, held in enumerate(before):
        for index in range(held_count):
            outs[which][index] = held[index]
    for index in range(held_count):
        rows = slice(index * fresh_len, (index + 1) * fresh_len)
        put(1, index, turned[rows])
        put(2, index, plain[rows])

    factor = 1.0 / math.sqrt(HEAD) / math.log(2.0)
    starts = [(2 * HEAD * pair) // LANES * LANES for pair in range(pairs)]
    lane = lax.broadcasted_iota(jnp.int32, (fresh_len, WINDOW), 1)

    def owned(pair, member):
        begin = (2 * pair + member) * HEAD - starts[pair]
        return (lane >= begin) & (lane < begin + HEAD)

    def contract(left, right):
        return lax.dot_general(
            left, right, (((1,), (1,)), ((), ())), preferred_element_type=jnp.float32
        )

    zero = jnp.zeros((fresh_len, WINDOW), jnp.bfloat16)
    spread_rows = heads * fresh_len
    row = lax.broadcasted_iota(jnp.int32, (2 * fresh_len, fresh_len), 0)
    causal_pair = lax.rem(row, fresh_len) >= lax.broadcasted_iota(
        jnp.int32, (2 * fresh_len, fresh_len), 1
    )
    for index in range(held_count):
        rows = slice(index * fresh_len, (index + 1) * fresh_len)
        spread = []
        for pair in range(pairs):
            window = queries[rows, starts[pair] : starts[pair] + WINDOW]
            spread.append(
                jnp.concatenate(
                    [jnp.where(owned(pair, member), window, zero) for member in range(2)], axis=0
                )
            )
        scores = jnp.concatenate(
            [
                jnp.where(
                    causal_pair,
                    contract(spread[pair], turned[rows, starts[pair] : starts[pair] + WINDOW]),
                    -1e30,
                )
                for pair in range(pairs)
            ],
            axis=0,
        )
        peak = jnp.max(scores, axis=1, keepdims=True)
        weight = jnp.exp2((scores - peak) * factor)
        denom = jnp.sum(weight, axis=1, keepdims=True)
        weight = weight.astype(jnp.bfloat16)
        mixed = jnp.concatenate(
            [
                jnp.dot(
                    weight[pair * 2 * fresh_len : (pair + 1) * 2 * fresh_len],
                    plain[rows, starts[pair] : starts[pair] + WINDOW],
                    preferred_element_type=jnp.float32,
                )
                for pair in range(pairs)
            ],
            axis=0,
        )

        def finish(entry, carry, index=index):
            for copy in copies(index, entry):
                copy.wait()
            return carry

        lax.fori_loop(0, counts[index] * CHUNK_PAGES, finish, 0)

        def step(part, carry, index=index, spread=spread):
            peak, denom, mixed = carry
            scores = jnp.concatenate(
                [
                    contract(spread[pair], cached(keys, index, part, pair))
                    for pair in range(pairs)
                ],
                axis=0,
            )
            position = part * chunk + lax.broadcasted_iota(jnp.int32, (spread_rows, chunk), 1)
            scores = jnp.where(position < lengths[index], scores, -1e30)
            higher = jnp.maximum(peak, jnp.max(scores, axis=1, keepdims=True))
            shrink = jnp.exp2((peak - higher) * factor)
            weight = jnp.exp2((scores - higher) * factor)
            denom = denom * shrink + jnp.sum(weight, axis=1, keepdims=True)
            weight = weight.astype(jnp.bfloat16)
            added = jnp.concatenate(
                [
                    jnp.dot(
                        weight[pair * 2 * fresh_len : (pair + 1) * 2 * fresh_len],
                        cached(values, index, part, pair),
                        preferred_element_type=jnp.float32,
                    )
                    for pair in range(pairs)
                ],
                axis=0,
            )
            return higher, denom, mixed * shrink + added

        peak, denom, mixed = lax.fori_loop(0, counts[index], step, (peak, denom, mixed))
        mixed = mixed / denom
        tiles = [None] * (width // LANES)
        for pair in range(pairs):
            for member in range(2):
                begin = (2 * pair + member) * fresh_len
                part = jnp.where(owned(pair, member), mixed[begin : begin + fresh_len], 0.0)
                for side in range(2):
                    place_at = starts[pair] // LANES + side
                    tile = part[:, side * LANES : (side + 1) * LANES]
                    tiles[place_at] = tile if tiles[place_at] is None else tiles[place_at] + tile
        put(0, index, jnp.concatenate(tiles, axis=1).astype(jnp.bfloat16))


def per_device(
    req_size,
    wgt_size,
    arrivals,
    group_of,
    lengths,
    page_table,
    ln_gain,
    ln_bias,
    w_qkv,
    qkv_bias,
    key_pool,
    value_pool,
):
    req_count, fresh_len, width = arrivals.shape
    rows = req_count * fresh_len
    depth, local_cols = w_qkv.shape
    half_cols = local_cols // 2
    heads = local_cols // (3 * HEAD)
    page = key_pool.shape[1]
    chips = req_size // 2
    block = 2 * depth
    everyone = group_of.shape[0]
    me = lax.axis_index("req")
    layer = lax.axis_index("wgt")
    core = me & 1
    chip = me >> 1

    def swap(value, distance):
        return lax.ppermute(
            value, "req", [(device, device ^ distance) for device in range(req_size)]
        )

    def after(value, others):
        return lax.optimization_barrier((value, others))[0]

    half = req_count // 2
    layer = lax.axis_index("wgt")
    per = chips // wgt_size

    widened = arrivals.reshape(rows, width).astype(jnp.float32)
    middle = jnp.mean(widened, axis=-1)
    square = jnp.sum(jnp.square(widened - middle[:, None]), axis=-1)
    local = jnp.stack([middle, square])
    stats = jnp.broadcast_to(local[None], (wgt_size, 2, rows))
    stats = lax.all_to_all(stats, "wgt", 0, 0, tiled=True)
    center = jnp.mean(stats[:, 0], axis=0)
    square = jnp.sum(stats[:, 1] + width * jnp.square(stats[:, 0] - center[None]), axis=0)
    scale = lax.rsqrt(square / (width * wgt_size) + EPS)
    gain, shift = (
        lax.dynamic_slice_in_dim(value, layer * width, width).astype(jnp.float32)
        for value in (ln_gain, ln_bias)
    )
    tokens = (widened - center[:, None]) * scale[:, None] * gain + shift
    tokens = tokens.astype(jnp.bfloat16)
    if per > 1:
        tokens = tokens.reshape(rows, per, block)

    def route(turn):
        pairs = []
        for device in range(req_size):
            for at in range(wgt_size):
                to = device // 2
                origin = turn ^ (at * per + to % per)
                pairs.append(
                    ((2 * origin + device % 2) * wgt_size + to // per, device * wgt_size + at)
                )
        value = tokens
        if per > 1:
            value = lax.dynamic_index_in_dim(tokens, (chip ^ turn) % per, 1, False)
        return lax.ppermute(value, ("req", "wgt"), pairs)

    received = [route(turn) for turn in range(chips)]

    ids = jnp.arange(everyone, dtype=jnp.int32)
    same_group = group_of[:, None] == group_of[None, :]
    earlier = ids[None, :] < ids[:, None]
    rank = jnp.sum((same_group & earlier).astype(jnp.int32), axis=1)
    part_of, within = rank // half, rank % half
    wanted = (part_of * req_size + (group_of ^ me)) * half + within
    origin = ids // req_count
    row = (((origin & 1) ^ core) * chips + (origin >> 1)) * req_count + ids % req_count
    sources = jnp.sum(jnp.where(wanted[None, :] == ids[:, None], row[None, :], 0), axis=1)

    lane = np.arange(heads * HEAD) % HEAD
    half_rot = ROT // 2
    inverse = jnp.power(10000.0, -jnp.asarray(lane % half_rot, jnp.float32) * 2.0 / ROT)
    positions = (
        lengths[:, None] + jnp.arange(fresh_len, dtype=jnp.int32)[None, :]
    ).astype(jnp.float32)
    angles = positions.reshape(rows, 1) * inverse[None, :]
    turns = jnp.asarray(lane < ROT)[None, :]
    cosine = jnp.where(turns, jnp.cos(angles), 1.0)
    sine = jnp.sin(angles)
    sine_up = jnp.where(jnp.asarray(lane < half_rot)[None, :], -sine, 0.0)
    sine_down = jnp.where(turns & jnp.asarray(lane >= half_rot)[None, :], sine, 0.0)

    tables = [
        value.reshape(req_count, fresh_len, heads * HEAD)
        for value in (cosine, sine_up, sine_down)
    ]
    bias = qkv_bias.astype(jnp.float32).reshape(1, local_cols)
    place = jnp.stack([core, layer * per + chip % per]).astype(jnp.int32)
    chunk_rows = half * fresh_len
    span = page_table.shape[1]
    pages = span + (half - 1) * (span // 2)

    held = after(w_qkv, local)
    own_rows = lax.dynamic_slice_in_dim(held, core * half_cols, half_cols, 1)
    other_rows = swap(lax.dynamic_slice_in_dim(held, (1 - core) * half_cols, half_cols, 1), 1)

    received += [swap(piece, 1) for piece in received]
    received = [piece.reshape(req_count, fresh_len, block) for piece in received]

    square_plane = chips == 4
    if square_plane:
        plan = [([2, 6], jnp.bfloat16), ([5, 7], jnp.bfloat16)]
        plan += [([distance], jnp.float32) for distance in (0, 4, 1, 3)]
    else:
        plan = [([0], jnp.float32)]
        plan += [([distance], jnp.bfloat16) for distance in range(1, req_size)]

    def collect(blocks):
        if not square_plane:
            sums = [blocks[0]]
            sums += [swap(block, distance) for distance, block in enumerate(blocks[1:], 1)]
            return sums[::2], sums[1::2]
        along_x, along_y = swap(blocks[0], 2), swap(blocks[1], 4)
        own, own_y, other, other_x = blocks[2:]
        behind_y = swap((own_y + along_x[1:]).astype(jnp.bfloat16), 4)
        behind_x = swap((other_x + along_y[1:]).astype(jnp.bfloat16), 2)
        return [own, along_x, behind_y], [swap(other + along_y[:1], 1), swap(behind_x, 1)]

    projected = []
    for part in range(2):
        projected.append(
            pl.pallas_call(
                functools.partial(project_kernel, part, plan),
                out_shape=[
                    jax.ShapeDtypeStruct((len(members), chunk_rows, half_cols), kind)
                    for members, kind in plan
                ],
                in_specs=[SMEM] * 2 + [HBM] * (req_size + 2),
                out_specs=[VMEM] * len(plan),
                scratch_shapes=[
                    pltpu.VMEM((everyone, fresh_len, block), jnp.bfloat16),
                    pltpu.VMEM((block, half_cols), jnp.bfloat16),
                    pltpu.VMEM((min(req_size, 4) * chunk_rows, block), jnp.bfloat16),
                    pltpu.SemaphoreType.DMA((req_size,)),
                    pltpu.SemaphoreType.DMA((2,)),
                ],
                compiler_params=pltpu.CompilerParams(vmem_limit_bytes=VMEM_LIMIT),
                name="project",
            )(place, sources, *received, own_rows, other_rows)
        )

    results = []
    for part in range(2):
        near, far = collect(projected[part])
        operands = [
            place, lengths, page_table, *near, *far, bias, *tables, key_pool, value_pool
        ]
        terms = len(near), len(far)
        specs = [SMEM] * 3 + [VMEM] * (sum(terms) + 4) + [HBM] * 2
        count = half if part == 0 else req_count
        out = jax.ShapeDtypeStruct((count, fresh_len, heads * HEAD), jnp.bfloat16)
        results = pl.pallas_call(
            functools.partial(
                attend_kernel, (terms, half, fresh_len, page, heads, part)
            ),
            out_shape=[out] * 3,
            in_specs=specs + [VMEM] * len(results),
            out_specs=[VMEM] * 3,
            scratch_shapes=[
                pltpu.VMEM((pages, page, heads * HEAD), jnp.bfloat16),
                pltpu.VMEM((pages, page, heads * HEAD), jnp.bfloat16),
                pltpu.SemaphoreType.DMA((half,)),
            ],
            compiler_params=pltpu.CompilerParams(vmem_limit_bytes=VMEM_LIMIT),
            name="attend",
        )(*operands, *results)
    return tuple(results)


def solution(mesh):
    in_specs = (
        P("req", None, "wgt"),
        P(),
        P("req"),
        P("req", None),
        P(),
        P(),
        P("req", "wgt"),
        P("wgt"),
        P("req", None, "wgt"),
        P("req", None, "wgt"),
    )
    out_specs = (P("req", None, "wgt"), P("req", None, "wgt"), P("req", None, "wgt"))
    return jax.shard_map(
        functools.partial(per_device, mesh.shape["req"], mesh.shape["wgt"]),
        mesh=mesh,
        in_specs=in_specs,
        out_specs=out_specs,
        check_vma=False,
    )
```

```python
import functools
import math

import jax
import jax.numpy as jnp
import numpy as np
from jax import lax
from jax.experimental import pallas as pl
from jax.experimental.pallas import tpu as pltpu
from jax.sharding import PartitionSpec as P

HEAD = 96
ROT = 24
EPS = 1e-05
LANES = 128
WINDOW = 2 * LANES
CHUNK_PAGES = 4
VMEM_LIMIT = 58 * 1024 * 1024

SMEM = pl.BlockSpec(memory_space=pltpu.SMEM)
VMEM = pl.BlockSpec(memory_space=pltpu.VMEM)
HBM = pl.BlockSpec(memory_space=pltpu.HBM)


def project_kernel(part, plan, place, position, *refs):
    groups = sum(len(members) for members, _ in plan)
    tokens = refs[:groups]
    own_rows, other_rows = refs[groups : groups + 2]
    outs = refs[groups + 2 : -4]
    weights, picked, sems, weight_sems = refs[-4:]
    core, begin = place[0], place[1]
    depth = own_rows.shape[0]
    chips = groups // 2
    req_count, fresh_len, width = tokens[0].shape
    half_cols = weights.shape[1]
    rows = outs[0].shape[1]
    held_count = rows // fresh_len

    def columns(ref):
        if ref.shape[1] == half_cols:
            return ref
        return ref.at[:, pl.ds(pl.multiple_of(core * half_cols, LANES), half_cols)]

    copies = [
        pltpu.make_async_copy(
            columns(own_rows),
            weights.at[pl.ds(pl.multiple_of(core * depth, 16), depth)],
            weight_sems.at[0],
        ),
        pltpu.make_async_copy(
            columns(other_rows),
            weights.at[pl.ds(pl.multiple_of((1 - core) * depth, 16), depth)],
            weight_sems.at[1],
        ),
    ]
    fetches = []
    for index, token in enumerate(tokens):
        row = (index // chips * chips + (index % chips ^ begin)) * req_count
        for item in range(req_count):
            to = position[row + item] - part * groups * held_count
            mine = (to >= 0) & (to < groups * held_count)
            to = jnp.where(mine, to, 0)
            fetches.append(
                (
                    mine,
                    pltpu.make_async_copy(
                        token.at[item], picked.at[to], sems.at[index * req_count + item]
                    ),
                )
            )
    for mine, fetch in fetches:

        @pl.when(mine)
        def _():
            fetch.start()

    for copy in copies:
        copy.start()
    for mine, fetch in fetches:

        @pl.when(mine)
        def _():
            fetch.wait()

    for copy in copies:
        copy.wait()
    together = min(groups, 4)
    targets = [
        (output, index) for output, (members, _) in enumerate(plan) for index in range(len(members))
    ]
    for first in range(0, groups, together):
        these = targets[first : first + together]
        value = picked[first * held_count : (first + together) * held_count]
        result = jnp.dot(
            value.reshape(together * rows, width),
            weights[...],
            preferred_element_type=jnp.float32,
        )
        for count, (output, index) in enumerate(these):
            outs[output][index] = result[count * rows : (count + 1) * rows].astype(
                outs[output].dtype
            )


def attend_kernel(shape, place, all_lengths, table, *refs):
    terms, held_count, fresh_len, page, heads = shape
    sums = []
    for count in terms:
        sums.append(sum(ref[0].astype(jnp.float32) for ref in refs[:count]))
        refs = refs[count:]
    bias, cosine, sine_up, sine_down, key_pool, value_pool, *outs = refs[:-3]
    keys, values, sems = refs[-3:]
    chunk = CHUNK_PAGES * page
    pairs = heads // 2

    lengths = [all_lengths[index] for index in range(held_count)]
    counts = [pl.cdiv(lengths[index], chunk) for index in range(held_count)]
    bases = [jnp.int32(0)]
    for count in counts[:-1]:
        bases.append(bases[-1] + count * CHUNK_PAGES)

    def copies(index, entry):
        number = table[index, entry]
        to = bases[index] + entry
        return (
            pltpu.make_async_copy(key_pool.at[number], keys.at[to], sems.at[index]),
            pltpu.make_async_copy(value_pool.at[number], values.at[to], sems.at[index]),
        )

    for index in range(held_count):

        def start(entry, carry, index=index):
            for copy in copies(index, entry):
                copy.start()
            return carry

        lax.fori_loop(0, counts[index] * CHUNK_PAGES, start, 0)

    def cached(pages, index, part, pair):
        held = pages[
            pl.ds(bases[index] + part * CHUNK_PAGES, CHUNK_PAGES),
            :,
            starts[pair] : starts[pair] + WINDOW,
        ]
        return held.reshape(chunk, WINDOW)

    near = jnp.concatenate(sums[::2], axis=0)
    far = jnp.concatenate(sums[1::2], axis=0)
    core = place[0]
    halves = jnp.where(core == 0, near, far), jnp.where(core == 0, far, near)
    halves = [
        half + bias[:, side * half.shape[1] : (side + 1) * half.shape[1]]
        for side, half in enumerate(halves)
    ]

    def kind(which):
        pieces = []
        for head in range(heads):
            half = halves[head // pairs]
            begin = (head % pairs) * 3 * HEAD + which * HEAD
            pieces.append(half[:, begin : begin + HEAD])
        return jnp.concatenate(pieces, axis=1)

    width = heads * HEAD

    def rows_of(ref):
        return ref[...].reshape(held_count * fresh_len, width)

    cosine, sine_up, sine_down = rows_of(cosine), rows_of(sine_up), rows_of(sine_down)

    def turn(block):
        half_rot = ROT // 2
        return (
            block * cosine
            + pltpu.roll(block, width - half_rot, 1) * sine_up
            + pltpu.roll(block, half_rot, 1) * sine_down
        )

    queries = turn(kind(0)).astype(jnp.bfloat16)
    turned = turn(kind(1)).astype(jnp.bfloat16)
    plain = kind(2).astype(jnp.bfloat16)

    for index in range(held_count):
        rows = slice(index * fresh_len, (index + 1) * fresh_len)
        outs[1][index] = turned[rows]
        outs[2][index] = plain[rows]

    factor = 1.0 / math.sqrt(HEAD) / math.log(2.0)
    starts = [(2 * HEAD * pair) // LANES * LANES for pair in range(pairs)]
    lane = lax.broadcasted_iota(jnp.int32, (fresh_len, WINDOW), 1)

    def owned(pair, member):
        begin = (2 * pair + member) * HEAD - starts[pair]
        return (lane >= begin) & (lane < begin + HEAD)

    def contract(left, right):
        return lax.dot_general(
            left, right, (((1,), (1,)), ((), ())), preferred_element_type=jnp.float32
        )

    zero = jnp.zeros((fresh_len, WINDOW), jnp.bfloat16)
    spread_rows = heads * fresh_len
    row = lax.broadcasted_iota(jnp.int32, (2 * fresh_len, fresh_len), 0)
    causal_pair = lax.rem(row, fresh_len) >= lax.broadcasted_iota(
        jnp.int32, (2 * fresh_len, fresh_len), 1
    )
    for index in range(held_count):
        rows = slice(index * fresh_len, (index + 1) * fresh_len)
        spread = []
        for pair in range(pairs):
            window = queries[rows, starts[pair] : starts[pair] + WINDOW]
            spread.append(
                jnp.concatenate(
                    [jnp.where(owned(pair, member), window, zero) for member in range(2)], axis=0
                )
            )
        scores = jnp.concatenate(
            [
                jnp.where(
                    causal_pair,
                    contract(spread[pair], turned[rows, starts[pair] : starts[pair] + WINDOW]),
                    -1e30,
                )
                for pair in range(pairs)
            ],
            axis=0,
        )
        peak = jnp.max(scores, axis=1, keepdims=True)
        weight = jnp.exp2((scores - peak) * factor)
        denom = jnp.sum(weight, axis=1, keepdims=True)
        weight = weight.astype(jnp.bfloat16)
        mixed = jnp.concatenate(
            [
                jnp.dot(
                    weight[pair * 2 * fresh_len : (pair + 1) * 2 * fresh_len],
                    plain[rows, starts[pair] : starts[pair] + WINDOW],
                    preferred_element_type=jnp.float32,
                )
                for pair in range(pairs)
            ],
            axis=0,
        )

        def finish(entry, carry, index=index):
            for copy in copies(index, entry):
                copy.wait()
            return carry

        lax.fori_loop(0, counts[index] * CHUNK_PAGES, finish, 0)

        def step(part, carry, index=index, spread=spread):
            peak, denom, mixed = carry
            scores = jnp.concatenate(
                [
                    contract(spread[pair], cached(keys, index, part, pair))
                    for pair in range(pairs)
                ],
                axis=0,
            )
            position = part * chunk + lax.broadcasted_iota(jnp.int32, (spread_rows, chunk), 1)
            scores = jnp.where(position < lengths[index], scores, -1e30)
            higher = jnp.maximum(peak, jnp.max(scores, axis=1, keepdims=True))
            shrink = jnp.exp2((peak - higher) * factor)
            weight = jnp.exp2((scores - higher) * factor)
            denom = denom * shrink + jnp.sum(weight, axis=1, keepdims=True)
            weight = weight.astype(jnp.bfloat16)
            added = jnp.concatenate(
                [
                    jnp.dot(
                        weight[pair * 2 * fresh_len : (pair + 1) * 2 * fresh_len],
                        cached(values, index, part, pair),
                        preferred_element_type=jnp.float32,
                    )
                    for pair in range(pairs)
                ],
                axis=0,
            )
            return higher, denom, mixed * shrink + added

        peak, denom, mixed = lax.fori_loop(0, counts[index], step, (peak, denom, mixed))
        mixed = mixed / denom
        tiles = [None] * (width // LANES)
        for pair in range(pairs):
            for member in range(2):
                begin = (2 * pair + member) * fresh_len
                part = jnp.where(owned(pair, member), mixed[begin : begin + fresh_len], 0.0)
                for side in range(2):
                    place_at = starts[pair] // LANES + side
                    tile = part[:, side * LANES : (side + 1) * LANES]
                    tiles[place_at] = tile if tiles[place_at] is None else tiles[place_at] + tile
        outs[0][index] = jnp.concatenate(tiles, axis=1).astype(jnp.bfloat16)


def per_device(
    req_size,
    wgt_size,
    arrivals,
    group_of,
    lengths,
    page_table,
    ln_gain,
    ln_bias,
    w_qkv,
    qkv_bias,
    key_pool,
    value_pool,
):
    req_count, fresh_len, width = arrivals.shape
    rows = req_count * fresh_len
    depth, local_cols = w_qkv.shape
    half_cols = local_cols // 2
    heads = local_cols // (3 * HEAD)
    page = key_pool.shape[1]
    chips = req_size // 2
    block = 2 * depth
    everyone = group_of.shape[0]
    me = lax.axis_index("req")
    layer = lax.axis_index("wgt")
    core = me & 1
    chip = me >> 1

    def swap(value, distance):
        return lax.ppermute(
            value, "req", [(device, device ^ distance) for device in range(req_size)]
        )

    def after(value, others):
        return lax.optimization_barrier((value, others))[0]

    half = req_count // 2
    layer = lax.axis_index("wgt")
    per = chips // wgt_size

    widened = arrivals.reshape(rows, width).astype(jnp.float32)
    middle = jnp.mean(widened, axis=-1)
    square = jnp.sum(jnp.square(widened - middle[:, None]), axis=-1)
    local = jnp.stack([middle, square])
    stats = jnp.broadcast_to(local[None], (wgt_size, 2, rows))
    stats = lax.all_to_all(stats, "wgt", 0, 0, tiled=True)
    center = jnp.mean(stats[:, 0], axis=0)
    square = jnp.sum(stats[:, 1] + width * jnp.square(stats[:, 0] - center[None]), axis=0)
    scale = lax.rsqrt(square / (width * wgt_size) + EPS)
    gain, shift = (
        lax.dynamic_slice_in_dim(value, layer * width, width).astype(jnp.float32)
        for value in (ln_gain, ln_bias)
    )
    tokens = (widened - center[:, None]) * scale[:, None] * gain + shift
    tokens = tokens.astype(jnp.bfloat16)
    if per > 1:
        tokens = tokens.reshape(rows, per, block)

    def route(turn):
        pairs = []
        for device in range(req_size):
            for at in range(wgt_size):
                to = device // 2
                origin = turn ^ (at * per + to % per)
                pairs.append(
                    ((2 * origin + device % 2) * wgt_size + to // per, device * wgt_size + at)
                )
        value = tokens
        if per > 1:
            value = lax.dynamic_index_in_dim(tokens, (chip ^ turn) % per, 1, False)
        return lax.ppermute(value, ("req", "wgt"), pairs)

    received = [route(turn) for turn in range(chips)]

    square_plane = chips == 4
    if square_plane:
        plan = [([2, 6], jnp.bfloat16), ([5, 7], jnp.bfloat16)]
        plan += [([distance], jnp.float32) for distance in (0, 4, 1, 3)]
    else:
        plan = [([0], jnp.float32)]
        plan += [([distance], jnp.bfloat16) for distance in range(1, req_size)]

    ids = jnp.arange(everyone, dtype=jnp.int32)
    same_group = group_of[:, None] == group_of[None, :]
    earlier = ids[None, :] < ids[:, None]
    rank = jnp.sum((same_group & earlier).astype(jnp.int32), axis=1)
    part_of, within = rank // half, rank % half
    place_of = np.zeros(req_size, np.int32)
    place_of[[target for members, _ in plan for target in members]] = np.arange(req_size)
    place_of = jnp.asarray(place_of)[group_of ^ me]
    spot = (part_of * req_size + place_of) * half + within
    origin = ids // req_count
    row = (((origin & 1) ^ core) * chips + (origin >> 1)) * req_count + ids % req_count
    position = jnp.sum(jnp.where(row[None, :] == ids[:, None], spot[None, :], 0), axis=1)

    lane = np.arange(heads * HEAD) % HEAD
    half_rot = ROT // 2
    inverse = jnp.power(10000.0, -jnp.asarray(lane % half_rot, jnp.float32) * 2.0 / ROT)
    positions = (
        lengths[:, None] + jnp.arange(fresh_len, dtype=jnp.int32)[None, :]
    ).astype(jnp.float32)
    angles = positions.reshape(rows, 1) * inverse[None, :]
    turns = jnp.asarray(lane < ROT)[None, :]
    cosine = jnp.where(turns, jnp.cos(angles), 1.0)
    sine = jnp.sin(angles)
    sine_up = jnp.where(jnp.asarray(lane < half_rot)[None, :], -sine, 0.0)
    sine_down = jnp.where(turns & jnp.asarray(lane >= half_rot)[None, :], sine, 0.0)

    tables = [
        value.reshape(req_count, fresh_len, heads * HEAD)
        for value in (cosine, sine_up, sine_down)
    ]
    bias = qkv_bias.astype(jnp.float32).reshape(1, local_cols)
    place = jnp.stack([core, layer * per + chip % per]).astype(jnp.int32)
    chunk_rows = half * fresh_len
    span = page_table.shape[1]
    pages = span + (req_count - 1) * (span // 2)

    if half_cols % LANES == 0:
        own_rows, other_rows = w_qkv, swap(after(w_qkv, scale), 1)
    else:
        own_rows = lax.dynamic_slice_in_dim(w_qkv, core * half_cols, half_cols, 1)
        other_rows = lax.dynamic_slice_in_dim(w_qkv, (1 - core) * half_cols, half_cols, 1)
        other_rows = swap(other_rows, 1)

    received += [swap(piece, 1) for piece in received]
    received = [piece.reshape(req_count, fresh_len, block) for piece in received]
    received[0] = after(received[0], tables)

    def collect(blocks):
        if not square_plane:
            sums = [blocks[0]]
            sums += [swap(block, distance) for distance, block in enumerate(blocks[1:], 1)]
            return sums[::2], sums[1::2]
        along_x, along_y = swap(blocks[0], 2), swap(blocks[1], 4)
        own, own_y, other, other_x = blocks[2:]
        behind_y = swap((own_y + along_x[1:]).astype(jnp.bfloat16), 4)
        behind_x = swap((other_x + along_y[1:]).astype(jnp.bfloat16), 2)
        return [own, along_x, behind_y], [swap(other + along_y[:1], 1), swap(behind_x, 1)]

    projected = []
    for part in range(2):
        projected.append(
            pl.pallas_call(
                functools.partial(project_kernel, part, plan),
                out_shape=[
                    jax.ShapeDtypeStruct((len(members), chunk_rows, half_cols), kind)
                    for members, kind in plan
                ],
                in_specs=[SMEM] * 2 + [HBM] * (req_size + 2),
                out_specs=[VMEM] * len(plan),
                scratch_shapes=[
                    pltpu.VMEM((block, half_cols), jnp.bfloat16),
                    pltpu.VMEM((req_size * half, fresh_len, block), jnp.bfloat16),
                    pltpu.SemaphoreType.DMA((everyone,)),
                    pltpu.SemaphoreType.DMA((2,)),
                ],
                compiler_params=pltpu.CompilerParams(vmem_limit_bytes=VMEM_LIMIT),
                name="project",
            )(place, position, *received, own_rows, other_rows)
        )

    terms, sums = [], []
    for blocks in projected:
        for side in collect(blocks):
            terms.append(len(side))
            sums += side
    out = jax.ShapeDtypeStruct((req_count, fresh_len, heads * HEAD), jnp.bfloat16)
    return tuple(
        pl.pallas_call(
            functools.partial(attend_kernel, (terms, req_count, fresh_len, page, heads)),
            out_shape=[out] * 3,
            in_specs=[SMEM] * 3 + [VMEM] * (len(sums) + 4) + [HBM] * 2,
            out_specs=[VMEM] * 3,
            scratch_shapes=[
                pltpu.VMEM((pages, page, heads * HEAD), jnp.bfloat16),
                pltpu.VMEM((pages, page, heads * HEAD), jnp.bfloat16),
                pltpu.SemaphoreType.DMA((req_count,)),
            ],
            compiler_params=pltpu.CompilerParams(vmem_limit_bytes=VMEM_LIMIT),
            name="attend",
        )(place, lengths, page_table, *sums, bias, *tables, key_pool, value_pool)
    )


def solution(mesh):
    in_specs = (
        P("req", None, "wgt"),
        P(),
        P("req"),
        P("req", None),
        P(),
        P(),
        P("req", "wgt"),
        P("wgt"),
        P("req", None, "wgt"),
        P("req", None, "wgt"),
    )
    out_specs = (P("req", None, "wgt"), P("req", None, "wgt"), P("req", None, "wgt"))
    return jax.shard_map(
        functools.partial(per_device, mesh.shape["req"], mesh.shape["wgt"]),
        mesh=mesh,
        in_specs=in_specs,
        out_specs=out_specs,
        check_vma=False,
    )
```

```python
import functools
import math

import jax
import jax.numpy as jnp
import numpy as np
from jax import lax
from jax.experimental import pallas as pl
from jax.experimental.pallas import tpu as pltpu
from jax.sharding import PartitionSpec as P

HEAD = 96
ROT = 24
EPS = 1e-05
LANES = 128
WINDOW = 2 * LANES
CHUNK_PAGES = 4
VMEM_LIMIT = 58 * 1024 * 1024

SMEM = pl.BlockSpec(memory_space=pltpu.SMEM)
VMEM = pl.BlockSpec(memory_space=pltpu.VMEM)
HBM = pl.BlockSpec(memory_space=pltpu.HBM)


def measure_kernel(arrivals, out):
    requests, fresh_len, width = arrivals.shape
    lane = lax.broadcasted_iota(jnp.int32, (fresh_len, LANES), 1)
    for index in range(requests):
        value = arrivals[index].astype(jnp.float32)
        center = jnp.sum(value, axis=-1, keepdims=True) / width
        square = jnp.sum(jnp.square(value - center), axis=-1, keepdims=True)
        packed = jnp.where(lane == 0, center, jnp.where(lane == 1, square, 0.0))
        for layer in range(out.shape[0]):
            out[layer, index] = packed


def norm_kernel(arrivals, stats, gain, bias, out):
    requests, _, width = arrivals.shape
    depth = stats.shape[0]
    for index in range(requests):
        pairs = [stats[layer, index] for layer in range(depth)]
        center = sum(pair[:, 0:1] for pair in pairs) / depth
        square = sum(pair[:, 1:2] + width * jnp.square(pair[:, 0:1] - center) for pair in pairs)
        scale = lax.rsqrt(square / (depth * width) + EPS)
        value = (arrivals[index].astype(jnp.float32) - center) * scale
        out[index] = (value * gain[...] + bias[...]).astype(jnp.bfloat16)


def project_kernel(part, plan, place, position, *refs):
    groups = sum(len(members) for members, _ in plan)
    tokens = refs[:groups]
    own_rows, other_rows = refs[groups : groups + 2]
    outs = refs[groups + 2 : groups + 2 + len(plan)]
    weights, picked, sems, weight_sems, out_sems, *ready = refs[groups + 2 + len(plan) :]
    stores = []
    core, begin = place[0], place[1]
    depth = own_rows.shape[0]
    chips = groups // 2
    req_count, fresh_len, width = tokens[0].shape
    half_cols = weights.shape[1]
    rows = outs[0].shape[1]
    held_count = rows // fresh_len

    def columns(ref):
        if ref.shape[1] == half_cols:
            return ref
        return ref.at[:, pl.ds(pl.multiple_of(core * half_cols, LANES), half_cols)]

    copies = [
        pltpu.make_async_copy(
            columns(own_rows),
            weights.at[pl.ds(pl.multiple_of(core * depth, 16), depth)],
            weight_sems.at[0],
        ),
        pltpu.make_async_copy(
            columns(other_rows),
            weights.at[pl.ds(pl.multiple_of((1 - core) * depth, 16), depth)],
            weight_sems.at[1],
        ),
    ]
    for index, token in enumerate(tokens):
        row = (index // chips * chips + (index % chips ^ begin)) * req_count
        for item in range(req_count):
            to = position[row + item] - part * groups * held_count

            @pl.when((to >= 0) & (to < groups * held_count))
            def _(token=token, item=item, to=to):
                pltpu.make_async_copy(token.at[item], picked.at[to], sems.at[to]).start()

    for copy in copies:
        copy.start()
    together = min(groups, 4)
    targets = [
        (output, index) for output, (members, _) in enumerate(plan) for index in range(len(members))
    ]
    for first in range(0, groups, together):
        these = targets[first : first + together]
        for at in range(first * held_count, (first + together) * held_count):
            pltpu.make_async_copy(tokens[0].at[0], picked.at[at], sems.at[at]).wait()
        if first == 0:
            for copy in copies:
                copy.wait()
        value = picked[first * held_count : (first + together) * held_count]
        result = jnp.dot(
            value.reshape(together * rows, width),
            weights[...],
            preferred_element_type=jnp.float32,
        )
        for count, (output, index) in enumerate(these):
            ready[output][index] = result[count * rows : (count + 1) * rows].astype(
                ready[output].dtype
            )
            stores.append(
                pltpu.make_async_copy(
                    ready[output].at[index],
                    outs[output].at[index],
                    out_sems.at[first + count],
                )
            )
            stores[-1].start()
    for store in stores:
        store.wait()


def attend_kernel(shape, place, all_lengths, table, *refs):
    terms, held_count, fresh_len, page, heads = shape
    sums = []
    for count in terms:
        sums.append(sum(ref[0].astype(jnp.float32) for ref in refs[:count]))
        refs = refs[count:]
    bias, cosine, sine_up, sine_down, key_pool, value_pool, *outs = refs[:-3]
    keys, values, sems = refs[-3:]
    chunk = CHUNK_PAGES * page
    pairs = heads // 2

    lengths = [all_lengths[index] for index in range(held_count)]
    counts = [pl.cdiv(lengths[index], chunk) for index in range(held_count)]
    bases = [jnp.int32(0)]
    for count in counts[:-1]:
        bases.append(bases[-1] + count * CHUNK_PAGES)

    def copies(index, entry):
        number = table[index, entry]
        to = bases[index] + entry
        return (
            pltpu.make_async_copy(key_pool.at[number], keys.at[to], sems.at[index]),
            pltpu.make_async_copy(value_pool.at[number], values.at[to], sems.at[index]),
        )

    for index in range(held_count):

        def start(entry, carry, index=index):
            for copy in copies(index, entry):
                copy.start()
            return carry

        lax.fori_loop(0, counts[index] * CHUNK_PAGES, start, 0)

    def cached(pages, index, part, pair):
        held = pages[
            pl.ds(bases[index] + part * CHUNK_PAGES, CHUNK_PAGES),
            :,
            starts[pair] : starts[pair] + WINDOW,
        ]
        return held.reshape(chunk, WINDOW)

    near = jnp.concatenate(sums[::2], axis=0)
    far = jnp.concatenate(sums[1::2], axis=0)
    core = place[0]
    halves = jnp.where(core == 0, near, far), jnp.where(core == 0, far, near)
    halves = [
        half + bias[:, side * half.shape[1] : (side + 1) * half.shape[1]]
        for side, half in enumerate(halves)
    ]

    def kind(which):
        pieces = []
        for head in range(heads):
            half = halves[head // pairs]
            begin = (head % pairs) * 3 * HEAD + which * HEAD
            pieces.append(half[:, begin : begin + HEAD])
        return jnp.concatenate(pieces, axis=1)

    width = heads * HEAD

    def rows_of(ref):
        table = ref[...].reshape(held_count * fresh_len, HEAD)
        return jnp.concatenate([table] * heads, axis=1)

    cosine, sine_up, sine_down = rows_of(cosine), rows_of(sine_up), rows_of(sine_down)

    def turn(block):
        half_rot = ROT // 2
        return (
            block * cosine
            + pltpu.roll(block, width - half_rot, 1) * sine_up
            + pltpu.roll(block, half_rot, 1) * sine_down
        )

    queries = turn(kind(0)).astype(jnp.bfloat16)
    turned = turn(kind(1)).astype(jnp.bfloat16)
    plain = kind(2).astype(jnp.bfloat16)

    for index in range(held_count):
        rows = slice(index * fresh_len, (index + 1) * fresh_len)
        outs[1][index] = turned[rows]
        outs[2][index] = plain[rows]

    factor = 1.0 / math.sqrt(HEAD) / math.log(2.0)
    starts = [(2 * HEAD * pair) // LANES * LANES for pair in range(pairs)]
    lane = lax.broadcasted_iota(jnp.int32, (fresh_len, WINDOW), 1)

    def owned(pair, member):
        begin = (2 * pair + member) * HEAD - starts[pair]
        return (lane >= begin) & (lane < begin + HEAD)

    def contract(left, right):
        return lax.dot_general(
            left, right, (((1,), (1,)), ((), ())), preferred_element_type=jnp.float32
        )

    zero = jnp.zeros((fresh_len, WINDOW), jnp.bfloat16)
    spread_rows = heads * fresh_len
    row = lax.broadcasted_iota(jnp.int32, (2 * fresh_len, fresh_len), 0)
    causal_pair = lax.rem(row, fresh_len) >= lax.broadcasted_iota(
        jnp.int32, (2 * fresh_len, fresh_len), 1
    )
    for index in range(held_count):
        rows = slice(index * fresh_len, (index + 1) * fresh_len)
        spread = []
        for pair in range(pairs):
            window = queries[rows, starts[pair] : starts[pair] + WINDOW]
            spread.append(
                jnp.concatenate(
                    [jnp.where(owned(pair, member), window, zero) for member in range(2)], axis=0
                )
            )
        scores = jnp.concatenate(
            [
                jnp.where(
                    causal_pair,
                    contract(spread[pair], turned[rows, starts[pair] : starts[pair] + WINDOW]),
                    -1e30,
                )
                for pair in range(pairs)
            ],
            axis=0,
        )
        peak = jnp.max(scores, axis=1, keepdims=True)
        weight = jnp.exp2((scores - peak) * factor)
        denom = jnp.sum(weight, axis=1, keepdims=True)
        weight = weight.astype(jnp.bfloat16)
        mixed = jnp.concatenate(
            [
                jnp.dot(
                    weight[pair * 2 * fresh_len : (pair + 1) * 2 * fresh_len],
                    plain[rows, starts[pair] : starts[pair] + WINDOW],
                    preferred_element_type=jnp.float32,
                )
                for pair in range(pairs)
            ],
            axis=0,
        )

        def finish(entry, carry, index=index):
            for copy in copies(index, entry):
                copy.wait()
            return carry

        lax.fori_loop(0, counts[index] * CHUNK_PAGES, finish, 0)

        def step(part, carry, index=index, spread=spread):
            peak, denom, mixed = carry
            scores = jnp.concatenate(
                [
                    contract(spread[pair], cached(keys, index, part, pair))
                    for pair in range(pairs)
                ],
                axis=0,
            )
            position = part * chunk + lax.broadcasted_iota(jnp.int32, (spread_rows, chunk), 1)
            scores = jnp.where(position < lengths[index], scores, -1e30)
            higher = jnp.maximum(peak, jnp.max(scores, axis=1, keepdims=True))
            shrink = jnp.exp2((peak - higher) * factor)
            weight = jnp.exp2((scores - higher) * factor)
            denom = denom * shrink + jnp.sum(weight, axis=1, keepdims=True)
            weight = weight.astype(jnp.bfloat16)
            added = jnp.concatenate(
                [
                    jnp.dot(
                        weight[pair * 2 * fresh_len : (pair + 1) * 2 * fresh_len],
                        cached(values, index, part, pair),
                        preferred_element_type=jnp.float32,
                    )
                    for pair in range(pairs)
                ],
                axis=0,
            )
            return higher, denom, mixed * shrink + added

        peak, denom, mixed = lax.fori_loop(0, counts[index], step, (peak, denom, mixed))
        mixed = mixed / denom
        tiles = [None] * (width // LANES)
        for pair in range(pairs):
            for member in range(2):
                begin = (2 * pair + member) * fresh_len
                part = jnp.where(owned(pair, member), mixed[begin : begin + fresh_len], 0.0)
                for side in range(2):
                    place_at = starts[pair] // LANES + side
                    tile = part[:, side * LANES : (side + 1) * LANES]
                    tiles[place_at] = tile if tiles[place_at] is None else tiles[place_at] + tile
        outs[0][index] = jnp.concatenate(tiles, axis=1).astype(jnp.bfloat16)


def per_device(
    req_size,
    wgt_size,
    arrivals,
    group_of,
    lengths,
    page_table,
    ln_gain,
    ln_bias,
    w_qkv,
    qkv_bias,
    key_pool,
    value_pool,
):
    req_count, fresh_len, width = arrivals.shape
    rows = req_count * fresh_len
    depth, local_cols = w_qkv.shape
    half_cols = local_cols // 2
    heads = local_cols // (3 * HEAD)
    page = key_pool.shape[1]
    chips = req_size // 2
    block = 2 * depth
    everyone = group_of.shape[0]
    me = lax.axis_index("req")
    layer = lax.axis_index("wgt")
    core = me & 1
    chip = me >> 1

    def swap(value, distance):
        return lax.ppermute(
            value, "req", [(device, device ^ distance) for device in range(req_size)]
        )

    def after(value, others):
        return lax.optimization_barrier((value, others))[0]

    half = req_count // 2
    layer = lax.axis_index("wgt")
    per = chips // wgt_size

    other_rows = lax.dynamic_slice_in_dim(w_qkv, (1 - core) * half_cols, half_cols, 1)
    if half_cols % LANES == 0:
        own_rows = w_qkv
    else:
        own_rows = lax.dynamic_slice_in_dim(w_qkv, core * half_cols, half_cols, 1)
    arrivals = after(arrivals, other_rows)
    other_rows = swap(other_rows, 1)

    params = pltpu.CompilerParams(vmem_limit_bytes=VMEM_LIMIT)
    stats = pl.pallas_call(
        measure_kernel,
        out_shape=jax.ShapeDtypeStruct((wgt_size, req_count, fresh_len, LANES), jnp.float32),
        in_specs=[VMEM],
        out_specs=VMEM,
        compiler_params=params,
        name="measure",
    )(arrivals)
    stats = lax.all_to_all(stats, "wgt", 0, 0, tiled=True)
    gain, shift = (
        lax.dynamic_slice_in_dim(value, layer * width, width).astype(jnp.float32).reshape(1, width)
        for value in (ln_gain, ln_bias)
    )
    tokens = pl.pallas_call(
        norm_kernel,
        out_shape=jax.ShapeDtypeStruct((req_count, fresh_len, width), jnp.bfloat16),
        in_specs=[VMEM] * 4,
        out_specs=VMEM,
        compiler_params=params,
        name="norm",
    )(arrivals, stats, gain, shift)
    tokens = tokens.reshape(rows, per, block) if per > 1 else tokens.reshape(rows, width)

    def route(turn):
        pairs = []
        for device in range(req_size):
            for at in range(wgt_size):
                to = device // 2
                origin = turn ^ (at * per + to % per)
                pairs.append(
                    ((2 * origin + device % 2) * wgt_size + to // per, device * wgt_size + at)
                )
        value = tokens
        if per > 1:
            value = lax.dynamic_index_in_dim(tokens, (chip ^ turn) % per, 1, False)
        return lax.ppermute(value, ("req", "wgt"), pairs)

    received = [route(turn) for turn in range(chips)]

    square_plane = chips == 4
    if square_plane:
        plan = [([2, 6], jnp.bfloat16), ([5, 7], jnp.bfloat16)]
        plan += [([distance], jnp.float32) for distance in (0, 4, 1, 3)]
    else:
        plan = [([0], jnp.float32)]
        plan += [([distance], jnp.bfloat16) for distance in range(1, req_size)]

    ids = jnp.arange(everyone, dtype=jnp.int32)
    same_group = group_of[:, None] == group_of[None, :]
    earlier = ids[None, :] < ids[:, None]
    rank = jnp.sum((same_group & earlier).astype(jnp.int32), axis=1)
    part_of, within = rank // half, rank % half
    place_of = np.zeros(req_size, np.int32)
    place_of[[target for members, _ in plan for target in members]] = np.arange(req_size)
    place_of = jnp.asarray(place_of)[group_of ^ me]
    spot = (part_of * req_size + place_of) * half + within
    origin = ids // req_count
    row = (((origin & 1) ^ core) * chips + (origin >> 1)) * req_count + ids % req_count
    position = jnp.sum(jnp.where(row[None, :] == ids[:, None], spot[None, :], 0), axis=1)

    lane = np.arange(HEAD)
    half_rot = ROT // 2
    inverse = jnp.power(10000.0, -jnp.asarray(lane % half_rot, jnp.float32) * 2.0 / ROT)
    positions = (
        lengths[:, None] + jnp.arange(fresh_len, dtype=jnp.int32)[None, :]
    ).astype(jnp.float32)
    angles = positions.reshape(rows, 1) * inverse[None, :]
    turns = jnp.asarray(lane < ROT)[None, :]
    cosine = jnp.where(turns, jnp.cos(angles), 1.0)
    sine = jnp.sin(angles)
    sine_up = jnp.where(jnp.asarray(lane < half_rot)[None, :], -sine, 0.0)
    sine_down = jnp.where(turns & jnp.asarray(lane >= half_rot)[None, :], sine, 0.0)

    tables = [
        value.reshape(req_count, fresh_len, HEAD) for value in (cosine, sine_up, sine_down)
    ]
    bias = qkv_bias.astype(jnp.float32).reshape(1, local_cols)
    place = jnp.stack([core, layer * per + chip % per]).astype(jnp.int32)
    chunk_rows = half * fresh_len
    span = page_table.shape[1]
    pages = span + (req_count - 1) * (span // 2)

    received += [swap(piece, 1) for piece in received]
    received = [piece.reshape(req_count, fresh_len, block) for piece in received]

    def collect(blocks):
        if not square_plane:
            sums = [blocks[0]]
            sums += [swap(block, distance) for distance, block in enumerate(blocks[1:], 1)]
            return sums[::2], sums[1::2]
        along_x, along_y = swap(blocks[0], 2), swap(blocks[1], 4)
        own, own_y, other, other_x = blocks[2:]
        behind_y = swap((own_y + along_x[1:]).astype(jnp.bfloat16), 4)
        behind_x = swap((other_x + along_y[1:]).astype(jnp.bfloat16), 2)
        return [own, along_x, behind_y], [swap(other + along_y[:1], 1), swap(behind_x, 1)]

    projected = []
    for part in range(2):
        projected.append(
            pl.pallas_call(
                functools.partial(project_kernel, part, plan),
                out_shape=[
                    jax.ShapeDtypeStruct((len(members), chunk_rows, half_cols), kind)
                    for members, kind in plan
                ],
                in_specs=[SMEM] * 2 + [HBM] * (req_size + 2),
                out_specs=[HBM] * len(plan),
                scratch_shapes=[
                    pltpu.VMEM((block, half_cols), jnp.bfloat16),
                    pltpu.VMEM((req_size * half, fresh_len, block), jnp.bfloat16),
                    pltpu.SemaphoreType.DMA((req_size * half,)),
                    pltpu.SemaphoreType.DMA((2,)),
                    pltpu.SemaphoreType.DMA((req_size,)),
                ]
                + [
                    pltpu.VMEM((len(members), chunk_rows, half_cols), kind)
                    for members, kind in plan
                ],
                compiler_params=pltpu.CompilerParams(vmem_limit_bytes=VMEM_LIMIT),
                name="project",
            )(place, position, *received, own_rows, other_rows)
        )

    terms, sums = [], []
    for blocks in projected:
        for side in collect(blocks):
            terms.append(len(side))
            sums += side
    out = jax.ShapeDtypeStruct((req_count, fresh_len, heads * HEAD), jnp.bfloat16)
    return tuple(
        pl.pallas_call(
            functools.partial(attend_kernel, (terms, req_count, fresh_len, page, heads)),
            out_shape=[out] * 3,
            in_specs=[SMEM] * 3 + [VMEM] * (len(sums) + 4) + [HBM] * 2,
            out_specs=[VMEM] * 3,
            scratch_shapes=[
                pltpu.VMEM((pages, page, heads * HEAD), jnp.bfloat16),
                pltpu.VMEM((pages, page, heads * HEAD), jnp.bfloat16),
                pltpu.SemaphoreType.DMA((req_count,)),
            ],
            compiler_params=pltpu.CompilerParams(vmem_limit_bytes=VMEM_LIMIT),
            name="attend",
        )(place, lengths, page_table, *sums, bias, *tables, key_pool, value_pool)
    )


def solution(mesh):
    in_specs = (
        P("req", None, "wgt"),
        P(),
        P("req"),
        P("req", None),
        P(),
        P(),
        P("req", "wgt"),
        P("wgt"),
        P("req", None, "wgt"),
        P("req", None, "wgt"),
    )
    out_specs = (P("req", None, "wgt"), P("req", None, "wgt"), P("req", None, "wgt"))
    return jax.shard_map(
        functools.partial(per_device, mesh.shape["req"], mesh.shape["wgt"]),
        mesh=mesh,
        in_specs=in_specs,
        out_specs=out_specs,
        check_vma=False,
    )
```

```python
import functools
import math

import jax
import jax.numpy as jnp
import numpy as np
from jax import lax
from jax.experimental import pallas as pl
from jax.experimental.pallas import tpu as pltpu
from jax.sharding import PartitionSpec as P

HEAD = 96
ROT = 24
EPS = 1e-05
LANES = 128
WINDOW = 2 * LANES
CHUNK_PAGES = 4
VMEM_LIMIT = 58 * 1024 * 1024

SMEM = pl.BlockSpec(memory_space=pltpu.SMEM)
VMEM = pl.BlockSpec(memory_space=pltpu.VMEM)
HBM = pl.BlockSpec(memory_space=pltpu.HBM)


def project_kernel(part, plan, place, position, *refs):
    groups = sum(len(members) for members, _ in plan)
    tokens = refs[:groups]
    own_rows, other_rows = refs[groups : groups + 2]
    outs = refs[groups + 2 : -4]
    weights, picked, sems, weight_sems = refs[-4:]
    core, begin = place[0], place[1]
    depth = own_rows.shape[0]
    chips = groups // 2
    req_count, fresh_len, width = tokens[0].shape
    half_cols = weights.shape[1]
    rows = outs[0].shape[1]
    held_count = rows // fresh_len

    def columns(ref):
        if ref.shape[1] == half_cols:
            return ref
        return ref.at[:, pl.ds(pl.multiple_of(core * half_cols, LANES), half_cols)]

    copies = [
        pltpu.make_async_copy(
            columns(own_rows),
            weights.at[pl.ds(pl.multiple_of(core * depth, 16), depth)],
            weight_sems.at[0],
        ),
        pltpu.make_async_copy(
            columns(other_rows),
            weights.at[pl.ds(pl.multiple_of((1 - core) * depth, 16), depth)],
            weight_sems.at[1],
        ),
    ]
    fetches = []
    for index, token in enumerate(tokens):
        row = (index // chips * chips + (index % chips ^ begin)) * req_count
        for item in range(req_count):
            to = position[row + item] - part * groups * held_count
            mine = (to >= 0) & (to < groups * held_count)
            to = jnp.where(mine, to, 0)
            fetches.append(
                (
                    mine,
                    pltpu.make_async_copy(
                        token.at[item], picked.at[to], sems.at[index * req_count + item]
                    ),
                )
            )
    for mine, fetch in fetches:

        @pl.when(mine)
        def _():
            fetch.start()

    for copy in copies:
        copy.start()
    for mine, fetch in fetches:

        @pl.when(mine)
        def _():
            fetch.wait()

    for copy in copies:
        copy.wait()
    together = min(groups, 4)
    targets = [
        (output, index) for output, (members, _) in enumerate(plan) for index in range(len(members))
    ]
    for first in range(0, groups, together):
        these = targets[first : first + together]
        value = picked[first * held_count : (first + together) * held_count]
        result = jnp.dot(
            value.reshape(together * rows, width),
            weights[...],
            preferred_element_type=jnp.float32,
        )
        for count, (output, index) in enumerate(these):
            outs[output][index] = result[count * rows : (count + 1) * rows].astype(
                outs[output].dtype
            )


def attend_kernel(shape, place, all_lengths, table, *refs):
    terms, held_count, fresh_len, page, heads = shape
    sums = []
    for count in terms:
        sums.append(sum(ref[0].astype(jnp.float32) for ref in refs[:count]))
        refs = refs[count:]
    bias, cosine, sine_up, sine_down, key_pool, value_pool, *outs = refs[:-3]
    keys, values, sems = refs[-3:]
    chunk = CHUNK_PAGES * page
    pairs = heads // 2

    lengths = [all_lengths[index] for index in range(held_count)]
    counts = [pl.cdiv(lengths[index], chunk) for index in range(held_count)]
    bases = [jnp.int32(0)]
    for count in counts[:-1]:
        bases.append(bases[-1] + count * CHUNK_PAGES)

    def copies(index, entry):
        number = table[index, entry]
        to = bases[index] + entry
        return (
            pltpu.make_async_copy(key_pool.at[number], keys.at[to], sems.at[index]),
            pltpu.make_async_copy(value_pool.at[number], values.at[to], sems.at[index]),
        )

    for index in range(held_count):

        def start(entry, carry, index=index):
            for copy in copies(index, entry):
                copy.start()
            return carry

        lax.fori_loop(0, counts[index] * CHUNK_PAGES, start, 0)

    def cached(pages, index, part, pair):
        held = pages[
            pl.ds(bases[index] + part * CHUNK_PAGES, CHUNK_PAGES),
            :,
            starts[pair] : starts[pair] + WINDOW,
        ]
        return held.reshape(chunk, WINDOW)

    near = jnp.concatenate(sums[::2], axis=0)
    far = jnp.concatenate(sums[1::2], axis=0)
    core = place[0]
    halves = jnp.where(core == 0, near, far), jnp.where(core == 0, far, near)
    halves = [
        half + bias[:, side * half.shape[1] : (side + 1) * half.shape[1]]
        for side, half in enumerate(halves)
    ]

    def kind(which):
        pieces = []
        for head in range(heads):
            half = halves[head // pairs]
            begin = (head % pairs) * 3 * HEAD + which * HEAD
            pieces.append(half[:, begin : begin + HEAD])
        return jnp.concatenate(pieces, axis=1)

    width = heads * HEAD

    def rows_of(ref):
        table = ref[...].reshape(held_count * fresh_len, HEAD)
        return jnp.concatenate([table] * heads, axis=1)

    cosine, sine_up, sine_down = rows_of(cosine), rows_of(sine_up), rows_of(sine_down)

    def turn(block):
        half_rot = ROT // 2
        return (
            block * cosine
            + pltpu.roll(block, width - half_rot, 1) * sine_up
            + pltpu.roll(block, half_rot, 1) * sine_down
        )

    queries = turn(kind(0)).astype(jnp.bfloat16)
    turned = turn(kind(1)).astype(jnp.bfloat16)
    plain = kind(2).astype(jnp.bfloat16)

    for index in range(held_count):
        rows = slice(index * fresh_len, (index + 1) * fresh_len)
        outs[1][index] = turned[rows]
        outs[2][index] = plain[rows]

    factor = 1.0 / math.sqrt(HEAD) / math.log(2.0)
    starts = [(2 * HEAD * pair) // LANES * LANES for pair in range(pairs)]
    lane = lax.broadcasted_iota(jnp.int32, (fresh_len, WINDOW), 1)

    def owned(pair, member):
        begin = (2 * pair + member) * HEAD - starts[pair]
        return (lane >= begin) & (lane < begin + HEAD)

    def contract(left, right):
        return lax.dot_general(
            left, right, (((1,), (1,)), ((), ())), preferred_element_type=jnp.float32
        )

    zero = jnp.zeros((fresh_len, WINDOW), jnp.bfloat16)
    spread_rows = heads * fresh_len
    row = lax.broadcasted_iota(jnp.int32, (2 * fresh_len, fresh_len), 0)
    causal_pair = lax.rem(row, fresh_len) >= lax.broadcasted_iota(
        jnp.int32, (2 * fresh_len, fresh_len), 1
    )
    for index in range(held_count):
        rows = slice(index * fresh_len, (index + 1) * fresh_len)
        spread = []
        for pair in range(pairs):
            window = queries[rows, starts[pair] : starts[pair] + WINDOW]
            spread.append(
                jnp.concatenate(
                    [jnp.where(owned(pair, member), window, zero) for member in range(2)], axis=0
                )
            )
        scores = jnp.concatenate(
            [
                jnp.where(
                    causal_pair,
                    contract(spread[pair], turned[rows, starts[pair] : starts[pair] + WINDOW]),
                    -1e30,
                )
                for pair in range(pairs)
            ],
            axis=0,
        )
        peak = jnp.max(scores, axis=1, keepdims=True)
        weight = jnp.exp2((scores - peak) * factor)
        denom = jnp.sum(weight, axis=1, keepdims=True)
        weight = weight.astype(jnp.bfloat16)
        mixed = jnp.concatenate(
            [
                jnp.dot(
                    weight[pair * 2 * fresh_len : (pair + 1) * 2 * fresh_len],
                    plain[rows, starts[pair] : starts[pair] + WINDOW],
                    preferred_element_type=jnp.float32,
                )
                for pair in range(pairs)
            ],
            axis=0,
        )

        def finish(entry, carry, index=index):
            for copy in copies(index, entry):
                copy.wait()
            return carry

        lax.fori_loop(0, counts[index] * CHUNK_PAGES, finish, 0)

        def step(part, carry, index=index, spread=spread):
            peak, denom, mixed = carry
            scores = jnp.concatenate(
                [
                    contract(spread[pair], cached(keys, index, part, pair))
                    for pair in range(pairs)
                ],
                axis=0,
            )
            position = part * chunk + lax.broadcasted_iota(jnp.int32, (spread_rows, chunk), 1)
            scores = jnp.where(position < lengths[index], scores, -1e30)
            higher = jnp.maximum(peak, jnp.max(scores, axis=1, keepdims=True))
            shrink = jnp.exp2((peak - higher) * factor)
            weight = jnp.exp2((scores - higher) * factor)
            denom = denom * shrink + jnp.sum(weight, axis=1, keepdims=True)
            weight = weight.astype(jnp.bfloat16)
            added = jnp.concatenate(
                [
                    jnp.dot(
                        weight[pair * 2 * fresh_len : (pair + 1) * 2 * fresh_len],
                        cached(values, index, part, pair),
                        preferred_element_type=jnp.float32,
                    )
                    for pair in range(pairs)
                ],
                axis=0,
            )
            return higher, denom, mixed * shrink + added

        peak, denom, mixed = lax.fori_loop(0, counts[index], step, (peak, denom, mixed))
        mixed = mixed / denom
        tiles = [None] * (width // LANES)
        for pair in range(pairs):
            for member in range(2):
                begin = (2 * pair + member) * fresh_len
                part = jnp.where(owned(pair, member), mixed[begin : begin + fresh_len], 0.0)
                for side in range(2):
                    place_at = starts[pair] // LANES + side
                    tile = part[:, side * LANES : (side + 1) * LANES]
                    tiles[place_at] = tile if tiles[place_at] is None else tiles[place_at] + tile
        outs[0][index] = jnp.concatenate(tiles, axis=1).astype(jnp.bfloat16)


def per_device(
    req_size,
    wgt_size,
    arrivals,
    group_of,
    lengths,
    page_table,
    ln_gain,
    ln_bias,
    w_qkv,
    qkv_bias,
    key_pool,
    value_pool,
):
    req_count, fresh_len, width = arrivals.shape
    rows = req_count * fresh_len
    depth, local_cols = w_qkv.shape
    half_cols = local_cols // 2
    heads = local_cols // (3 * HEAD)
    page = key_pool.shape[1]
    chips = req_size // 2
    block = 2 * depth
    everyone = group_of.shape[0]
    me = lax.axis_index("req")
    layer = lax.axis_index("wgt")
    core = me & 1
    chip = me >> 1

    def swap(value, distance):
        return lax.ppermute(
            value, "req", [(device, device ^ distance) for device in range(req_size)]
        )

    def after(value, others):
        return lax.optimization_barrier((value, others))[0]

    half = req_count // 2
    layer = lax.axis_index("wgt")
    per = chips // wgt_size

    widened = arrivals.reshape(rows, width).astype(jnp.float32)
    middle = jnp.mean(widened, axis=-1)
    square = jnp.sum(jnp.square(widened - middle[:, None]), axis=-1)
    local = jnp.stack([middle, square])
    stats = jnp.broadcast_to(local[None], (wgt_size, 2, rows))
    stats = lax.all_to_all(stats, "wgt", 0, 0, tiled=True)
    center = jnp.mean(stats[:, 0], axis=0)
    square = jnp.sum(stats[:, 1] + width * jnp.square(stats[:, 0] - center[None]), axis=0)
    scale = lax.rsqrt(square / (width * wgt_size) + EPS)
    gain, shift = (
        lax.dynamic_slice_in_dim(value, layer * width, width).astype(jnp.float32)
        for value in (ln_gain, ln_bias)
    )
    tokens = (widened - center[:, None]) * scale[:, None] * gain + shift
    tokens = tokens.astype(jnp.bfloat16)
    if per > 1:
        tokens = tokens.reshape(rows, per, block)

    def route(turn):
        pairs = []
        for device in range(req_size):
            for at in range(wgt_size):
                to = device // 2
                origin = turn ^ (at * per + to % per)
                pairs.append(
                    ((2 * origin + device % 2) * wgt_size + to // per, device * wgt_size + at)
                )
        value = tokens
        if per > 1:
            value = lax.dynamic_index_in_dim(tokens, (chip ^ turn) % per, 1, False)
        return lax.ppermute(value, ("req", "wgt"), pairs)

    received = [route(turn) for turn in range(chips)]

    square_plane = chips == 4
    if square_plane:
        plan = [([2, 6], jnp.bfloat16), ([5, 7], jnp.bfloat16)]
        plan += [([distance], jnp.float32) for distance in (0, 4, 1, 3)]
    else:
        plan = [([0], jnp.float32)]
        plan += [([distance], jnp.bfloat16) for distance in range(1, req_size)]

    ids = jnp.arange(everyone, dtype=jnp.int32)
    same_group = group_of[:, None] == group_of[None, :]
    earlier = ids[None, :] < ids[:, None]
    rank = jnp.sum((same_group & earlier).astype(jnp.int32), axis=1)
    part_of, within = rank // half, rank % half
    place_of = np.zeros(req_size, np.int32)
    place_of[[target for members, _ in plan for target in members]] = np.arange(req_size)
    place_of = jnp.asarray(place_of)[group_of ^ me]
    spot = (part_of * req_size + place_of) * half + within
    origin = ids // req_count
    row = (((origin & 1) ^ core) * chips + (origin >> 1)) * req_count + ids % req_count
    position = jnp.sum(jnp.where(row[None, :] == ids[:, None], spot[None, :], 0), axis=1)

    lane = np.arange(HEAD)
    half_rot = ROT // 2
    inverse = jnp.power(10000.0, -jnp.asarray(lane % half_rot, jnp.float32) * 2.0 / ROT)
    positions = (
        lengths[:, None] + jnp.arange(fresh_len, dtype=jnp.int32)[None, :]
    ).astype(jnp.float32)
    angles = positions.reshape(rows, 1) * inverse[None, :]
    turns = jnp.asarray(lane < ROT)[None, :]
    cosine = jnp.where(turns, jnp.cos(angles), 1.0)
    sine = jnp.sin(angles)
    sine_up = jnp.where(jnp.asarray(lane < half_rot)[None, :], -sine, 0.0)
    sine_down = jnp.where(turns & jnp.asarray(lane >= half_rot)[None, :], sine, 0.0)

    tables = [
        value.reshape(req_count, fresh_len, HEAD) for value in (cosine, sine_up, sine_down)
    ]
    bias = qkv_bias.astype(jnp.float32).reshape(1, local_cols)
    place = jnp.stack([core, layer * per + chip % per]).astype(jnp.int32)
    chunk_rows = half * fresh_len
    span = page_table.shape[1]
    pages = span + (req_count - 1) * (span // 2)

    held = after(w_qkv, local)
    if half_cols % LANES == 0:
        own_rows = w_qkv
    else:
        own_rows = lax.dynamic_slice_in_dim(held, core * half_cols, half_cols, 1)
    other_rows = swap(lax.dynamic_slice_in_dim(held, (1 - core) * half_cols, half_cols, 1), 1)

    received += [swap(piece, 1) for piece in received]
    received = [piece.reshape(req_count, fresh_len, block) for piece in received]

    def collect(blocks):
        if not square_plane:
            sums = [blocks[0]]
            sums += [swap(block, distance) for distance, block in enumerate(blocks[1:], 1)]
            return sums[::2], sums[1::2]
        along_x, along_y = swap(blocks[0], 2), swap(blocks[1], 4)
        own, own_y, other, other_x = blocks[2:]
        behind_y = swap((own_y + along_x[1:]).astype(jnp.bfloat16), 4)
        behind_x = swap((other_x + along_y[1:]).astype(jnp.bfloat16), 2)
        return [own, along_x, behind_y], [swap(other + along_y[:1], 1), swap(behind_x, 1)]

    projected = []
    for part in range(2):
        projected.append(
            pl.pallas_call(
                functools.partial(project_kernel, part, plan),
                out_shape=[
                    jax.ShapeDtypeStruct((len(members), chunk_rows, half_cols), kind)
                    for members, kind in plan
                ],
                in_specs=[SMEM] * 2 + [HBM] * (req_size + 2),
                out_specs=[VMEM] * len(plan),
                scratch_shapes=[
                    pltpu.VMEM((block, half_cols), jnp.bfloat16),
                    pltpu.VMEM((req_size * half, fresh_len, block), jnp.bfloat16),
                    pltpu.SemaphoreType.DMA((everyone,)),
                    pltpu.SemaphoreType.DMA((2,)),
                ],
                compiler_params=pltpu.CompilerParams(vmem_limit_bytes=VMEM_LIMIT),
                name="project",
            )(place, position, *received, own_rows, other_rows)
        )

    terms, sums = [], []
    for blocks in projected:
        for side in collect(blocks):
            terms.append(len(side))
            sums += side
    out = jax.ShapeDtypeStruct((req_count, fresh_len, heads * HEAD), jnp.bfloat16)
    return tuple(
        pl.pallas_call(
            functools.partial(attend_kernel, (terms, req_count, fresh_len, page, heads)),
            out_shape=[out] * 3,
            in_specs=[SMEM] * 3 + [VMEM] * (len(sums) + 4) + [HBM] * 2,
            out_specs=[VMEM] * 3,
            scratch_shapes=[
                pltpu.VMEM((pages, page, heads * HEAD), jnp.bfloat16),
                pltpu.VMEM((pages, page, heads * HEAD), jnp.bfloat16),
                pltpu.SemaphoreType.DMA((req_count,)),
            ],
            compiler_params=pltpu.CompilerParams(vmem_limit_bytes=VMEM_LIMIT),
            name="attend",
        )(place, lengths, page_table, *sums, bias, *tables, key_pool, value_pool)
    )


def solution(mesh):
    in_specs = (
        P("req", None, "wgt"),
        P(),
        P("req"),
        P("req", None),
        P(),
        P(),
        P("req", "wgt"),
        P("wgt"),
        P("req", None, "wgt"),
        P("req", None, "wgt"),
    )
    out_specs = (P("req", None, "wgt"), P("req", None, "wgt"), P("req", None, "wgt"))
    return jax.shard_map(
        functools.partial(per_device, mesh.shape["req"], mesh.shape["wgt"]),
        mesh=mesh,
        in_specs=in_specs,
        out_specs=out_specs,
        check_vma=False,
    )
```

```python
import functools
import math

import jax
import jax.numpy as jnp
import numpy as np
from jax import lax
from jax.experimental import pallas as pl
from jax.experimental.pallas import tpu as pltpu
from jax.sharding import PartitionSpec as P

HEAD = 96
ROT = 24
EPS = 1e-05
LANES = 128
WINDOW = 2 * LANES
CHUNK_PAGES = 4
VMEM_LIMIT = 58 * 1024 * 1024

SMEM = pl.BlockSpec(memory_space=pltpu.SMEM)
VMEM = pl.BlockSpec(memory_space=pltpu.VMEM)
HBM = pl.BlockSpec(memory_space=pltpu.HBM)


def project_kernel(part, plan, place, position, *refs):
    groups = sum(len(members) for members, _ in plan)
    tokens = refs[:groups]
    own_rows, other_rows, scaling = refs[groups : groups + 3]
    outs = refs[groups + 3 : -4]
    weights, picked, sems, weight_sems = refs[-4:]
    core, begin = place[0], place[1]
    depth = own_rows.shape[0]
    chips = groups // 2
    req_count, fresh_len, width = tokens[0].shape
    half_cols = weights.shape[1]
    rows = outs[0].shape[1]
    held_count = rows // fresh_len

    def columns(ref):
        if ref.shape[1] == half_cols:
            return ref
        return ref.at[:, pl.ds(pl.multiple_of(core * half_cols, LANES), half_cols)]

    copies = [
        pltpu.make_async_copy(
            columns(own_rows),
            weights.at[pl.ds(pl.multiple_of(core * depth, 16), depth)],
            weight_sems.at[0],
        ),
        pltpu.make_async_copy(
            columns(other_rows),
            weights.at[pl.ds(pl.multiple_of((1 - core) * depth, 16), depth)],
            weight_sems.at[1],
        ),
    ]
    fetches = []
    for index, token in enumerate(tokens):
        row = (index // chips * chips + (index % chips ^ begin)) * req_count
        for item in range(req_count):
            to = position[row + item] - part * groups * held_count
            mine = (to >= 0) & (to < groups * held_count)
            to = jnp.where(mine, to, 0)
            fetches.append(
                (
                    mine,
                    pltpu.make_async_copy(
                        token.at[item], picked.at[to], sems.at[index * req_count + item]
                    ),
                )
            )
    for mine, fetch in fetches:

        @pl.when(mine)
        def _():
            fetch.start()

    for copy in copies:
        copy.start()
    for mine, fetch in fetches:

        @pl.when(mine)
        def _():
            fetch.wait()

    for copy in copies:
        copy.wait()
    together = min(groups, 4)
    targets = [
        (output, index) for output, (members, _) in enumerate(plan) for index in range(len(members))
    ]
    for first in range(0, groups, together):
        these = targets[first : first + together]
        value = picked[first * held_count : (first + together) * held_count]
        result = jnp.dot(
            value.reshape(together * rows, width),
            weights[...],
            preferred_element_type=jnp.float32,
        )
        for count, (output, index) in enumerate(these):
            outs[output][index] = result[count * rows : (count + 1) * rows].astype(
                outs[output].dtype
            )
    if part == 1:
        outs[-1][...] = jnp.dot(
            scaling[...], weights[...], preferred_element_type=jnp.float32
        )[: outs[-1].shape[0]]


def attend_kernel(shape, place, all_lengths, table, *refs):
    terms, held_count, fresh_len, page, heads, depth = shape
    sums = []
    for count in terms:
        sums.append(sum(ref[0].astype(jnp.float32) for ref in refs[:count]))
        refs = refs[count:]
    factors, folded, bias, cosine, sine_up, sine_down, key_pool, value_pool, *outs = refs[:-3]
    keys, values, sems = refs[-3:]
    chunk = CHUNK_PAGES * page
    pairs = heads // 2

    lengths = [all_lengths[index] for index in range(held_count)]
    counts = [pl.cdiv(lengths[index], chunk) for index in range(held_count)]
    bases = [jnp.int32(0)]
    for count in counts[:-1]:
        bases.append(bases[-1] + count * CHUNK_PAGES)

    def copies(index, entry):
        number = table[index, entry]
        to = bases[index] + entry
        return (
            pltpu.make_async_copy(key_pool.at[number], keys.at[to], sems.at[index]),
            pltpu.make_async_copy(value_pool.at[number], values.at[to], sems.at[index]),
        )

    for index in range(held_count):

        def start(entry, carry, index=index):
            for copy in copies(index, entry):
                copy.start()
            return carry

        lax.fori_loop(0, counts[index] * CHUNK_PAGES, start, 0)

    def cached(pages, index, part, pair):
        held = pages[
            pl.ds(bases[index] + part * CHUNK_PAGES, CHUNK_PAGES),
            :,
            starts[pair] : starts[pair] + WINDOW,
        ]
        return held.reshape(chunk, WINDOW)

    near = jnp.concatenate(sums[::2], axis=0)
    far = jnp.concatenate(sums[1::2], axis=0)
    core = place[0]
    halves = jnp.where(core == 0, near, far), jnp.where(core == 0, far, near)
    factors = factors[...].reshape(held_count * fresh_len, depth + 1)
    devices = folded.shape[0]
    per = devices // 2 // depth
    finished = []
    for side, half in enumerate(halves):
        half = half * factors[:, 0:1] + bias[:, side * half.shape[1] : (side + 1) * half.shape[1]]
        for device in range(side, devices, 2):
            layer = device // 2 // per
            lines = folded[device]
            half = half + factors[:, layer + 1 : layer + 2] * lines[0:1] + lines[1:2]
        finished.append(half)
    halves = finished

    def kind(which):
        pieces = []
        for head in range(heads):
            half = halves[head // pairs]
            begin = (head % pairs) * 3 * HEAD + which * HEAD
            pieces.append(half[:, begin : begin + HEAD])
        return jnp.concatenate(pieces, axis=1)

    width = heads * HEAD

    def rows_of(ref):
        table = ref[...].reshape(held_count * fresh_len, HEAD)
        return jnp.concatenate([table] * heads, axis=1)

    cosine, sine_up, sine_down = rows_of(cosine), rows_of(sine_up), rows_of(sine_down)

    def turn(block):
        half_rot = ROT // 2
        return (
            block * cosine
            + pltpu.roll(block, width - half_rot, 1) * sine_up
            + pltpu.roll(block, half_rot, 1) * sine_down
        )

    queries = turn(kind(0)).astype(jnp.bfloat16)
    turned = turn(kind(1)).astype(jnp.bfloat16)
    plain = kind(2).astype(jnp.bfloat16)

    for index in range(held_count):
        rows = slice(index * fresh_len, (index + 1) * fresh_len)
        outs[1][index] = turned[rows]
        outs[2][index] = plain[rows]

    factor = 1.0 / math.sqrt(HEAD) / math.log(2.0)
    starts = [(2 * HEAD * pair) // LANES * LANES for pair in range(pairs)]
    lane = lax.broadcasted_iota(jnp.int32, (fresh_len, WINDOW), 1)

    def owned(pair, member):
        begin = (2 * pair + member) * HEAD - starts[pair]
        return (lane >= begin) & (lane < begin + HEAD)

    def contract(left, right):
        return lax.dot_general(
            left, right, (((1,), (1,)), ((), ())), preferred_element_type=jnp.float32
        )

    zero = jnp.zeros((fresh_len, WINDOW), jnp.bfloat16)
    spread_rows = heads * fresh_len
    row = lax.broadcasted_iota(jnp.int32, (2 * fresh_len, fresh_len), 0)
    causal_pair = lax.rem(row, fresh_len) >= lax.broadcasted_iota(
        jnp.int32, (2 * fresh_len, fresh_len), 1
    )
    for index in range(held_count):
        rows = slice(index * fresh_len, (index + 1) * fresh_len)
        spread = []
        for pair in range(pairs):
            window = queries[rows, starts[pair] : starts[pair] + WINDOW]
            spread.append(
                jnp.concatenate(
                    [jnp.where(owned(pair, member), window, zero) for member in range(2)], axis=0
                )
            )
        scores = jnp.concatenate(
            [
                jnp.where(
                    causal_pair,
                    contract(spread[pair], turned[rows, starts[pair] : starts[pair] + WINDOW]),
                    -1e30,
                )
                for pair in range(pairs)
            ],
            axis=0,
        )
        peak = jnp.max(scores, axis=1, keepdims=True)
        weight = jnp.exp2((scores - peak) * factor)
        denom = jnp.sum(weight, axis=1, keepdims=True)
        weight = weight.astype(jnp.bfloat16)
        mixed = jnp.concatenate(
            [
                jnp.dot(
                    weight[pair * 2 * fresh_len : (pair + 1) * 2 * fresh_len],
                    plain[rows, starts[pair] : starts[pair] + WINDOW],
                    preferred_element_type=jnp.float32,
                )
                for pair in range(pairs)
            ],
            axis=0,
        )

        def finish(entry, carry, index=index):
            for copy in copies(index, entry):
                copy.wait()
            return carry

        lax.fori_loop(0, counts[index] * CHUNK_PAGES, finish, 0)

        def step(part, carry, index=index, spread=spread):
            peak, denom, mixed = carry
            scores = jnp.concatenate(
                [
                    contract(spread[pair], cached(keys, index, part, pair))
                    for pair in range(pairs)
                ],
                axis=0,
            )
            position = part * chunk + lax.broadcasted_iota(jnp.int32, (spread_rows, chunk), 1)
            scores = jnp.where(position < lengths[index], scores, -1e30)
            higher = jnp.maximum(peak, jnp.max(scores, axis=1, keepdims=True))
            shrink = jnp.exp2((peak - higher) * factor)
            weight = jnp.exp2((scores - higher) * factor)
            denom = denom * shrink + jnp.sum(weight, axis=1, keepdims=True)
            weight = weight.astype(jnp.bfloat16)
            added = jnp.concatenate(
                [
                    jnp.dot(
                        weight[pair * 2 * fresh_len : (pair + 1) * 2 * fresh_len],
                        cached(values, index, part, pair),
                        preferred_element_type=jnp.float32,
                    )
                    for pair in range(pairs)
                ],
                axis=0,
            )
            return higher, denom, mixed * shrink + added

        peak, denom, mixed = lax.fori_loop(0, counts[index], step, (peak, denom, mixed))
        mixed = mixed / denom
        tiles = [None] * (width // LANES)
        for pair in range(pairs):
            for member in range(2):
                begin = (2 * pair + member) * fresh_len
                part = jnp.where(owned(pair, member), mixed[begin : begin + fresh_len], 0.0)
                for side in range(2):
                    place_at = starts[pair] // LANES + side
                    tile = part[:, side * LANES : (side + 1) * LANES]
                    tiles[place_at] = tile if tiles[place_at] is None else tiles[place_at] + tile
        outs[0][index] = jnp.concatenate(tiles, axis=1).astype(jnp.bfloat16)


def per_device(
    req_size,
    wgt_size,
    arrivals,
    group_of,
    lengths,
    page_table,
    ln_gain,
    ln_bias,
    w_qkv,
    qkv_bias,
    key_pool,
    value_pool,
):
    req_count, fresh_len, width = arrivals.shape
    rows = req_count * fresh_len
    depth, local_cols = w_qkv.shape
    half_cols = local_cols // 2
    heads = local_cols // (3 * HEAD)
    page = key_pool.shape[1]
    chips = req_size // 2
    block = 2 * depth
    everyone = group_of.shape[0]
    me = lax.axis_index("req")
    layer = lax.axis_index("wgt")
    core = me & 1
    chip = me >> 1

    def swap(value, distance):
        return lax.ppermute(
            value, "req", [(device, device ^ distance) for device in range(req_size)]
        )

    def after(value, others):
        return lax.optimization_barrier((value, others))[0]

    half = req_count // 2
    layer = lax.axis_index("wgt")
    per = chips // wgt_size

    widened = arrivals.reshape(rows, width).astype(jnp.float32)
    middle = jnp.mean(widened, axis=-1)
    gain = lax.dynamic_slice_in_dim(ln_gain, layer * width, width).astype(jnp.float32)
    tokens = ((widened - middle[:, None]) * gain).astype(jnp.bfloat16)
    if per > 1:
        tokens = tokens.reshape(rows, per, block)

    def route(turn):
        pairs = []
        for device in range(req_size):
            for at in range(wgt_size):
                to = device // 2
                origin = turn ^ (at * per + to % per)
                pairs.append(
                    ((2 * origin + device % 2) * wgt_size + to // per, device * wgt_size + at)
                )
        value = tokens
        if per > 1:
            value = lax.dynamic_index_in_dim(tokens, (chip ^ turn) % per, 1, False)
        return lax.ppermute(value, ("req", "wgt"), pairs)

    received = [route(turn) for turn in range(chips)]

    square = jnp.sum(jnp.square(widened - middle[:, None]), axis=-1)
    stats = jnp.broadcast_to(jnp.stack([middle, square])[None], (wgt_size, 2, rows))
    stats = lax.all_to_all(stats, "wgt", 0, 0, tiled=True)
    center = jnp.mean(stats[:, 0], axis=0)
    apart = stats[:, 0] - center[None]
    square = jnp.sum(stats[:, 1] + width * jnp.square(apart), axis=0)
    scale = lax.rsqrt(square / (width * wgt_size) + EPS)
    factors = jnp.concatenate([scale[None], apart * scale[None]], axis=0)
    factors = jnp.broadcast_to(factors[None], (req_size, wgt_size + 1, rows))

    square_plane = chips == 4
    if square_plane:
        plan = [([2, 6], jnp.bfloat16), ([5, 7], jnp.bfloat16)]
        plan += [([distance], jnp.float32) for distance in (0, 4, 1, 3)]
    else:
        plan = [([0], jnp.float32)]
        plan += [([distance], jnp.bfloat16) for distance in range(1, req_size)]

    ids = jnp.arange(everyone, dtype=jnp.int32)
    same_group = group_of[:, None] == group_of[None, :]
    earlier = ids[None, :] < ids[:, None]
    rank = jnp.sum((same_group & earlier).astype(jnp.int32), axis=1)
    part_of, within = rank // half, rank % half
    place_of = np.zeros(req_size, np.int32)
    place_of[[target for members, _ in plan for target in members]] = np.arange(req_size)
    place_of = jnp.asarray(place_of)[group_of ^ me]
    spot = (part_of * req_size + place_of) * half + within
    origin = ids // req_count
    row = (((origin & 1) ^ core) * chips + (origin >> 1)) * req_count + ids % req_count
    position = jnp.sum(jnp.where(row[None, :] == ids[:, None], spot[None, :], 0), axis=1)

    served = me * req_count + jnp.arange(req_count, dtype=jnp.int32)
    slot_of = group_of * req_count + rank
    served = jnp.sum(jnp.where(slot_of[None, :] == served[:, None], ids[None, :], 0), axis=1)
    scaling = jnp.zeros((16, block), jnp.bfloat16)
    for line, value in enumerate((ln_gain, ln_bias)):
        value = lax.dynamic_slice_in_dim(value, chip * block, block)
        scaling = scaling.at[line].set(value)

    lane = np.arange(HEAD)
    half_rot = ROT // 2
    inverse = jnp.power(10000.0, -jnp.asarray(lane % half_rot, jnp.float32) * 2.0 / ROT)
    positions = (
        lengths[:, None] + jnp.arange(fresh_len, dtype=jnp.int32)[None, :]
    ).astype(jnp.float32)
    angles = positions.reshape(rows, 1) * inverse[None, :]
    turns = jnp.asarray(lane < ROT)[None, :]
    cosine = jnp.where(turns, jnp.cos(angles), 1.0)
    sine = jnp.sin(angles)
    sine_up = jnp.where(jnp.asarray(lane < half_rot)[None, :], -sine, 0.0)
    sine_down = jnp.where(turns & jnp.asarray(lane >= half_rot)[None, :], sine, 0.0)

    tables = [
        value.reshape(req_count, fresh_len, HEAD) for value in (cosine, sine_up, sine_down)
    ]
    bias = qkv_bias.astype(jnp.float32).reshape(1, local_cols)
    place = jnp.stack([core, layer * per + chip % per]).astype(jnp.int32)
    chunk_rows = half * fresh_len
    span = page_table.shape[1]
    pages = span + (req_count - 1) * (span // 2)

    held = w_qkv
    if half_cols % LANES == 0:
        own_rows = w_qkv
    else:
        own_rows = lax.dynamic_slice_in_dim(held, core * half_cols, half_cols, 1)
    other_rows = swap(lax.dynamic_slice_in_dim(held, (1 - core) * half_cols, half_cols, 1), 1)

    received += [swap(piece, 1) for piece in received]
    received = [piece.reshape(req_count, fresh_len, block) for piece in received]

    def collect(blocks):
        if not square_plane:
            sums = [blocks[0]]
            sums += [swap(block, distance) for distance, block in enumerate(blocks[1:], 1)]
            return sums[::2], sums[1::2]
        along_x, along_y = swap(blocks[0], 2), swap(blocks[1], 4)
        own, own_y, other, other_x = blocks[2:]
        behind_y = swap((own_y + along_x[1:]).astype(jnp.bfloat16), 4)
        behind_x = swap((other_x + along_y[1:]).astype(jnp.bfloat16), 2)
        return [own, along_x, behind_y], [swap(other + along_y[:1], 1), swap(behind_x, 1)]

    projected = []
    for part in range(2):
        projected.append(
            pl.pallas_call(
                functools.partial(project_kernel, part, plan),
                out_shape=[
                    jax.ShapeDtypeStruct((len(members), chunk_rows, half_cols), kind)
                    for members, kind in plan
                ]
                + [jax.ShapeDtypeStruct((8, half_cols), jnp.float32)] * part,
                in_specs=[SMEM] * 2 + [HBM] * (req_size + 2) + [VMEM],
                out_specs=[VMEM] * (len(plan) + part),
                scratch_shapes=[
                    pltpu.VMEM((block, half_cols), jnp.bfloat16),
                    pltpu.VMEM((req_size * half, fresh_len, block), jnp.bfloat16),
                    pltpu.SemaphoreType.DMA((everyone,)),
                    pltpu.SemaphoreType.DMA((2,)),
                ],
                compiler_params=pltpu.CompilerParams(vmem_limit_bytes=VMEM_LIMIT),
                name="project",
            )(place, position, *received, own_rows, other_rows, scaling)
        )

    factors = lax.all_to_all(after(factors, projected[0][0]), "req", 0, 0, tiled=True)
    factors = factors.reshape(req_size, wgt_size + 1, req_count, fresh_len)
    factors = factors.transpose(0, 2, 3, 1).reshape(everyone, fresh_len, wgt_size + 1)
    factors = jnp.take(factors, served, axis=0)

    folded = jnp.broadcast_to(projected[1][-1][None], (req_size, 8, half_cols))
    folded = lax.all_to_all(folded, "req", 0, 0, tiled=True)

    terms, sums = [], []
    for blocks in projected:
        for side in collect(blocks[: len(plan)]):
            terms.append(len(side))
            sums += side
    out = jax.ShapeDtypeStruct((req_count, fresh_len, heads * HEAD), jnp.bfloat16)
    return tuple(
        pl.pallas_call(
            functools.partial(attend_kernel, (terms, req_count, fresh_len, page, heads, wgt_size)),
            out_shape=[out] * 3,
            in_specs=[SMEM] * 3 + [VMEM] * (len(sums) + 6) + [HBM] * 2,
            out_specs=[VMEM] * 3,
            scratch_shapes=[
                pltpu.VMEM((pages, page, heads * HEAD), jnp.bfloat16),
                pltpu.VMEM((pages, page, heads * HEAD), jnp.bfloat16),
                pltpu.SemaphoreType.DMA((req_count,)),
            ],
            compiler_params=pltpu.CompilerParams(vmem_limit_bytes=VMEM_LIMIT),
            name="attend",
        )(place, lengths, page_table, *sums, factors, folded, bias, *tables, key_pool, value_pool)
    )


def solution(mesh):
    in_specs = (
        P("req", None, "wgt"),
        P(),
        P("req"),
        P("req", None),
        P(),
        P(),
        P("req", "wgt"),
        P("wgt"),
        P("req", None, "wgt"),
        P("req", None, "wgt"),
    )
    out_specs = (P("req", None, "wgt"), P("req", None, "wgt"), P("req", None, "wgt"))
    return jax.shard_map(
        functools.partial(per_device, mesh.shape["req"], mesh.shape["wgt"]),
        mesh=mesh,
        in_specs=in_specs,
        out_specs=out_specs,
        check_vma=False,
    )
```

```python
import functools
import math

import jax
import jax.numpy as jnp
import numpy as np
from jax import lax
from jax.experimental import pallas as pl
from jax.experimental.pallas import tpu as pltpu
from jax.sharding import PartitionSpec as P

HEAD = 96
ROT = 24
EPS = 1e-05
LANES = 128
WINDOW = 2 * LANES
CHUNK_PAGES = 4
VMEM_LIMIT = 58 * 1024 * 1024

SMEM = pl.BlockSpec(memory_space=pltpu.SMEM)
VMEM = pl.BlockSpec(memory_space=pltpu.VMEM)
HBM = pl.BlockSpec(memory_space=pltpu.HBM)


def project_kernel(part, plan, place, position, *refs):
    groups = sum(len(members) for members, _ in plan)
    tokens = refs[:groups]
    own_rows, other_rows, scaling = refs[groups : groups + 3]
    outs = refs[groups + 3 : -4]
    weights, picked, sems, weight_sems = refs[-4:]
    core, begin = place[0], place[1]
    depth = own_rows.shape[0]
    chips = groups // 2
    req_count, fresh_len, width = tokens[0].shape
    half_cols = weights.shape[1]
    rows = outs[0].shape[1]
    held_count = rows // fresh_len

    def columns(ref):
        if ref.shape[1] == half_cols:
            return ref
        return ref.at[:, pl.ds(pl.multiple_of(core * half_cols, LANES), half_cols)]

    copies = [
        pltpu.make_async_copy(
            columns(own_rows),
            weights.at[pl.ds(pl.multiple_of(core * depth, 16), depth)],
            weight_sems.at[0],
        ),
        pltpu.make_async_copy(
            columns(other_rows),
            weights.at[pl.ds(pl.multiple_of((1 - core) * depth, 16), depth)],
            weight_sems.at[1],
        ),
    ]
    fetches = []
    for index, token in enumerate(tokens):
        row = (index // chips * chips + (index % chips ^ begin)) * req_count
        for item in range(req_count):
            to = position[row + item] - part * groups * held_count
            mine = (to >= 0) & (to < groups * held_count)
            to = jnp.where(mine, to, 0)
            fetches.append(
                (
                    mine,
                    pltpu.make_async_copy(
                        token.at[item], picked.at[to], sems.at[index * req_count + item]
                    ),
                )
            )
    for mine, fetch in fetches:

        @pl.when(mine)
        def _():
            fetch.start()

    for copy in copies:
        copy.start()
    for mine, fetch in fetches:

        @pl.when(mine)
        def _():
            fetch.wait()

    for copy in copies:
        copy.wait()
    together = min(groups, 4)
    targets = [
        (output, index) for output, (members, _) in enumerate(plan) for index in range(len(members))
    ]
    for first in range(0, groups, together):
        these = targets[first : first + together]
        value = picked[first * held_count : (first + together) * held_count]
        result = jnp.dot(
            value.reshape(together * rows, width),
            weights[...],
            preferred_element_type=jnp.float32,
        )
        for count, (output, index) in enumerate(these):
            outs[output][index] = result[count * rows : (count + 1) * rows].astype(
                outs[output].dtype
            )
    if part == 0:
        outs[-1][...] = jnp.dot(
            scaling[...], weights[...], preferred_element_type=jnp.float32
        )[: outs[-1].shape[0]]


def attend_kernel(shape, place, all_lengths, table, *refs):
    terms, held_count, fresh_len, page, heads, depth = shape
    sums = []
    for count in terms:
        sums.append(sum(ref[0].astype(jnp.float32) for ref in refs[:count]))
        refs = refs[count:]
    factors, folded, bias, cosine, sine_up, sine_down, key_pool, value_pool, *outs = refs[:-3]
    keys, values, sems = refs[-3:]
    chunk = CHUNK_PAGES * page
    pairs = heads // 2

    lengths = [all_lengths[index] for index in range(held_count)]
    counts = [pl.cdiv(lengths[index], chunk) for index in range(held_count)]
    bases = [jnp.int32(0)]
    for count in counts[:-1]:
        bases.append(bases[-1] + count * CHUNK_PAGES)

    def copies(index, entry):
        number = table[index, entry]
        to = bases[index] + entry
        return (
            pltpu.make_async_copy(key_pool.at[number], keys.at[to], sems.at[index]),
            pltpu.make_async_copy(value_pool.at[number], values.at[to], sems.at[index]),
        )

    for index in range(held_count):

        def start(entry, carry, index=index):
            for copy in copies(index, entry):
                copy.start()
            return carry

        lax.fori_loop(0, counts[index] * CHUNK_PAGES, start, 0)

    def cached(pages, index, part, pair):
        held = pages[
            pl.ds(bases[index] + part * CHUNK_PAGES, CHUNK_PAGES),
            :,
            starts[pair] : starts[pair] + WINDOW,
        ]
        return held.reshape(chunk, WINDOW)

    near = jnp.concatenate(sums[::2], axis=0)
    far = jnp.concatenate(sums[1::2], axis=0)
    core = place[0]
    halves = jnp.where(core == 0, near, far), jnp.where(core == 0, far, near)
    factors = factors[...].reshape(held_count * fresh_len, depth + 1)
    devices = folded.shape[0]
    per = devices // 2 // depth
    finished = []
    for side, half in enumerate(halves):
        half = half * factors[:, 0:1] + bias[:, side * half.shape[1] : (side + 1) * half.shape[1]]
        for device in range(side, devices, 2):
            layer = device // 2 // per
            lines = folded[device]
            half = half + factors[:, layer + 1 : layer + 2] * lines[0:1] + lines[1:2]
        finished.append(half)
    halves = finished

    def kind(which):
        pieces = []
        for head in range(heads):
            half = halves[head // pairs]
            begin = (head % pairs) * 3 * HEAD + which * HEAD
            pieces.append(half[:, begin : begin + HEAD])
        return jnp.concatenate(pieces, axis=1)

    width = heads * HEAD

    def rows_of(ref):
        table = ref[...].reshape(held_count * fresh_len, HEAD)
        return jnp.concatenate([table] * heads, axis=1)

    cosine, sine_up, sine_down = rows_of(cosine), rows_of(sine_up), rows_of(sine_down)

    def turn(block):
        half_rot = ROT // 2
        return (
            block * cosine
            + pltpu.roll(block, width - half_rot, 1) * sine_up
            + pltpu.roll(block, half_rot, 1) * sine_down
        )

    queries = turn(kind(0)).astype(jnp.bfloat16)
    turned = turn(kind(1)).astype(jnp.bfloat16)
    plain = kind(2).astype(jnp.bfloat16)

    for index in range(held_count):
        rows = slice(index * fresh_len, (index + 1) * fresh_len)
        outs[1][index] = turned[rows]
        outs[2][index] = plain[rows]

    factor = 1.0 / math.sqrt(HEAD) / math.log(2.0)
    starts = [(2 * HEAD * pair) // LANES * LANES for pair in range(pairs)]
    lane = lax.broadcasted_iota(jnp.int32, (fresh_len, WINDOW), 1)

    def owned(pair, member):
        begin = (2 * pair + member) * HEAD - starts[pair]
        return (lane >= begin) & (lane < begin + HEAD)

    def contract(left, right):
        return lax.dot_general(
            left, right, (((1,), (1,)), ((), ())), preferred_element_type=jnp.float32
        )

    zero = jnp.zeros((fresh_len, WINDOW), jnp.bfloat16)
    spread_rows = heads * fresh_len
    row = lax.broadcasted_iota(jnp.int32, (2 * fresh_len, fresh_len), 0)
    causal_pair = lax.rem(row, fresh_len) >= lax.broadcasted_iota(
        jnp.int32, (2 * fresh_len, fresh_len), 1
    )
    for index in range(held_count):
        rows = slice(index * fresh_len, (index + 1) * fresh_len)
        spread = []
        for pair in range(pairs):
            window = queries[rows, starts[pair] : starts[pair] + WINDOW]
            spread.append(
                jnp.concatenate(
                    [jnp.where(owned(pair, member), window, zero) for member in range(2)], axis=0
                )
            )
        scores = jnp.concatenate(
            [
                jnp.where(
                    causal_pair,
                    contract(spread[pair], turned[rows, starts[pair] : starts[pair] + WINDOW]),
                    -1e30,
                )
                for pair in range(pairs)
            ],
            axis=0,
        )
        peak = jnp.max(scores, axis=1, keepdims=True)
        weight = jnp.exp2((scores - peak) * factor)
        denom = jnp.sum(weight, axis=1, keepdims=True)
        weight = weight.astype(jnp.bfloat16)
        mixed = jnp.concatenate(
            [
                jnp.dot(
                    weight[pair * 2 * fresh_len : (pair + 1) * 2 * fresh_len],
                    plain[rows, starts[pair] : starts[pair] + WINDOW],
                    preferred_element_type=jnp.float32,
                )
                for pair in range(pairs)
            ],
            axis=0,
        )

        def finish(entry, carry, index=index):
            for copy in copies(index, entry):
                copy.wait()
            return carry

        lax.fori_loop(0, counts[index] * CHUNK_PAGES, finish, 0)

        def step(part, carry, index=index, spread=spread):
            peak, denom, mixed = carry
            scores = jnp.concatenate(
                [
                    contract(spread[pair], cached(keys, index, part, pair))
                    for pair in range(pairs)
                ],
                axis=0,
            )
            position = part * chunk + lax.broadcasted_iota(jnp.int32, (spread_rows, chunk), 1)
            scores = jnp.where(position < lengths[index], scores, -1e30)
            higher = jnp.maximum(peak, jnp.max(scores, axis=1, keepdims=True))
            shrink = jnp.exp2((peak - higher) * factor)
            weight = jnp.exp2((scores - higher) * factor)
            denom = denom * shrink + jnp.sum(weight, axis=1, keepdims=True)
            weight = weight.astype(jnp.bfloat16)
            added = jnp.concatenate(
                [
                    jnp.dot(
                        weight[pair * 2 * fresh_len : (pair + 1) * 2 * fresh_len],
                        cached(values, index, part, pair),
                        preferred_element_type=jnp.float32,
                    )
                    for pair in range(pairs)
                ],
                axis=0,
            )
            return higher, denom, mixed * shrink + added

        peak, denom, mixed = lax.fori_loop(0, counts[index], step, (peak, denom, mixed))
        mixed = mixed / denom
        tiles = [None] * (width // LANES)
        for pair in range(pairs):
            for member in range(2):
                begin = (2 * pair + member) * fresh_len
                part = jnp.where(owned(pair, member), mixed[begin : begin + fresh_len], 0.0)
                for side in range(2):
                    place_at = starts[pair] // LANES + side
                    tile = part[:, side * LANES : (side + 1) * LANES]
                    tiles[place_at] = tile if tiles[place_at] is None else tiles[place_at] + tile
        outs[0][index] = jnp.concatenate(tiles, axis=1).astype(jnp.bfloat16)


def per_device(
    req_size,
    wgt_size,
    arrivals,
    group_of,
    lengths,
    page_table,
    ln_gain,
    ln_bias,
    w_qkv,
    qkv_bias,
    key_pool,
    value_pool,
):
    req_count, fresh_len, width = arrivals.shape
    rows = req_count * fresh_len
    depth, local_cols = w_qkv.shape
    half_cols = local_cols // 2
    heads = local_cols // (3 * HEAD)
    page = key_pool.shape[1]
    chips = req_size // 2
    block = 2 * depth
    everyone = group_of.shape[0]
    me = lax.axis_index("req")
    layer = lax.axis_index("wgt")
    core = me & 1
    chip = me >> 1

    def swap(value, distance):
        return lax.ppermute(
            value, "req", [(device, device ^ distance) for device in range(req_size)]
        )

    def after(value, others):
        return lax.optimization_barrier((value, others))[0]

    half = req_count // 2
    layer = lax.axis_index("wgt")
    per = chips // wgt_size

    widened = arrivals.reshape(rows, width).astype(jnp.float32)
    middle = jnp.mean(widened, axis=-1)
    gain = lax.dynamic_slice_in_dim(ln_gain, layer * width, width).astype(jnp.float32)
    tokens = ((widened - middle[:, None]) * gain).astype(jnp.bfloat16)
    if per > 1:
        tokens = tokens.reshape(rows, per, block)

    def route(turn):
        pairs = []
        for device in range(req_size):
            for at in range(wgt_size):
                to = device // 2
                origin = turn ^ (at * per + to % per)
                pairs.append(
                    ((2 * origin + device % 2) * wgt_size + to // per, device * wgt_size + at)
                )
        value = tokens
        if per > 1:
            value = lax.dynamic_index_in_dim(tokens, (chip ^ turn) % per, 1, False)
        return lax.ppermute(value, ("req", "wgt"), pairs)

    received = [route(turn) for turn in range(chips)]

    square = jnp.sum(jnp.square(widened - middle[:, None]), axis=-1)
    stats = jnp.broadcast_to(jnp.stack([middle, square])[None], (wgt_size, 2, rows))
    stats = lax.all_to_all(stats, "wgt", 0, 0, tiled=True)
    center = jnp.mean(stats[:, 0], axis=0)
    apart = stats[:, 0] - center[None]
    square = jnp.sum(stats[:, 1] + width * jnp.square(apart), axis=0)
    scale = lax.rsqrt(square / (width * wgt_size) + EPS)
    factors = jnp.concatenate([scale[None], apart * scale[None]], axis=0)

    square_plane = chips == 4
    if square_plane:
        plan = [([2, 6], jnp.bfloat16), ([5, 7], jnp.bfloat16)]
        plan += [([distance], jnp.float32) for distance in (0, 4, 1, 3)]
    else:
        plan = [([0], jnp.float32)]
        plan += [([distance], jnp.bfloat16) for distance in range(1, req_size)]

    ids = jnp.arange(everyone, dtype=jnp.int32)
    same_group = group_of[:, None] == group_of[None, :]
    earlier = ids[None, :] < ids[:, None]
    rank = jnp.sum((same_group & earlier).astype(jnp.int32), axis=1)
    part_of, within = rank // half, rank % half
    place_of = np.zeros(req_size, np.int32)
    place_of[[target for members, _ in plan for target in members]] = np.arange(req_size)
    place_of = jnp.asarray(place_of)[group_of ^ me]
    spot = (part_of * req_size + place_of) * half + within
    origin = ids // req_count
    row = (((origin & 1) ^ core) * chips + (origin >> 1)) * req_count + ids % req_count
    position = jnp.sum(jnp.where(row[None, :] == ids[:, None], spot[None, :], 0), axis=1)

    served = me * req_count + jnp.arange(req_count, dtype=jnp.int32)
    slot_of = group_of * req_count + rank
    served = jnp.sum(jnp.where(slot_of[None, :] == served[:, None], ids[None, :], 0), axis=1)
    scaling = jnp.zeros((16, block), jnp.bfloat16)
    for line, value in enumerate((ln_gain, ln_bias)):
        value = lax.dynamic_slice_in_dim(value, chip * block, block)
        scaling = scaling.at[line].set(value)

    lane = np.arange(HEAD)
    half_rot = ROT // 2
    inverse = jnp.power(10000.0, -jnp.asarray(lane % half_rot, jnp.float32) * 2.0 / ROT)
    positions = (
        lengths[:, None] + jnp.arange(fresh_len, dtype=jnp.int32)[None, :]
    ).astype(jnp.float32)
    angles = positions.reshape(rows, 1) * inverse[None, :]
    turns = jnp.asarray(lane < ROT)[None, :]
    cosine = jnp.where(turns, jnp.cos(angles), 1.0)
    sine = jnp.sin(angles)
    sine_up = jnp.where(jnp.asarray(lane < half_rot)[None, :], -sine, 0.0)
    sine_down = jnp.where(turns & jnp.asarray(lane >= half_rot)[None, :], sine, 0.0)

    tables = [
        value.reshape(req_count, fresh_len, HEAD) for value in (cosine, sine_up, sine_down)
    ]
    bias = qkv_bias.astype(jnp.float32).reshape(1, local_cols)
    place = jnp.stack([core, layer * per + chip % per]).astype(jnp.int32)
    chunk_rows = half * fresh_len
    span = page_table.shape[1]
    pages = span + (req_count - 1) * (span // 2)

    held = w_qkv
    if half_cols % LANES == 0:
        own_rows = w_qkv
    else:
        own_rows = lax.dynamic_slice_in_dim(held, core * half_cols, half_cols, 1)
    other_rows = swap(lax.dynamic_slice_in_dim(held, (1 - core) * half_cols, half_cols, 1), 1)

    received += [swap(piece, 1) for piece in received]
    received = [piece.reshape(req_count, fresh_len, block) for piece in received]

    def collect(blocks):
        if not square_plane:
            sums = [blocks[0]]
            sums += [swap(block, distance) for distance, block in enumerate(blocks[1:], 1)]
            return sums[::2], sums[1::2], sums[1:]
        along_x, along_y = swap(blocks[0], 2), swap(blocks[1], 4)
        own, own_y, other, other_x = blocks[2:]
        behind_y = swap((own_y + along_x[1:]).astype(jnp.bfloat16), 4)
        behind_x = swap((other_x + along_y[1:]).astype(jnp.bfloat16), 2)
        far = [swap(other + along_y[:1], 1), swap(behind_x, 1)]
        return [own, along_x, behind_y], far, [along_x, along_y]

    projected = []
    for part in range(2):
        projected.append(
            pl.pallas_call(
                functools.partial(project_kernel, part, plan),
                out_shape=[
                    jax.ShapeDtypeStruct((len(members), chunk_rows, half_cols), kind)
                    for members, kind in plan
                ]
                + [jax.ShapeDtypeStruct((8, half_cols), jnp.float32)] * (1 - part),
                in_specs=[SMEM] * 2 + [HBM] * (req_size + 2) + [VMEM],
                out_specs=[VMEM] * (len(plan) + 1 - part),
                scratch_shapes=[
                    pltpu.VMEM((block, half_cols), jnp.bfloat16),
                    pltpu.VMEM((req_size * half, fresh_len, block), jnp.bfloat16),
                    pltpu.SemaphoreType.DMA((everyone,)),
                    pltpu.SemaphoreType.DMA((2,)),
                ],
                compiler_params=pltpu.CompilerParams(vmem_limit_bytes=VMEM_LIMIT),
                name="project",
            )(place, position, *received, own_rows, other_rows, scaling)
        )

    terms, sums, first = [], [], None
    for blocks in projected:
        near, far, arrived = collect(blocks[: len(plan)])
        terms += [len(near), len(far)]
        sums += near + far
        first = first or arrived

    count = wgt_size + 1
    lines = projected[0][-1][:2]
    message = jnp.zeros((-(-(count + 2) // 8) * 8, half_cols), jnp.float32)
    message = message.at[:2].set(lines).at[2 : 2 + count, :rows].set(factors)
    message = jnp.broadcast_to(after(message, first)[None], (req_size, *message.shape))
    folded = lax.all_to_all(message, "req", 0, 0, tiled=True)
    factors = folded[:, 2 : 2 + count, :rows].reshape(req_size, count, req_count, fresh_len)
    factors = factors.transpose(0, 2, 3, 1).reshape(everyone, fresh_len, count)
    factors = jnp.take(factors, served, axis=0)

    out = jax.ShapeDtypeStruct((req_count, fresh_len, heads * HEAD), jnp.bfloat16)
    return tuple(
        pl.pallas_call(
            functools.partial(attend_kernel, (terms, req_count, fresh_len, page, heads, wgt_size)),
            out_shape=[out] * 3,
            in_specs=[SMEM] * 3 + [VMEM] * (len(sums) + 6) + [HBM] * 2,
            out_specs=[VMEM] * 3,
            scratch_shapes=[
                pltpu.VMEM((pages, page, heads * HEAD), jnp.bfloat16),
                pltpu.VMEM((pages, page, heads * HEAD), jnp.bfloat16),
                pltpu.SemaphoreType.DMA((req_count,)),
            ],
            compiler_params=pltpu.CompilerParams(vmem_limit_bytes=VMEM_LIMIT),
            name="attend",
        )(place, lengths, page_table, *sums, factors, folded, bias, *tables, key_pool, value_pool)
    )


def solution(mesh):
    in_specs = (
        P("req", None, "wgt"),
        P(),
        P("req"),
        P("req", None),
        P(),
        P(),
        P("req", "wgt"),
        P("wgt"),
        P("req", None, "wgt"),
        P("req", None, "wgt"),
    )
    out_specs = (P("req", None, "wgt"), P("req", None, "wgt"), P("req", None, "wgt"))
    return jax.shard_map(
        functools.partial(per_device, mesh.shape["req"], mesh.shape["wgt"]),
        mesh=mesh,
        in_specs=in_specs,
        out_specs=out_specs,
        check_vma=False,
    )
```

```python
import functools
import math

import jax
import jax.numpy as jnp
import numpy as np
from jax import lax
from jax.experimental import pallas as pl
from jax.experimental.pallas import tpu as pltpu
from jax.sharding import PartitionSpec as P

HEAD = 96
ROT = 24
EPS = 1e-05
LANES = 128
WINDOW = 2 * LANES
CHUNK_PAGES = 4
VMEM_LIMIT = 58 * 1024 * 1024
PROJECT_LIMIT = 20 * 1024 * 1024

SMEM = pl.BlockSpec(memory_space=pltpu.SMEM)
VMEM = pl.BlockSpec(memory_space=pltpu.VMEM)
HBM = pl.BlockSpec(memory_space=pltpu.HBM)


def project_kernel(part, plan, place, position, *refs):
    groups = sum(len(members) for members, _ in plan)
    tokens = refs[:groups]
    own_rows, other_rows = refs[groups : groups + 2]
    outs = refs[groups + 2 : -4]
    weights, picked, sems, weight_sems = refs[-4:]
    core, begin = place[0], place[1]
    depth = own_rows.shape[0]
    chips = groups // 2
    req_count, fresh_len, width = tokens[0].shape
    half_cols = weights.shape[1]
    rows = outs[0].shape[1]
    held_count = rows // fresh_len

    def columns(ref):
        if ref.shape[1] == half_cols:
            return ref
        return ref.at[:, pl.ds(pl.multiple_of(core * half_cols, LANES), half_cols)]

    copies = [
        pltpu.make_async_copy(
            columns(own_rows),
            weights.at[pl.ds(pl.multiple_of(core * depth, 16), depth)],
            weight_sems.at[0],
        ),
        pltpu.make_async_copy(
            columns(other_rows),
            weights.at[pl.ds(pl.multiple_of((1 - core) * depth, 16), depth)],
            weight_sems.at[1],
        ),
    ]
    fetches = []
    for index, token in enumerate(tokens):
        row = (index // chips * chips + (index % chips ^ begin)) * req_count
        for item in range(req_count):
            to = position[row + item] - part * groups * held_count
            mine = (to >= 0) & (to < groups * held_count)
            to = jnp.where(mine, to, 0)
            fetches.append(
                (
                    mine,
                    pltpu.make_async_copy(
                        token.at[item], picked.at[to], sems.at[index * req_count + item]
                    ),
                )
            )
    for mine, fetch in fetches:

        @pl.when(mine)
        def _():
            fetch.start()

    for copy in copies:
        copy.start()
    for mine, fetch in fetches:

        @pl.when(mine)
        def _():
            fetch.wait()

    for copy in copies:
        copy.wait()
    together = min(groups, 4)
    targets = [
        (output, index) for output, (members, _) in enumerate(plan) for index in range(len(members))
    ]
    for first in range(0, groups, together):
        these = targets[first : first + together]
        value = picked[first * held_count : (first + together) * held_count]
        result = jnp.dot(
            value.reshape(together * rows, width),
            weights[...],
            preferred_element_type=jnp.float32,
        )
        for count, (output, index) in enumerate(these):
            outs[output][index] = result[count * rows : (count + 1) * rows].astype(
                outs[output].dtype
            )


def attend_kernel(shape, place, all_lengths, table, *refs):
    terms, held_count, fresh_len, page, heads = shape
    sums = []
    for count in terms:
        sums.append(sum(ref[0].astype(jnp.float32) for ref in refs[:count]))
        refs = refs[count:]
    bias, cosine, sine_up, sine_down, key_pool, value_pool, *outs = refs[:-3]
    keys, values, sems = refs[-3:]
    chunk = CHUNK_PAGES * page
    pairs = heads // 2

    lengths = [all_lengths[index] for index in range(held_count)]
    counts = [pl.cdiv(lengths[index], chunk) for index in range(held_count)]
    bases = [jnp.int32(0)]
    for count in counts[:-1]:
        bases.append(bases[-1] + count * CHUNK_PAGES)

    def copies(index, entry):
        number = table[index, entry]
        to = bases[index] + entry
        return (
            pltpu.make_async_copy(key_pool.at[number], keys.at[to], sems.at[index]),
            pltpu.make_async_copy(value_pool.at[number], values.at[to], sems.at[index]),
        )

    for index in range(held_count):

        def start(entry, carry, index=index):
            for copy in copies(index, entry):
                copy.start()
            return carry

        lax.fori_loop(0, counts[index] * CHUNK_PAGES, start, 0)

    def cached(pages, index, part, pair):
        held = pages[
            pl.ds(bases[index] + part * CHUNK_PAGES, CHUNK_PAGES),
            :,
            starts[pair] : starts[pair] + WINDOW,
        ]
        return held.reshape(chunk, WINDOW)

    near = jnp.concatenate(sums[::2], axis=0)
    far = jnp.concatenate(sums[1::2], axis=0)
    core = place[0]
    halves = jnp.where(core == 0, near, far), jnp.where(core == 0, far, near)
    halves = [
        half + bias[:, side * half.shape[1] : (side + 1) * half.shape[1]]
        for side, half in enumerate(halves)
    ]

    def kind(which):
        pieces = []
        for head in range(heads):
            half = halves[head // pairs]
            begin = (head % pairs) * 3 * HEAD + which * HEAD
            pieces.append(half[:, begin : begin + HEAD])
        return jnp.concatenate(pieces, axis=1)

    width = heads * HEAD

    def rows_of(ref):
        table = ref[...].reshape(held_count * fresh_len, HEAD)
        return jnp.concatenate([table] * heads, axis=1)

    cosine, sine_up, sine_down = rows_of(cosine), rows_of(sine_up), rows_of(sine_down)

    def turn(block):
        half_rot = ROT // 2
        return (
            block * cosine
            + pltpu.roll(block, width - half_rot, 1) * sine_up
            + pltpu.roll(block, half_rot, 1) * sine_down
        )

    queries = turn(kind(0)).astype(jnp.bfloat16)
    turned = turn(kind(1)).astype(jnp.bfloat16)
    plain = kind(2).astype(jnp.bfloat16)

    for index in range(held_count):
        rows = slice(index * fresh_len, (index + 1) * fresh_len)
        outs[1][index] = turned[rows]
        outs[2][index] = plain[rows]

    factor = 1.0 / math.sqrt(HEAD) / math.log(2.0)
    starts = [(2 * HEAD * pair) // LANES * LANES for pair in range(pairs)]
    lane = lax.broadcasted_iota(jnp.int32, (fresh_len, WINDOW), 1)

    def owned(pair, member):
        begin = (2 * pair + member) * HEAD - starts[pair]
        return (lane >= begin) & (lane < begin + HEAD)

    def contract(left, right):
        return lax.dot_general(
            left, right, (((1,), (1,)), ((), ())), preferred_element_type=jnp.float32
        )

    zero = jnp.zeros((fresh_len, WINDOW), jnp.bfloat16)
    spread_rows = heads * fresh_len
    row = lax.broadcasted_iota(jnp.int32, (2 * fresh_len, fresh_len), 0)
    causal_pair = lax.rem(row, fresh_len) >= lax.broadcasted_iota(
        jnp.int32, (2 * fresh_len, fresh_len), 1
    )
    for index in range(held_count):
        rows = slice(index * fresh_len, (index + 1) * fresh_len)
        spread = []
        for pair in range(pairs):
            window = queries[rows, starts[pair] : starts[pair] + WINDOW]
            spread.append(
                jnp.concatenate(
                    [jnp.where(owned(pair, member), window, zero) for member in range(2)], axis=0
                )
            )
        scores = jnp.concatenate(
            [
                jnp.where(
                    causal_pair,
                    contract(spread[pair], turned[rows, starts[pair] : starts[pair] + WINDOW]),
                    -1e30,
                )
                for pair in range(pairs)
            ],
            axis=0,
        )
        peak = jnp.max(scores, axis=1, keepdims=True)
        weight = jnp.exp2((scores - peak) * factor)
        denom = jnp.sum(weight, axis=1, keepdims=True)
        weight = weight.astype(jnp.bfloat16)
        mixed = jnp.concatenate(
            [
                jnp.dot(
                    weight[pair * 2 * fresh_len : (pair + 1) * 2 * fresh_len],
                    plain[rows, starts[pair] : starts[pair] + WINDOW],
                    preferred_element_type=jnp.float32,
                )
                for pair in range(pairs)
            ],
            axis=0,
        )

        def finish(entry, carry, index=index):
            for copy in copies(index, entry):
                copy.wait()
            return carry

        lax.fori_loop(0, counts[index] * CHUNK_PAGES, finish, 0)

        def step(part, carry, index=index, spread=spread):
            peak, denom, mixed = carry
            scores = jnp.concatenate(
                [
                    contract(spread[pair], cached(keys, index, part, pair))
                    for pair in range(pairs)
                ],
                axis=0,
            )
            position = part * chunk + lax.broadcasted_iota(jnp.int32, (spread_rows, chunk), 1)
            scores = jnp.where(position < lengths[index], scores, -1e30)
            higher = jnp.maximum(peak, jnp.max(scores, axis=1, keepdims=True))
            shrink = jnp.exp2((peak - higher) * factor)
            weight = jnp.exp2((scores - higher) * factor)
            denom = denom * shrink + jnp.sum(weight, axis=1, keepdims=True)
            weight = weight.astype(jnp.bfloat16)
            added = jnp.concatenate(
                [
                    jnp.dot(
                        weight[pair * 2 * fresh_len : (pair + 1) * 2 * fresh_len],
                        cached(values, index, part, pair),
                        preferred_element_type=jnp.float32,
                    )
                    for pair in range(pairs)
                ],
                axis=0,
            )
            return higher, denom, mixed * shrink + added

        peak, denom, mixed = lax.fori_loop(0, counts[index], step, (peak, denom, mixed))
        mixed = mixed / denom
        tiles = [None] * (width // LANES)
        for pair in range(pairs):
            for member in range(2):
                begin = (2 * pair + member) * fresh_len
                part = jnp.where(owned(pair, member), mixed[begin : begin + fresh_len], 0.0)
                for side in range(2):
                    place_at = starts[pair] // LANES + side
                    tile = part[:, side * LANES : (side + 1) * LANES]
                    tiles[place_at] = tile if tiles[place_at] is None else tiles[place_at] + tile
        outs[0][index] = jnp.concatenate(tiles, axis=1).astype(jnp.bfloat16)


def per_device(
    req_size,
    wgt_size,
    arrivals,
    group_of,
    lengths,
    page_table,
    ln_gain,
    ln_bias,
    w_qkv,
    qkv_bias,
    key_pool,
    value_pool,
):
    req_count, fresh_len, width = arrivals.shape
    rows = req_count * fresh_len
    depth, local_cols = w_qkv.shape
    half_cols = local_cols // 2
    heads = local_cols // (3 * HEAD)
    page = key_pool.shape[1]
    chips = req_size // 2
    block = 2 * depth
    everyone = group_of.shape[0]
    me = lax.axis_index("req")
    layer = lax.axis_index("wgt")
    core = me & 1
    chip = me >> 1

    def swap(value, distance):
        return lax.ppermute(
            value, "req", [(device, device ^ distance) for device in range(req_size)]
        )

    def after(value, others):
        return lax.optimization_barrier((value, others))[0]

    half = req_count // 2
    layer = lax.axis_index("wgt")
    per = chips // wgt_size

    widened = arrivals.reshape(rows, width).astype(jnp.float32)
    middle = jnp.mean(widened, axis=-1)
    square = jnp.sum(jnp.square(widened - middle[:, None]), axis=-1)
    local = jnp.stack([middle, square])
    stats = jnp.broadcast_to(local[None], (wgt_size, 2, rows))
    stats = lax.all_to_all(stats, "wgt", 0, 0, tiled=True)
    center = jnp.mean(stats[:, 0], axis=0)
    square = jnp.sum(stats[:, 1] + width * jnp.square(stats[:, 0] - center[None]), axis=0)
    scale = lax.rsqrt(square / (width * wgt_size) + EPS)
    gain, shift = (
        lax.dynamic_slice_in_dim(value, layer * width, width).astype(jnp.float32)
        for value in (ln_gain, ln_bias)
    )
    tokens = (widened - center[:, None]) * scale[:, None] * gain + shift
    tokens = tokens.astype(jnp.bfloat16)
    if per > 1:
        tokens = tokens.reshape(rows, per, block)

    def route(turn):
        pairs = []
        for device in range(req_size):
            for at in range(wgt_size):
                to = device // 2
                origin = turn ^ (at * per + to % per)
                pairs.append(
                    ((2 * origin + device % 2) * wgt_size + to // per, device * wgt_size + at)
                )
        value = tokens
        if per > 1:
            value = lax.dynamic_index_in_dim(tokens, (chip ^ turn) % per, 1, False)
        return lax.ppermute(value, ("req", "wgt"), pairs)

    received = [route(turn) for turn in range(chips)]

    square_plane = chips == 4
    if square_plane:
        plan = [([2, 6], jnp.bfloat16), ([5, 7], jnp.bfloat16)]
        plan += [([distance], jnp.float32) for distance in (0, 4, 1, 3)]
    else:
        plan = [([0], jnp.float32)]
        plan += [([distance], jnp.bfloat16) for distance in range(1, req_size)]

    ids = jnp.arange(everyone, dtype=jnp.int32)
    same_group = group_of[:, None] == group_of[None, :]
    earlier = ids[None, :] < ids[:, None]
    rank = jnp.sum((same_group & earlier).astype(jnp.int32), axis=1)
    part_of, within = rank // half, rank % half
    place_of = np.zeros(req_size, np.int32)
    place_of[[target for members, _ in plan for target in members]] = np.arange(req_size)
    place_of = jnp.asarray(place_of)[group_of ^ me]
    spot = (part_of * req_size + place_of) * half + within
    origin = ids // req_count
    row = (((origin & 1) ^ core) * chips + (origin >> 1)) * req_count + ids % req_count
    position = jnp.sum(jnp.where(row[None, :] == ids[:, None], spot[None, :], 0), axis=1)

    lane = np.arange(HEAD)
    half_rot = ROT // 2
    inverse = jnp.power(10000.0, -jnp.asarray(lane % half_rot, jnp.float32) * 2.0 / ROT)
    positions = (
        lengths[:, None] + jnp.arange(fresh_len, dtype=jnp.int32)[None, :]
    ).astype(jnp.float32)
    angles = positions.reshape(rows, 1) * inverse[None, :]
    turns = jnp.asarray(lane < ROT)[None, :]
    cosine = jnp.where(turns, jnp.cos(angles), 1.0)
    sine = jnp.sin(angles)
    sine_up = jnp.where(jnp.asarray(lane < half_rot)[None, :], -sine, 0.0)
    sine_down = jnp.where(turns & jnp.asarray(lane >= half_rot)[None, :], sine, 0.0)

    tables = [
        value.reshape(req_count, fresh_len, HEAD) for value in (cosine, sine_up, sine_down)
    ]
    bias = qkv_bias.astype(jnp.float32).reshape(1, local_cols)
    place = jnp.stack([core, layer * per + chip % per]).astype(jnp.int32)
    chunk_rows = half * fresh_len
    span = page_table.shape[1]
    pages = span + (req_count - 1) * (span // 2)

    held = after(w_qkv, local)
    if half_cols % LANES == 0:
        own_rows = w_qkv
    else:
        own_rows = lax.dynamic_slice_in_dim(held, core * half_cols, half_cols, 1)
    other_rows = swap(lax.dynamic_slice_in_dim(held, (1 - core) * half_cols, half_cols, 1), 1)

    received += [swap(piece, 1) for piece in received]
    received = [piece.reshape(req_count, fresh_len, block) for piece in received]

    def collect(blocks):
        if not square_plane:
            sums = [blocks[0]]
            sums += [swap(block, distance) for distance, block in enumerate(blocks[1:], 1)]
            return sums[::2], sums[1::2]
        along_x, along_y = swap(blocks[0], 2), swap(blocks[1], 4)
        own, own_y, other, other_x = blocks[2:]
        behind_y = swap((own_y + along_x[1:]).astype(jnp.bfloat16), 4)
        behind_x = swap((other_x + along_y[1:]).astype(jnp.bfloat16), 2)
        return [own, along_x, behind_y], [swap(other + along_y[:1], 1), swap(behind_x, 1)]

    projected = []
    for part in range(2):
        projected.append(
            pl.pallas_call(
                functools.partial(project_kernel, part, plan),
                out_shape=[
                    jax.ShapeDtypeStruct((len(members), chunk_rows, half_cols), kind)
                    for members, kind in plan
                ],
                in_specs=[SMEM] * 2 + [HBM] * (req_size + 2),
                out_specs=[VMEM] * len(plan),
                scratch_shapes=[
                    pltpu.VMEM((block, half_cols), jnp.bfloat16),
                    pltpu.VMEM((req_size * half, fresh_len, block), jnp.bfloat16),
                    pltpu.SemaphoreType.DMA((everyone,)),
                    pltpu.SemaphoreType.DMA((2,)),
                ],
                compiler_params=pltpu.CompilerParams(vmem_limit_bytes=PROJECT_LIMIT),
                name="project",
            )(place, position, *received, own_rows, other_rows)
        )

    terms, sums = [], []
    for blocks in projected:
        for side in collect(blocks):
            terms.append(len(side))
            sums += side
    out = jax.ShapeDtypeStruct((req_count, fresh_len, heads * HEAD), jnp.bfloat16)
    return tuple(
        pl.pallas_call(
            functools.partial(attend_kernel, (terms, req_count, fresh_len, page, heads)),
            out_shape=[out] * 3,
            in_specs=[SMEM] * 3 + [VMEM] * (len(sums) + 4) + [HBM] * 2,
            out_specs=[VMEM] * 3,
            scratch_shapes=[
                pltpu.VMEM((pages, page, heads * HEAD), jnp.bfloat16),
                pltpu.VMEM((pages, page, heads * HEAD), jnp.bfloat16),
                pltpu.SemaphoreType.DMA((req_count,)),
            ],
            compiler_params=pltpu.CompilerParams(vmem_limit_bytes=VMEM_LIMIT),
            name="attend",
        )(place, lengths, page_table, *sums, bias, *tables, key_pool, value_pool)
    )


def solution(mesh):
    in_specs = (
        P("req", None, "wgt"),
        P(),
        P("req"),
        P("req", None),
        P(),
        P(),
        P("req", "wgt"),
        P("wgt"),
        P("req", None, "wgt"),
        P("req", None, "wgt"),
    )
    out_specs = (P("req", None, "wgt"), P("req", None, "wgt"), P("req", None, "wgt"))
    return jax.shard_map(
        functools.partial(per_device, mesh.shape["req"], mesh.shape["wgt"]),
        mesh=mesh,
        in_specs=in_specs,
        out_specs=out_specs,
        check_vma=False,
    )
```
